32 devices in a mesh: rep: 4 (over x, core), fsdp: 8 (over z, y).
Axes of the slice: x: 2, y: 2, z: 4, core: 2. Of those that a mesh axis runs over, the one named last changes fastest.
Arguments:
- inputs: bfloat16 [24576, 1024], P(('rep', 'fsdp')), may hold values from -6 to 6
- noise_times: float32 [192], P(('rep', 'fsdp')), may hold values from 1 to 300
- cotangent: bfloat16 [24576, 1024], P(('rep', 'fsdp')), may hold values from -6 to 6
- norm1_gain: bfloat16 [1024], P('fsdp'), may hold values from 0.5 to 1.5
- norm1_bias: bfloat16 [1024], P('fsdp'), may hold values from -4 to 4
- norm1_time: bfloat16 [256, 2048], P('fsdp'), may hold values from -0.1875 to 0.1875
- project_weight: bfloat16 [1024, 3072], P('fsdp'), may hold values from -0.1875 to 0.1875
- project_bias: bfloat16 [3072], P('fsdp'), may hold values from -4 to 4
- output_weight: bfloat16 [1024, 1024], P('fsdp'), may hold values from -0.75 to 0.75
- output_bias: bfloat16 [1024], P('fsdp'), may hold values from -4 to 4
- norm2_gain: bfloat16 [1024], P('fsdp'), may hold values from 0.5 to 1.5
- norm2_bias: bfloat16 [1024], P('fsdp'), may hold values from -4 to 4
- norm2_time: bfloat16 [256, 2048], P('fsdp'), may hold values from -0.1875 to 0.1875
- up_weight: bfloat16 [1024, 4096], P('fsdp'), may hold values from -0.1875 to 0.1875
- up_bias: bfloat16 [4096], P('fsdp'), may hold values from -4 to 4
- down_weight: bfloat16 [4096, 1024], P('fsdp'), may hold values from -0.09375 to 0.09375
- down_bias: bfloat16 [1024], P('fsdp'), may hold values from -4 to 4
Outputs:
- layer_out: bfloat16 [24576, 1024], P(('rep', 'fsdp'))
- input_grad: float32 [24576, 1024], P(('rep', 'fsdp'))
- grad_norm1_gain: float32 [1024], P('fsdp')
- grad_norm1_bias: float32 [1024], P('fsdp')
- grad_norm1_time: float32 [256, 2048], P('fsdp')
- grad_project_weight: float32 [1024, 3072], P('fsdp')
- grad_project_bias: float32 [3072], P('fsdp')
- grad_output_weight: float32 [1024, 1024], P('fsdp')
- grad_output_bias: float32 [1024], P('fsdp')
- grad_norm2_gain: float32 [1024], P('fsdp')
- grad_norm2_bias: float32 [1024], P('fsdp')
- grad_norm2_time: float32 [256, 2048], P('fsdp')
- grad_up_weight: float32 [1024, 4096], P('fsdp')
- grad_up_bias: float32 [4096], P('fsdp')
- grad_down_weight: float32 [4096, 1024], P('fsdp')
- grad_down_bias: float32 [1024], P('fsdp')
The draws below stay inside these ranges and needn't reach their ends.
All inputs are finite; a program needn't handle non-finite values.
Results may differ from the reference program's by a relative error of at most 0.017.
Values may be sent and summed in bfloat16 or wider, within the bound.
A program may use at most 192 MiB of HBM per device.

```python
import math
import jax
import jax.numpy as jnp
from jax import lax

D = 1024
HEADS = 16
FF = 4096
TE = 256
SEQ_LEN = 128
SEQS = 192
TOKENS = 24576


def spiked(drawn, own_key, source, target, shards_of, factor):
    def block_of(dim):
        return (jnp.arange(drawn.shape[dim]) // (drawn.shape[dim] // shards_of)).reshape((-1,) + (1,) * (drawn.ndim - 1 - dim))

    first = jax.random.permutation(own_key, shards_of)[block_of(target)]
    second = (block_of(target) + shards_of // 2) % shards_of
    return jnp.where((block_of(source) == first) | (block_of(source) == second), factor * drawn, drawn)


def shard_levels(stream_key, shape, shards, low, high):
    factor_of = 1.0
    for axis_at, blocks in shards:
        steps = jax.random.uniform(jax.random.fold_in(jax.random.fold_in(stream_key, 6), axis_at), (blocks,), jnp.float32, low / len(shards), high / len(shards))
        factor_of = factor_of * jnp.repeat(jnp.exp(steps), shape[axis_at] // blocks).reshape((-1,) + (1,) * (len(shape) - 1 - axis_at))
    return factor_of


def normal_values(key, shape, scale, most, cuts=(), kind=jnp.bfloat16):
    factor_of = shard_levels(key, shape, cuts, -0.22, 0.18) if cuts else 1.0
    entries = jax.random.normal(key, shape, jnp.float32) * scale * factor_of
    return jnp.minimum(jnp.maximum(entries, -most), most).astype(kind)


def gaussian_with(stream_key, dims, scale, limit, cuts, heavy, kind=jnp.bfloat16):
    values = scale * jax.random.normal(stream_key, dims, jnp.float32)
    if cuts:
        values = values * shard_levels(stream_key, dims, cuts, -0.22, 0.18)
    return jnp.clip(spiked(values, jax.random.fold_in(stream_key, 3), *heavy), -limit, limit).astype(kind)


def setup_inputs(seed: int = 0) -> dict:
    key_list = jax.random.split(jax.random.key(seed), 18)
    return {
        "inputs": normal_values(key_list[0], (TOKENS, D), 1.0, 6.0, ((0, 32),)),
        "noise_times": jnp.clip(jnp.exp(math.log(300.0) - 5.7037825 * jax.random.uniform(key_list[1], (SEQS,), jnp.float32) ** shard_levels(key_list[1], (SEQS,), ((0, 32),), -0.2, 0.2)), 1.0, 300.0),
        "cotangent": gaussian_with(key_list[2], (TOKENS, D), 1.0, 6.0, ((0, 32),), (0, 1, 32, 2.75)),
        "norm1_gain": jnp.clip(1.0 + 0.1 * jax.random.normal(key_list[3], (D,), jnp.float32), 0.5, 1.5).astype(jnp.bfloat16),
        "norm1_bias": normal_values(key_list[4], (D,), 0.3, 4.0, ((0, 8),)),
        "norm1_time": normal_values(key_list[5], (TE, 2 * D), (4 * TE) ** -0.5, 0.1875, ((0, 8),)),
        "project_weight": normal_values(key_list[6], (D, 3 * D), D ** -0.5, 0.1875, ((0, 8),)),
        "project_bias": normal_values(key_list[7], (3 * D,), 0.3, 4.0, ((0, 8),)),
        "output_weight": normal_values(key_list[8], (D, D), (D // 16) ** -0.5, 0.75, ((0, 8),)),
        "output_bias": normal_values(key_list[9], (D,), 0.3, 4.0, ((0, 8),)),
        "norm2_gain": jnp.clip(1.0 + 0.1 * jax.random.normal(key_list[10], (D,), jnp.float32), 0.5, 1.5).astype(jnp.bfloat16),
        "norm2_bias": normal_values(key_list[11], (D,), 0.3, 4.0, ((0, 8),)),
        "norm2_time": normal_values(key_list[12], (TE, 2 * D), (4 * TE) ** -0.5, 0.1875, ((0, 8),)),
        "up_weight": normal_values(key_list[13], (D, FF), D ** -0.5, 0.1875, ((0, 8),)),
        "up_bias": normal_values(key_list[14], (FF,), 0.3, 4.0, ((0, 8),)),
        "down_weight": normal_values(key_list[15], (FF, D), FF ** -0.5, 0.09375, ((0, 8),)),
        "down_bias": normal_values(key_list[16], (D,), 0.3, 4.0, ((0, 8),)),
    }


@jax.custom_vjp
def low(v):
    return lax.optimization_barrier(v.astype(jnp.bfloat16)).astype(jnp.float32)

@jax.custom_vjp
def low_back(v):
    return v

def low_keep(v):
    return (low(v), None)

def low_pass(kept, grad):
    return (grad,)

def back_keep(v):
    return (v, None)

def back_low(kept, grad):
    return (low(grad),)
low.defvjp(low_keep, low_pass)
low_back.defvjp(back_keep, back_low)
epsilon = 1e-05
highest = lax.Precision.HIGHEST

def features(noise_times, feat_width):
    half_width = feat_width // 2
    rates = jnp.exp(jnp.arange(half_width, dtype=jnp.float32) * (math.log(100.0) / half_width))
    phases = (jnp.log(noise_times) * 0.25)[:, None] * rates[None, :]
    return jnp.concatenate([jnp.sin(phases), jnp.cos(phases)], axis=1)

def rotary_tables(length, head_dim):
    half_width = head_dim // 2
    inverse = jnp.exp(jnp.arange(half_width, dtype=jnp.float32) * (-math.log(10000.0) / half_width))
    angles = jnp.arange(length, dtype=jnp.float32)[:, None] * inverse[None, :]
    return (jnp.cos(angles), jnp.sin(angles))

def rotate(values_in, cosine, sine_table):
    half_width = values_in.shape[-1] // 2
    first = values_in[..., :half_width]
    second = values_in[..., half_width:]
    cosine = cosine[None, :, None, :]
    sine_table = sine_table[None, :, None, :]
    return jnp.concatenate([first * cosine - second * sine_table, second * cosine + first * sine_table], axis=-1)

def time_norm(values_in, gain, bias, time_weight, time_feat, sequences):
    model_width = values_in.shape[1]
    modulation = jnp.dot(time_feat, time_weight, precision=highest)
    scale = gain[None, :] + modulation[:, :model_width]
    shift = bias[None, :] + modulation[:, model_width:]
    blocks = values_in.reshape(sequences, -1, model_width)
    centred = blocks - lax.optimization_barrier(jnp.mean(blocks, axis=-1, keepdims=True))
    normed = centred * lax.rsqrt(lax.optimization_barrier(jnp.mean(centred * centred, axis=-1, keepdims=True)) + epsilon)
    return (normed * scale[:, None, :] + shift[:, None, :]).reshape(values_in.shape)

def layer_block(weights, tokens_in, time_feat, sequences):
    norm1_gain, norm1_bias, norm1_time, project_weight, project_bias, output_weight, output_bias, norm2_gain, norm2_bias, norm2_time, up_weight, up_bias, down_weight, down_bias = weights
    model_width = tokens_in.shape[1]
    head_dim = model_width // HEADS
    factor = 1.0 / math.sqrt(head_dim)
    cosine, sine_table = rotary_tables(SEQ_LEN, head_dim)
    normed1 = low(time_norm(tokens_in, norm1_gain, norm1_bias, norm1_time, time_feat, sequences))
    joined = low_back(jnp.dot(normed1, project_weight, precision=highest) + project_bias)
    pieces = joined.reshape(sequences, SEQ_LEN, 3, HEADS, head_dim)
    queries = low(rotate(pieces[:, :, 0], cosine, sine_table) * factor)
    keys_low = low(rotate(pieces[:, :, 1], cosine, sine_table))
    values_low = low(pieces[:, :, 2])
    scores = low_back(jnp.einsum('slhe,smhe->shlm', queries, keys_low, precision=highest))
    peak_score = lax.optimization_barrier(jnp.max(scores, axis=-1, keepdims=True))
    unnormed = jnp.exp(scores - peak_score)
    probs = unnormed / lax.optimization_barrier(jnp.sum(unnormed, axis=-1, keepdims=True))
    context = jnp.einsum('shlm,smhe->slhe', low(probs), values_low, precision=highest)
    context = low(low_back(context.reshape(tokens_in.shape)))
    middle = tokens_in + low_back(jnp.dot(context, output_weight, precision=highest) + output_bias)
    normed2 = low(time_norm(middle, norm2_gain, norm2_bias, norm2_time, time_feat, sequences))
    up_proj = low_back(jnp.dot(normed2, up_weight, precision=highest) + up_bias)
    activ = low(jax.nn.gelu(up_proj, approximate=False))
    return middle + low_back(jnp.dot(activ, down_weight, precision=highest) + down_bias)

def reference(inputs, noise_times, cotangent, norm1_gain, norm1_bias, norm1_time, project_weight, project_bias, output_weight, output_bias, norm2_gain, norm2_bias, norm2_time, up_weight, up_bias, down_weight, down_bias):
    weights = tuple((weight.astype(jnp.float32) for weight in (norm1_gain, norm1_bias, norm1_time, project_weight, project_bias, output_weight, output_bias, norm2_gain, norm2_bias, norm2_time, up_weight, up_bias, down_weight, down_bias)))
    sequences = noise_times.shape[0]
    group_size = math.gcd(sequences, 32)
    group_count = sequences // group_size
    model_width = inputs.shape[1]
    tokens_in = inputs.astype(jnp.float32).reshape(group_count, group_size * SEQ_LEN, model_width)
    times_in = noise_times.reshape(group_count, group_size)
    cot_in = cotangent.astype(jnp.float32).reshape(group_count, group_size * SEQ_LEN, model_width)

    def advance(totals, item):
        block_tokens, block_times, block_cot = item
        time_feat = low(features(block_times, TE))
        block_out, pullback = jax.vjp(lambda weights_in, values_in: layer_block(weights_in, values_in, time_feat, group_size), weights, block_tokens)
        weight_grads, token_grad = pullback(block_cot)
        return (tuple((total + piece for total, piece in zip(totals, weight_grads))), (block_out, token_grad))
    zeros = tuple((jnp.zeros_like(weight) for weight in weights))
    totals, (outputs, token_grads) = lax.scan(advance, zeros, (tokens_in, times_in, cot_in))
    return (outputs.reshape(inputs.shape).astype(jnp.bfloat16), token_grads.reshape(inputs.shape), totals[0], totals[1], totals[2], totals[3], totals[4], totals[5], totals[6], totals[7], totals[8], totals[9], totals[10], totals[11], totals[12], totals[13])
```

```python
import math

import jax
import jax.numpy as jnp
from jax import lax
from jax.experimental import pallas as pl
from jax.experimental.pallas import tpu as pltpu
from jax.sharding import PartitionSpec as P

HEADS = 16
TE = 256


epsilon = 1e-05
highest = lax.Precision.HIGHEST
low_type = jnp.bfloat16
wide_type = jnp.float32


def features(noise_times, feat_width):
    half_width = feat_width // 2
    rates = jnp.exp(jnp.arange(half_width, dtype=jnp.float32) * (math.log(100.0) / half_width))
    phases = (jnp.log(noise_times) * 0.25)[:, None] * rates[None, :]
    return jnp.concatenate([jnp.sin(phases), jnp.cos(phases)], axis=1)


def rotary_tables(length, head_dim):
    half_width = head_dim // 2
    inverse = jnp.exp(jnp.arange(half_width, dtype=jnp.float32) * (-math.log(10000.0) / half_width))
    angles = jnp.arange(length, dtype=jnp.float32)[:, None] * inverse[None, :]
    return (jnp.cos(angles), jnp.sin(angles))


def rotate(values_in, cosine, sine_table):
    half_width = values_in.shape[-1] // 2
    first = values_in[..., :half_width]
    second = values_in[..., half_width:]
    cosine = cosine[None, :, None, :]
    sine_table = sine_table[None, :, None, :]
    return jnp.concatenate(
        [first * cosine - second * sine_table, second * cosine + first * sine_table], axis=-1
    )


def unrotate(grads_in, cosine, sine_table):
    half_width = grads_in.shape[-1] // 2
    first = grads_in[..., :half_width]
    second = grads_in[..., half_width:]
    cosine = cosine[None, :, None, :]
    sine_table = sine_table[None, :, None, :]
    return jnp.concatenate(
        [first * cosine + second * sine_table, second * cosine - first * sine_table], axis=-1
    )


def gelu_exact(values_in):
    return jax.nn.gelu(values_in, approximate=False)


def norm_forward(values_in, gain, bias, time_weight, time_feat, sequences):
    model_width = values_in.shape[1]
    modulation = jnp.dot(time_feat, time_weight, preferred_element_type=wide_type)
    scale = gain.astype(wide_type)[None, :] + modulation[:, :model_width]
    shift = bias.astype(wide_type)[None, :] + modulation[:, model_width:]
    blocks = values_in.reshape(sequences, -1, model_width)
    centred = blocks - jnp.mean(blocks, axis=-1, keepdims=True)
    inverse = lax.rsqrt(jnp.mean(centred * centred, axis=-1, keepdims=True) + epsilon)
    normed = centred * inverse
    result = (
        (normed * scale[:, None, :] + shift[:, None, :]).reshape(values_in.shape).astype(low_type)
    )
    return (result, (normed, inverse, scale))


def norm_backward(grads_in, kept_norm, time_feat):
    normed, inverse, scale = kept_norm
    shaped = grads_in.reshape(normed.shape)
    grad_scale = jnp.sum(shaped * normed, axis=1)
    grad_shift = jnp.sum(shaped, axis=1)
    grad_time = jnp.dot(
        time_feat.astype(wide_type).T,
        jnp.concatenate([grad_scale, grad_shift], axis=1),
        precision=highest,
    )
    grad_hat = shaped * scale[:, None, :]
    grad_values = inverse * (
        grad_hat
        - jnp.mean(grad_hat, axis=-1, keepdims=True)
        - normed * jnp.mean(grad_hat * normed, axis=-1, keepdims=True)
    )
    return (
        grad_values.reshape(grads_in.shape),
        jnp.sum(grad_scale, axis=0),
        jnp.sum(grad_shift, axis=0),
        grad_time,
    )


def attend_forward(
    normed1, project_weight, project_bias, output_weight, output_bias, cosine, sine_table, sequences
):
    token_count, model_width = normed1.shape
    head_dim = model_width // HEADS
    factor = 1.0 / math.sqrt(head_dim)
    joined = jnp.dot(
        normed1, project_weight, preferred_element_type=wide_type
    ) + project_bias.astype(wide_type)
    pieces = joined.reshape(sequences, -1, 3, HEADS, head_dim)
    queries = (rotate(pieces[:, :, 0], cosine, sine_table) * factor).astype(low_type)
    keys_low = rotate(pieces[:, :, 1], cosine, sine_table).astype(low_type)
    values_low = pieces[:, :, 2].astype(low_type)
    scores = jnp.einsum("slhe,smhe->shlm", queries, keys_low, preferred_element_type=wide_type)
    peak_score = jnp.max(scores, axis=-1, keepdims=True)
    unnormed = jnp.exp(scores - peak_score)
    totals = jnp.sum(unnormed, axis=-1, keepdims=True)
    probs_low = (unnormed / totals).astype(low_type)
    log_total = peak_score + jnp.log(totals)
    context = jnp.einsum("shlm,smhe->slhe", probs_low, values_low, preferred_element_type=wide_type)
    context = context.reshape(token_count, model_width).astype(low_type)
    branch = jnp.dot(context, output_weight, preferred_element_type=wide_type) + output_bias.astype(
        wide_type
    )
    return (branch, (queries, keys_low, values_low, log_total, context))


def attend_backward(
    grad_middle, kept_attn, project_weight, output_weight, normed1, cosine, sine_table
):
    queries, keys_low, values_low, log_total, context = kept_attn
    head_dim = queries.shape[3]
    token_count, model_width = context.shape
    factor = 1.0 / math.sqrt(head_dim)
    grad_branch = grad_middle.astype(low_type)
    grad_out_bias = jnp.sum(grad_branch.astype(wide_type), axis=0)
    grad_out_weight = jnp.einsum(
        "nd,ne->de", context, grad_branch, preferred_element_type=wide_type
    )
    grad_context = jnp.einsum(
        "ne,de->nd", grad_branch, output_weight, preferred_element_type=wide_type
    )
    grad_context = grad_context.astype(low_type).reshape(queries.shape)
    scores = jnp.einsum("slhe,smhe->shlm", queries, keys_low, preferred_element_type=wide_type)
    probs = jnp.exp(scores - log_total)
    probs_low = probs.astype(low_type)
    grad_values = jnp.einsum(
        "shlm,slhe->smhe", probs_low, grad_context, preferred_element_type=wide_type
    )
    grad_probs = jnp.einsum(
        "slhe,smhe->shlm", grad_context, values_low, preferred_element_type=wide_type
    )
    grad_scores = probs * (grad_probs - jnp.sum(grad_probs * probs, axis=-1, keepdims=True))
    grad_scores = grad_scores.astype(low_type)
    grad_queries = (
        jnp.einsum("shlm,smhe->slhe", grad_scores, keys_low, preferred_element_type=wide_type)
        * factor
    )
    grad_keys = jnp.einsum(
        "shlm,slhe->smhe", grad_scores, queries, preferred_element_type=wide_type
    )
    grad_joined = jnp.stack(
        [
            unrotate(grad_queries, cosine, sine_table),
            unrotate(grad_keys, cosine, sine_table),
            grad_values,
        ],
        axis=2,
    )
    grad_joined = grad_joined.reshape(token_count, 3 * model_width).astype(low_type)
    grad_proj_bias = jnp.sum(grad_joined.astype(wide_type), axis=0)
    grad_proj_weight = jnp.einsum(
        "nd,nf->df", normed1, grad_joined, preferred_element_type=wide_type
    )
    grad_normed = jnp.einsum(
        "nf,df->nd", grad_joined, project_weight, preferred_element_type=wide_type
    )
    return (grad_normed, grad_proj_weight, grad_proj_bias, grad_out_weight, grad_out_bias)


MESH = pl.DeviceIdType.MESH
CHUNK = 1024
FRONT = 384


class Place:
    def __init__(self):
        r, f = lax.axis_index("rep"), lax.axis_index("fsdp")
        self.r, self.f = r, f
        self.x, self.core = r // 2, r % 2
        self.z, self.y = f // 2, f % 2
        z = self.z
        self.zs = [z, z + 1 - 2 * (z % 2), (z + 2) % 4, 3 - z]
        self.same = [zk * 2 + self.y for zk in self.zs]
        self.other = [zk * 2 + 1 - self.y for zk in self.zs]
        self.across_x = ((1 - self.x) * 2 + self.core, f)
        self.across_y = (r, self.other[0])
        self.across_core = (self.x * 2 + 1 - self.core, f)
        self.diagonal = ((1 - self.x) * 2 + 1 - self.core, f)
        self.along_z = [(r, fk) for fk in self.same]
        self.group = [(r, fk) for fk in self.same[1:] + self.other]


def greet(peers):
    barrier = pltpu.get_barrier_semaphore()
    for peer in peers:
        pl.semaphore_signal(barrier, inc=1, device_id=peer, device_id_type=MESH)
    pl.semaphore_wait(barrier, len(peers))


def remote(src, dst, send, recv, peer):
    return pltpu.make_async_remote_copy(
        src_ref=src, dst_ref=dst, send_sem=send, recv_sem=recv, device_id=peer, device_id_type=MESH
    )


def gather_kernel(own, vec, full, vecs, send, recv, vsend, vrecv, lsem):
    at = Place()
    chunks, rows = own.shape[0], own.shape[1]
    half = rows // 2
    greet([at.across_core, at.across_x] + at.group)
    wide = CHUNK - FRONT
    mine = pl.ds(pl.multiple_of(at.x * FRONT, 128), wide)
    xcols = pl.ds(pl.multiple_of(at.x * wide, 128), FRONT)
    xland = pl.ds(pl.multiple_of((1 - at.x) * wide, 128), FRONT)
    lo = at.core * half

    def rows_of(f, core):
        return pl.ds(pl.multiple_of(f * rows + core * half, half), half)

    own_rows = pl.ds(pl.multiple_of(lo, half), half)
    seven = at.same[1:] + at.other

    def z_copy(c, k):
        dst = full.at[c, rows_of(at.f, at.core), mine]
        return remote(own.at[c, own_rows, mine], dst, send.at[c, k - 1], recv.at[c, k - 1], at.along_z[k])

    def z_land(c, k):
        dst = full.at[c, rows_of(at.same[k], at.core), mine]
        return remote(dst, dst, send.at[c, k - 1], recv.at[c, k - 1], at.along_z[k])

    def y_copy(c, k):
        dst = full.at[c, rows_of(at.same[k], at.core), mine]
        src = own.at[c, own_rows, mine] if k == 0 else dst
        return remote(src, dst, send.at[c, 3 + k], recv.at[c, 3 + k], at.across_y)

    def y_land(c, k):
        dst = full.at[c, rows_of(at.other[k], at.core), mine]
        return remote(dst, dst, send.at[c, 3 + k], recv.at[c, 3 + k], at.across_y)

    def x_copy(c, m):
        dst = full.at[c, rows_of(seven[m], at.core), xcols]
        return remote(dst, dst, send.at[c, 7 + m], recv.at[c, 7 + m], at.across_x)

    def x_land(c, m):
        dst = full.at[c, rows_of(seven[m], at.core), xland]
        return remote(dst, dst, send.at[c, 7 + m], recv.at[c, 7 + m], at.across_x)

    def core_copy(c, m):
        dst = full.at[c, rows_of(seven[m], at.core)]
        return remote(dst, dst, send.at[c, 14 + m], recv.at[c, 14 + m], at.across_core)

    def core_land(c, m):
        dst = full.at[c, rows_of(seven[m], 1 - at.core)]
        return remote(dst, dst, send.at[c, 14 + m], recv.at[c, 14 + m], at.across_core)

    def local(c):
        dst = full.at[c, pl.ds(pl.multiple_of(at.f * rows, rows), rows)]
        return pltpu.make_async_copy(own.at[c], dst, lsem.at[c])

    for i, peer in enumerate(at.group):
        remote(vec, vecs.at[at.f], vsend.at[i], vrecv.at[i], peer).start()
    vlocal = pltpu.make_async_copy(vec, vecs.at[at.f], vsend.at[7])
    vlocal.start()

    def first(c):
        for k in range(1, 4):
            z_copy(c, k).start()
        y_copy(c, 0).start()
        local(c).start()

    ahead = 2
    for c in range(ahead):
        first(c)

    def step(t, carry):
        @pl.when(t + ahead < chunks)
        def _():
            first(t + ahead)

        @pl.when(t < chunks)
        def _():
            for k in range(1, 4):
                z_land(t, k).wait_recv()
                y_copy(t, k).start()

        @pl.when(jnp.logical_and(t >= 1, t < chunks + 1))
        def _():
            c = t - 1
            for m in range(7):
                if m >= 3:
                    y_land(c, m - 3).wait_recv()
                x_copy(c, m).start()

        @pl.when(jnp.logical_and(t >= 2, t < chunks + 2))
        def _():
            c = t - 2
            for m in range(7):
                x_land(c, m).wait_recv()
                core_copy(c, m).start()

        @pl.when(t >= 3)
        def _():
            c = t - 3
            for m in range(7):
                core_land(c, m).wait_recv()
            local(c).wait()
            for k in range(1, 4):
                z_copy(c, k).wait_send()
            for k in range(4):
                y_copy(c, k).wait_send()
            for m in range(7):
                x_copy(c, m).wait_send()
                core_copy(c, m).wait_send()

        return carry

    lax.fori_loop(0, chunks + 3, step, 0)
    for i, peer in enumerate(at.group):
        f = seven[i]
        remote(vec, vecs.at[f], vsend.at[i], vrecv.at[i], peer).wait()
    vlocal.wait()


def gather_fast(own, vec):
    chunks, rows, _ = own.shape
    shards_of = 8
    any_space = pl.BlockSpec(memory_space=pl.ANY)
    return pl.pallas_call(
        gather_kernel,
        out_shape=(
            jax.ShapeDtypeStruct((chunks, shards_of * rows, CHUNK), own.dtype),
            jax.ShapeDtypeStruct((shards_of,) + vec.shape, vec.dtype),
        ),
        in_specs=[any_space, any_space],
        out_specs=(any_space, any_space),
        scratch_shapes=[
            pltpu.SemaphoreType.DMA((chunks, 21)),
            pltpu.SemaphoreType.DMA((chunks, 21)),
            pltpu.SemaphoreType.DMA((8,)),
            pltpu.SemaphoreType.DMA((7,)),
            pltpu.SemaphoreType.DMA((chunks,)),
        ],
        compiler_params=pltpu.CompilerParams(
            collective_id=0, has_side_effects=True, vmem_limit_bytes=32 * 2**20
        ),
        name="gather_weights",
    )(own, vec)


def add_low(a, b):
    return (a.astype(jnp.float32) + b.astype(jnp.float32)).astype(jnp.bfloat16)


def reduce_kernel(
    parts, vec, out, vec_out, held, l0, l1a, l1b, l2, l3, la, lv, lr, hsem, send, recv, vsend, vrecv
):
    at = Place()
    chunks = parts.shape[0]
    half = parts.shape[4]
    quarter = half // 2
    greet([at.across_core, at.across_x, at.diagonal] + at.group)
    front, back = pl.ds(0, FRONT), pl.ds(FRONT, CHUNK - FRONT)
    mine = pl.ds(pl.multiple_of(at.x * quarter, quarter), quarter)
    theirs = pl.ds(pl.multiple_of((1 - at.x) * quarter, quarter), quarter)
    slots = held.shape[0]

    def core_copy(c):
        return remote(parts.at[c, :, :, 1 - at.core], l0.at[c], send.at[c, 0], recv.at[c, 0], at.across_core)

    def load(c):
        return pltpu.make_async_copy(parts.at[c, :, :, at.core], held.at[c % slots], hsem.at[c % slots])

    def x_one(c):
        return remote(l0.at[c, :, :, theirs, front], l1a.at[c], send.at[c, 1], recv.at[c, 1], at.across_x)

    def y_one(c):
        return remote(l0.at[c, :, 1 - at.y, :, back], l1b.at[c], send.at[c, 2], recv.at[c, 2], at.across_y)

    def y_two(c):
        return remote(l1a.at[c, :, 1 - at.y], l2.at[c, :, :, front], send.at[c, 3], recv.at[c, 3], at.across_y)

    def x_two(c):
        return remote(l1b.at[c, :, theirs], l2.at[c, :, :, back], send.at[c, 4], recv.at[c, 4], at.across_x)

    def z_copy(c, k):
        return remote(l2.at[c, at.zs[k]], l3.at[c, k - 1], send.at[c, 4 + k], recv.at[c, 4 + k], at.along_z[k])

    def x_back(c):
        piece = la.at[c, at.core, at.x]
        return remote(piece, piece, send.at[c, 8], recv.at[c, 8], at.across_x)

    def core_back(c):
        piece = la.at[c, at.core]
        return remote(piece, piece, send.at[c, 9], recv.at[c, 9], at.across_core)

    def v_copy(i):
        f = (at.same[1:] + at.other)[i]
        return remote(vec.at[f], lv.at[i], vsend.at[i], vrecv.at[i], at.group[i])

    reps = [at.across_x, at.across_core, at.diagonal]

    def r_copy(i):
        return remote(lr.at[3], lr.at[i], vsend.at[7 + i], vrecv.at[7 + i], reps[i])

    for i in range(7):
        v_copy(i).start()
    for c in range(slots):
        load(c).start()

    def begin(c, carry):
        core_copy(c).start()
        return carry

    lax.fori_loop(0, chunks, begin, 0)

    def step(t, carry):
        @pl.when(t < chunks)
        def _():
            c = t
            load(c).wait()
            core_copy(c).wait_recv()

            def add(i, carry):
                z, y = i // 2, i % 2
                l0[c, z, y] = add_low(l0[c, z, y], held[c % slots, z, y])
                return carry

            lax.fori_loop(0, 8, add, 0)
            x_one(c).start()
            y_one(c).start()

            @pl.when(c + slots < chunks)
            def _():
                load(c + slots).start()

        @pl.when(jnp.logical_and(t >= 1, t < chunks + 1))
        def _():
            c = t - 1
            x_one(c).wait_recv()

            def add_a(i, carry):
                z, y = i // 2, i % 2
                l1a[c, z, y] = add_low(l1a[c, z, y], l0[c, z, y, mine, front])
                return carry

            lax.fori_loop(0, 8, add_a, 0)
            y_two(c).start()
            y_one(c).wait_recv()

            def add_b(z, carry):
                l1b[c, z] = add_low(l1b[c, z], l0[c, z, at.y, :, back])
                return carry

            lax.fori_loop(0, 4, add_b, 0)
            x_two(c).start()

        @pl.when(jnp.logical_and(t >= 2, t < chunks + 2))
        def _():
            c = t - 2
            y_two(c).wait_recv()
            x_two(c).wait_recv()

            def add_c(z, carry):
                l2[c, z, :, front] = add_low(l2[c, z, :, front], l1a[c, z, at.y])
                l2[c, z, :, back] = add_low(l2[c, z, :, back], l1b[c, z, mine])
                return carry

            lax.fori_loop(0, 4, add_c, 0)
            for k in range(1, 4):
                z_copy(c, k).start()

        @pl.when(jnp.logical_and(t >= 3, t < chunks + 3))
        def _():
            c = t - 3
            for k in range(1, 4):
                z_copy(c, k).wait_recv()
            total = l2[c, at.z].astype(jnp.float32)
            for k in range(3):
                total = total + l3[c, k].astype(jnp.float32)
            la[c, at.core, at.x] = total.astype(jnp.bfloat16)
            x_back(c).start()

        @pl.when(jnp.logical_and(t >= 4, t < chunks + 4))
        def _():
            c = t - 4
            there = la.at[c, at.core, 1 - at.x]
            remote(there, there, send.at[c, 8], recv.at[c, 8], at.across_x).wait_recv()
            core_back(c).start()

        @pl.when(t >= 5)
        def _():
            c = t - 5
            there = la.at[c, 1 - at.core]
            remote(there, there, send.at[c, 9], recv.at[c, 9], at.across_core).wait_recv()
            for j in range(4):
                out[c, j * quarter : (j + 1) * quarter, :] = la[c, j // 2, j % 2].astype(jnp.float32)
            core_copy(c).wait_send()
            x_one(c).wait_send()
            y_one(c).wait_send()
            x_two(c).wait_send()
            y_two(c).wait_send()
            for k in range(1, 4):
                z_copy(c, k).wait_send()
            x_back(c).wait_send()
            core_back(c).wait_send()

        return carry

    lax.fori_loop(0, chunks + 5, step, 0)
    total = vec[at.f]
    for i in range(7):
        v_copy(i).wait()
        total = total + lv[i]
    lr[3] = total
    for i in range(3):
        r_copy(i).start()
    for i in range(3):
        r_copy(i).wait()
        total = total + lr[i]
    vec_out[...] = total


def reduce_fast(parts, vec):
    chunks, depth, _ = parts.shape
    rows = depth // 8
    half, quarter = rows // 2, rows // 4
    low = jnp.bfloat16
    wide = CHUNK - FRONT
    shaped = parts.reshape(chunks, 4, 2, 2, half, CHUNK)
    vmem = pl.BlockSpec(memory_space=pltpu.VMEM)
    return pl.pallas_call(
        reduce_kernel,
        out_shape=(
            jax.ShapeDtypeStruct((chunks, rows, CHUNK), jnp.float32),
            jax.ShapeDtypeStruct(vec.shape[1:], jnp.float32),
        ),
        in_specs=[pl.BlockSpec(memory_space=pl.ANY), vmem],
        out_specs=(vmem, vmem),
        scratch_shapes=[
            pltpu.VMEM((3, 4, 2, half, CHUNK), low),
            pltpu.VMEM((chunks, 4, 2, half, CHUNK), low),
            pltpu.VMEM((chunks, 4, 2, quarter, FRONT), low),
            pltpu.VMEM((chunks, 4, half, wide), low),
            pltpu.VMEM((chunks, 4, quarter, CHUNK), low),
            pltpu.VMEM((chunks, 3, quarter, CHUNK), low),
            pltpu.VMEM((chunks, 2, 2, quarter, CHUNK), low),
            pltpu.VMEM((7,) + vec.shape[1:], jnp.float32),
            pltpu.VMEM((4,) + vec.shape[1:], jnp.float32),
            pltpu.SemaphoreType.DMA((3,)),
            pltpu.SemaphoreType.DMA((chunks, 10)),
            pltpu.SemaphoreType.DMA((chunks, 10)),
            pltpu.SemaphoreType.DMA((10,)),
            pltpu.SemaphoreType.DMA((10,)),
        ],
        compiler_params=pltpu.CompilerParams(
            collective_id=1, has_side_effects=True, vmem_limit_bytes=56 * 2**20
        ),
        name="reduce_gradients",
    )(shaped, vec)

def pack_local(weights):
    (project, output, up, down, time1, time2) = weights
    rows, width = output.shape
    shards_of = width // rows
    up_blocks = up.reshape(rows, shards_of, 4, rows).transpose(2, 0, 1, 3).reshape(4, rows, width)
    times = jnp.stack([time1, time2]).reshape(2, -1, 2, width).transpose(0, 2, 1, 3)
    return jnp.concatenate(
        [
            times.reshape(1, rows, width),
            project.reshape(rows, 3, width).transpose(1, 0, 2),
            output[None],
            up_blocks,
            down.reshape(4, rows, width),
        ]
    )


def pack_vectors(vectors, shards_of):
    flat = jnp.concatenate(vectors)
    return jnp.pad(flat.reshape(-1, 128), ((0, 3), (0, 0))) if flat.shape[0] == 13 * 128 else flat[None]


def gather_all(own, vec, shards_of):
    if shards_of == 8:
        return gather_fast(own, vec)
    full = lax.all_gather(own, "fsdp", axis=1, tiled=True)
    return full, lax.all_gather(vec, "fsdp", axis=0)


def reduce_all(parts, vec, shards_of):
    if shards_of == 8:
        return reduce_fast(parts, vec)
    mine = lax.psum_scatter(parts, "fsdp", scatter_dimension=1, tiled=True)
    mine = lax.psum(mine, "rep").astype(jnp.float32)
    vec = lax.psum_scatter(vec, "fsdp", scatter_dimension=0, tiled=True)[0]
    return mine, lax.psum(vec, "rep")


def shards(
    inputs, noise_times, cotangent, norm1_gain, norm1_bias, norm1_time, project_weight, project_bias,
    output_weight, output_bias, norm2_gain, norm2_bias, norm2_time, up_weight, up_bias, down_weight, down_bias,
):
    sequences = noise_times.shape[0]
    width = inputs.shape[1]
    rows = output_weight.shape[0]
    shards_of = width // rows
    time_feat = features(noise_times, TE).astype(low_type)
    cosine, sine_table = rotary_tables(inputs.shape[0] // sequences, width // HEADS)
    tokens_wide = inputs.astype(wide_type)
    own = pack_local((project_weight, output_weight, up_weight, down_weight, norm1_time, norm2_time))
    vectors = (norm1_gain, norm1_bias, project_bias, output_bias, norm2_gain, norm2_bias, up_bias, down_bias)
    sizes = [v.shape[0] for v in vectors]
    vec = pack_vectors(vectors, shards_of)
    full, vecs = gather_all(own, vec, shards_of)
    flat = vecs.reshape(shards_of, -1)
    at, whole = 0, []
    for size in sizes:
        whole.append(flat[:, at : at + size].reshape(-1))
        at += size
    gain1, bias1, bias_p, bias_o, gain2, bias2, bias_u, bias_d = whole
    bias_u = bias_u.reshape(shards_of, 4, rows).transpose(1, 0, 2).reshape(-1)
    times = full[0].reshape(shards_of, 2, 2, -1, width).transpose(1, 0, 3, 2, 4).reshape(2, TE, 2 * width)
    project = full[1:4].transpose(1, 0, 2).reshape(width, 3 * width)
    output = full[4]
    up = full[5:9].transpose(1, 0, 2).reshape(width, 4 * width)
    down = full[9:13].reshape(4 * width, width)
    normed1, kept_norm1 = norm_forward(tokens_wide, gain1, bias1, times[0], time_feat, sequences)
    branch, kept_attn = attend_forward(
        normed1, project, bias_p, output, bias_o, cosine, sine_table, sequences
    )
    middle = tokens_wide + branch
    normed2, kept_norm2 = norm_forward(middle, gain2, bias2, times[1], time_feat, sequences)
    up_proj = jnp.dot(normed2, up, preferred_element_type=wide_type) + bias_u.astype(wide_type)
    activ = gelu_exact(up_proj).astype(low_type)
    result = middle + jnp.dot(activ, down, preferred_element_type=wide_type) + bias_d.astype(wide_type)
    layer_out = result.astype(low_type)
    grad_down_bias = jnp.sum(cotangent.astype(wide_type), axis=0)
    grad_down = jnp.einsum("nf,nd->fd", activ, cotangent, preferred_element_type=wide_type)
    grad_activ = jnp.einsum("nd,fd->nf", cotangent, down, preferred_element_type=wide_type)
    unused, gelu_pull = jax.vjp(gelu_exact, up_proj)
    grad_up = gelu_pull(grad_activ)[0].astype(low_type)
    grad_up_bias = jnp.sum(grad_up.astype(wide_type), axis=0)
    grad_up_weight = jnp.einsum("nd,nf->df", normed2, grad_up, preferred_element_type=wide_type)
    grad_normed2 = jnp.einsum("nf,df->nd", grad_up, up, preferred_element_type=wide_type)
    grad_from2, grad_gain2, grad_bias2, grad_time2 = norm_backward(grad_normed2, kept_norm2, time_feat)
    grad_middle = cotangent.astype(wide_type) + grad_from2
    grad_normed1, grad_proj, grad_proj_bias, grad_out, grad_out_bias = attend_backward(
        grad_middle, kept_attn, project, output, normed1, cosine, sine_table
    )
    grad_from1, grad_gain1, grad_bias1, grad_time1 = norm_backward(grad_normed1, kept_norm1, time_feat)
    input_grad = grad_middle + grad_from1
    grad_times = jnp.stack([grad_time1, grad_time2]).reshape(2, shards_of, -1, 2, width)
    parts = jnp.concatenate(
        [
            grad_times.transpose(1, 0, 3, 2, 4).reshape(1, width, width).astype(low_type),
            grad_proj.astype(low_type).reshape(width, 3, width).transpose(1, 0, 2),
            grad_out.astype(low_type)[None],
            grad_up_weight.astype(low_type).reshape(width, 4, width).transpose(1, 0, 2),
            grad_down.astype(low_type).reshape(4, width, width),
        ]
    )
    grad_up_bias = grad_up_bias.reshape(4, shards_of, rows).transpose(1, 0, 2).reshape(-1)
    grad_vectors = (
        grad_gain1, grad_bias1, grad_proj_bias, grad_out_bias, grad_gain2, grad_bias2, grad_up_bias, grad_down_bias
    )
    grad_vec = jnp.concatenate([g.reshape(shards_of, -1) for g in grad_vectors], axis=1)
    pad = vec.size - grad_vec.shape[1]
    grad_vec = jnp.pad(grad_vec, ((0, 0), (0, pad))).reshape((shards_of,) + vec.shape)
    mine, mine_vec = reduce_all(parts, grad_vec, shards_of)
    mine_vec = mine_vec.reshape(-1)
    at, got = 0, []
    for size in sizes:
        got.append(mine_vec[at : at + size])
        at += size
    my_times = mine[0].reshape(2, 2, -1, width).transpose(0, 2, 1, 3).reshape(2, -1, 2 * width)
    my_project = mine[1:4].transpose(1, 0, 2).reshape(rows, 3 * width)
    my_up = mine[5:9].reshape(4, rows, shards_of, rows).transpose(1, 2, 0, 3).reshape(rows, 4 * width)
    my_down = mine[9:13].reshape(4 * rows, width)
    return (
        layer_out, input_grad, got[0], got[1], my_times[0], my_project, got[2], mine[4], got[3],
        got[4], got[5], my_times[1], my_up, got[6], my_down, got[7],
    )


def solution(mesh):
    placed = (
        P(("rep", "fsdp"), None),
        P(("rep", "fsdp")),
        P(("rep", "fsdp"), None),
        P("fsdp"),
        P("fsdp"),
        P("fsdp", None),
        P("fsdp", None),
        P("fsdp"),
        P("fsdp", None),
        P("fsdp"),
        P("fsdp"),
        P("fsdp"),
        P("fsdp", None),
        P("fsdp", None),
        P("fsdp"),
        P("fsdp", None),
        P("fsdp"),
    )
    return jax.shard_map(
        shards,
        mesh=mesh,
        in_specs=placed,
        out_specs=(
            P(("rep", "fsdp"), None),
            P(("rep", "fsdp"), None),
            P("fsdp"),
            P("fsdp"),
            P("fsdp", None),
            P("fsdp", None),
            P("fsdp"),
            P("fsdp", None),
            P("fsdp"),
            P("fsdp"),
            P("fsdp"),
            P("fsdp", None),
            P("fsdp", None),
            P("fsdp"),
            P("fsdp", None),
            P("fsdp"),
        ),
        check_vma=False,
    )
```

```python
import functools
import math

import jax
import jax.numpy as jnp
import numpy as np
from jax import lax
from jax.experimental import pallas as pl
from jax.experimental.pallas import tpu as pltpu
from jax.sharding import PartitionSpec as P

HEADS = 16
TE = 256
epsilon = 1e-05


MESH = pl.DeviceIdType.MESH
LOW, WIDE = jnp.bfloat16, jnp.float32
FRONT = 384
BLOCKS = 13
PIECES = 2 * BLOCKS
NT = (((1,), (1,)), ((), ()))
TN = (((0,), (0,)), ((), ()))


class Place:
    def __init__(self):
        r, f = lax.axis_index("rep"), lax.axis_index("fsdp")
        self.r, self.f = r, f
        self.x, self.core = r // 2, r % 2
        self.z, self.y = f // 2, f % 2
        z = self.z
        self.zs = [z, z + 1 - 2 * (z % 2), (z + 2) % 4, 3 - z]
        self.same = [zk * 2 + self.y for zk in self.zs]
        self.other = [zk * 2 + 1 - self.y for zk in self.zs]
        self.across_x = ((1 - self.x) * 2 + self.core, f)
        self.across_y = (r, self.other[0])
        self.across_core = (self.x * 2 + 1 - self.core, f)
        self.diagonal = ((1 - self.x) * 2 + 1 - self.core, f)
        self.along_z = [(r, fk) for fk in self.same]
        self.shards = self.same[1:] + self.other
        self.group = [(r, fk) for fk in self.shards]


def greet(peers):
    barrier = pltpu.get_barrier_semaphore()
    for peer in peers:
        pl.semaphore_signal(barrier, inc=1, device_id=peer, device_id_type=MESH)
    pl.semaphore_wait(barrier, len(peers))


def remote(src, dst, send, recv, peer):
    return pltpu.make_async_remote_copy(
        src_ref=src, dst_ref=dst, send_sem=send, recv_sem=recv, device_id=peer, device_id_type=MESH
    )


class Gather:
    steps = PIECES + 3

    def __init__(self, own, vec, full, vecs, send, recv, vsend, vrecv, lsem):
        self.at = Place()
        self.own, self.full, self.send, self.recv, self.lsem = own, full, send, recv, lsem
        self.vec, self.vecs, self.vsend, self.vrecv = vec, vecs, vsend, vrecv
        x = self.at.x
        rest = 1024 - FRONT
        self.mine = pl.ds(pl.multiple_of(x * FRONT, 128), rest)
        self.xcols = pl.ds(pl.multiple_of(x * rest, 128), FRONT)
        self.xland = pl.ds(pl.multiple_of((1 - x) * rest, 128), FRONT)

    def spot(self, c, z, y, cols, core=None):
        core = self.at.core if core is None else core
        return self.full.at[c // 2, z, y, core, c % 2, :, cols]

    def pair(self, c, i, src, dst, peer):
        return remote(src, dst, self.send.at[c, i], self.recv.at[c, i], peer)

    def z_copy(self, c, k):
        at = self.at
        src = self.own.at[c // 2, at.core, c % 2, :, self.mine]
        return self.pair(c, k - 1, src, self.spot(c, at.z, at.y, self.mine), at.along_z[k])

    def z_land(self, c, k):
        dst = self.spot(c, self.at.zs[k], self.at.y, self.mine)
        return self.pair(c, k - 1, dst, dst, self.at.along_z[k])

    def y_copy(self, c, k):
        at = self.at
        dst = self.spot(c, at.zs[k], at.y, self.mine)
        src = self.own.at[c // 2, at.core, c % 2, :, self.mine] if k == 0 else dst
        return self.pair(c, 3 + k, src, dst, at.across_y)

    def y_land(self, c, k):
        dst = self.spot(c, self.at.zs[k], 1 - self.at.y, self.mine)
        return self.pair(c, 3 + k, dst, dst, self.at.across_y)

    def x_place(self, c, k, cols):
        at = self.at
        if k < 3:
            return self.spot(c, at.zs[k + 1], at.y, cols)
        return self.spot(c, slice(None), 1 - at.y, cols)

    def x_copy(self, c, k):
        src = self.x_place(c, k, self.xcols)
        return self.pair(c, 7 + k, src, src, self.at.across_x)

    def x_land(self, c, k):
        dst = self.x_place(c, k, self.xland)
        return self.pair(c, 7 + k, dst, dst, self.at.across_x)

    def core_copy(self, c, core=None):
        part = self.spot(c, slice(None), slice(None), slice(None), core)
        return self.pair(c, 11, part, part, self.at.across_core)

    def local(self, c):
        at = self.at
        dst = self.spot(c, at.z, at.y, slice(None))
        return pltpu.make_async_copy(self.own.at[c // 2, at.core, c % 2], dst, self.lsem.at[c])

    def first(self, c):
        for k in range(1, 4):
            self.z_copy(c, k).start()
        self.y_copy(c, 0).start()
        self.local(c).start()

    ahead = 4

    def begin(self):
        at = self.at
        greet([at.across_core, at.across_x] + at.group)
        for i, peer in enumerate(at.group):
            remote(self.vec, self.vecs.at[at.f], self.vsend.at[i], self.vrecv.at[i], peer).start()
        for c in range(self.ahead):
            self.first(c)

    def vectors(self):
        at = self.at
        self.vecs[at.f] = self.vec[...]
        for i, peer in enumerate(at.group):
            remote(self.vec, self.vecs.at[at.shards[i]], self.vsend.at[i], self.vrecv.at[i], peer).wait()

    def step(self, t):
        @pl.when(t + self.ahead < PIECES)
        def _():
            self.first(t + self.ahead)

        @pl.when(t < PIECES)
        def _():
            for k in range(1, 4):
                self.z_land(t, k).wait_recv()
                self.y_copy(t, k).start()

        @pl.when(jnp.logical_and(t >= 1, t < PIECES + 1))
        def _():
            c = t - 1
            for k in range(4):
                if k == 3:
                    for j in range(4):
                        self.y_land(c, j).wait_recv()
                self.x_copy(c, k).start()

        @pl.when(jnp.logical_and(t >= 2, t < PIECES + 2))
        def _():
            c = t - 2
            self.local(c).wait()
            for k in range(4):
                self.x_land(c, k).wait_recv()
            self.core_copy(c).start()

        @pl.when(jnp.logical_and(t >= 3, t < PIECES + 3))
        def _():
            c = t - 3
            self.core_copy(c, 1 - self.at.core).wait_recv()
            for k in range(1, 4):
                self.z_copy(c, k).wait_send()
            for k in range(4):
                self.y_copy(c, k).wait_send()
                self.x_copy(c, k).wait_send()
            self.core_copy(c).wait_send()

    def run(self, lo, hi):
        def one(t, carry):
            self.step(t)
            return carry

        lax.fori_loop(lo, hi, one, 0)


GATHER_SCRATCH = [
    pltpu.VMEM((8, 16, 128), LOW),
    pltpu.SemaphoreType.DMA((PIECES, 12)),
    pltpu.SemaphoreType.DMA((PIECES, 12)),
    pltpu.SemaphoreType.DMA((7,)),
    pltpu.SemaphoreType.DMA((7,)),
    pltpu.SemaphoreType.DMA((PIECES,)),
]


GAIN1, BIAS1, BIAS_P, BIAS_O, GAIN2, BIAS2, BIAS_U, BIAS_D = 0, 1, 2, 5, 6, 7, 8, 12
HALF = 512
TILE = 32


def vector_spot(row, f):
    if BIAS_P <= row < BIAS_O:
        block = f * 3 + row - BIAS_P
        return BIAS_P + block // 8, block % 8
    return row, f


def for_each(count, body):
    def one(i, carry):
        body(i)
        return carry

    lax.fori_loop(0, count, one, 0)


def rows_at(i, size=TILE):
    return pl.ds(pl.multiple_of(i * size, size), size)


def lane_mean(v):
    return jnp.mean(v, axis=-1, keepdims=True)


def normalise(v):
    centred = v - lane_mean(v)
    inverse = lax.rsqrt(lane_mean(centred * centred) + epsilon)
    return centred * inverse, inverse


def row_of(ref, i):
    return ref[pl.ds(i, 1), :]


def modulated(ref, out, table, mods, gain, which, seqs):
    per = ref.shape[0] // seqs // TILE

    def body(i):
        s = i // per
        scale = table[gain : gain + 1, :] + row_of(mods, 2 * which * seqs + s)
        shift = table[gain + 1 : gain + 2, :] + row_of(mods, (2 * which + 1) * seqs + s)
        rows = rows_at(i)
        normed, _ = normalise(ref[rows, :].astype(WIDE))
        out[rows, :] = (normed * scale + shift).astype(LOW)

    for_each(ref.shape[0] // TILE, body)


def swapped(v):
    lane = lax.broadcasted_iota(jnp.int32, v.shape, 1)
    return jnp.where(lane % 64 < 32, pltpu.roll(v, 96, 1), pltpu.roll(v, 32, 1))


def forward_kernel(comm, seqs, *refs):
    refs = list(refs)
    take = lambda n: [refs.pop(0) for _ in range(n)]
    if comm:
        own, vec = take(2)
    else:
        full_in, table_in = take(2)
    tokens_hbm, feat, cosine, sine = take(4)
    if comm:
        (full,) = take(1)
    else:
        full = full_in
    table, mods = take(2)
    out_o, q_o, k_o, v_o, ctx_o, mid_o, normed2_o, activ_o, slope_o = take(9)
    tokens, weights, normed, q, k, v, ctx, mid, acc, activ, slope, wide, out_low = take(13)
    sem_in, sem_w, sem_out = take(3)
    tokens_n = tokens.shape[0]
    per = tokens_n // seqs

    tokens_in = pltpu.make_async_copy(tokens_hbm, tokens, sem_in)
    tokens_in.start()
    if comm:
        gather = Gather(own, vec, full, *refs)
        gather.begin()
        gather.vectors()
        for f in range(8):
            block = gather.vecs[f].astype(WIDE)
            for row in range(13):
                r, b = vector_spot(row, f)
                table[r : r + 1, b * 128 : (b + 1) * 128] = block[row : row + 1, :]
        run = gather.run
    else:
        table[...] = table_in[...]
        run = lambda lo, hi: None

    def weight(c, slot):
        copy = pltpu.make_async_copy(full.at[c], weights.at[slot], sem_w.at[slot])
        copy.start()
        copy.wait()
        return weights.at[slot]

    flat = (lambda w: w[...].reshape(1024, 1024)) if comm else (lambda w: w[...])

    saves = []

    def save(src, dst):
        copy = pltpu.make_async_copy(src, dst, sem_out.at[len(saves)])
        copy.start()
        saves.append(copy)

    run(0, 5)
    w = weight(0, 0)
    mods[...] = jnp.dot(feat[...], flat(w), preferred_element_type=WIDE)
    tokens_in.wait()
    modulated(tokens, normed, table, mods, GAIN1, 0, seqs)

    for j, (dst, dst_o) in enumerate([(q, q_o), (k, k_o), (v, v_o)]):
        run(5 + 2 * j, 7 + 2 * j)
        w = weight(1 + j, (1 + j) % 2)
        for h in range(2):
            cols = slice(h * HALF, (h + 1) * HALF)
            wide[...] = jnp.dot(normed[...], half_of(w, cols, comm), preferred_element_type=WIDE)
            bias = table[BIAS_P + j : BIAS_P + j + 1, cols]

            def body(i, h=h, bias=bias, dst=dst, j=j):
                rows = rows_at(i)
                where = pl.ds(pl.multiple_of((i % (per // TILE)) * TILE, TILE), TILE)
                piece = wide[rows, :] + bias
                if j == 2:
                    dst[rows, h * HALF : (h + 1) * HALF] = piece.astype(LOW)
                    return
                for n in range(HALF // 128):
                    part = piece[:, n * 128 : (n + 1) * 128]
                    turned = part * cosine[where, :] + swapped(part) * sine[where, :]
                    if j == 0:
                        turned = turned * 0.125
                    at = h * HALF + n * 128
                    dst[rows, at : at + 128] = turned.astype(LOW)

            for_each(tokens_n // TILE, body)
        save(dst, dst_o)

    lane = lax.broadcasted_iota(jnp.int32, (1, 128), 1)
    first_head = (lane < 64).astype(WIDE)
    second_head = 1.0 - first_head

    def heads(n):
        cols = pl.ds(pl.multiple_of(n * 128, 128), 128)
        for s in range(seqs):
            rows = slice(s * per, (s + 1) * per)
            qs = q[rows, cols]
            both = jnp.concatenate([qs * first_head.astype(LOW), qs * second_head.astype(LOW)], axis=0)
            scores = lax.dot_general(both, k[rows, cols], NT, preferred_element_type=WIDE)
            grown = jnp.exp(scores - jnp.max(scores, axis=-1, keepdims=True))
            probs = (grown / jnp.sum(grown, axis=-1, keepdims=True)).astype(LOW)
            mixed = jnp.dot(probs, v[rows, cols], preferred_element_type=WIDE)
            ctx[rows, cols] = (mixed[:per] * first_head + mixed[per:] * second_head).astype(LOW)
        if comm:
            pl.when(n >= 2)(lambda: gather.step(9 + n))

    for_each(8, heads)
    save(ctx, ctx_o)

    w = weight(4, 0)
    for h in range(2):
        cols = slice(h * HALF, (h + 1) * HALF)
        dot = jnp.dot(ctx[...], half_of(w, cols, comm), preferred_element_type=WIDE)
        mid[:, cols] = tokens[:, cols].astype(WIDE) + (dot + table[BIAS_O : BIAS_O + 1, cols])
    save(mid, mid_o)
    modulated(mid, normed, table, mods, GAIN2, 1, seqs)
    save(normed, normed2_o)

    def up(j):
        if comm:
            pl.when(j >= 1)(lambda: run(15 + 2 * j, 17 + 2 * j))
        w = weight(5 + j, 0)
        for h in range(2):
            cols = slice(h * HALF, (h + 1) * HALF)
            wide[...] = jnp.dot(normed[...], half_of(w, cols, comm), preferred_element_type=WIDE)

            def body(i, h=h, cols=cols):
                rows = rows_at(i)
                u = wide[rows, :] + table[pl.ds(BIAS_U + j, 1), cols]
                phi = 0.5 + 0.5 * lax.erf(u * (0.5**0.5))
                activ[j, rows, cols] = (u * phi).astype(LOW)
                bell = jnp.exp(-0.5 * (u * u)) * (1.0 / math.sqrt(2.0 * math.pi))
                slope[j, rows, cols] = (phi + u * bell).astype(LOW)

            for_each(tokens_n // TILE, body)

    for_each(4, up)
    save(activ, activ_o)
    save(slope, slope_o)

    def down(j):
        if comm:
            pl.when(j >= 1)(lambda: run(21 + 2 * j, 23 + 2 * j))
        w = weight(9 + j, 0)
        for h in range(2):
            cols = slice(h * HALF, (h + 1) * HALF)
            dot = jnp.dot(activ[j], half_of(w, cols, comm), preferred_element_type=WIDE)

            @pl.when(j == 0)
            def _():
                acc[:, cols] = mid[:, cols] + table[BIAS_D : BIAS_D + 1, cols] + dot

            @pl.when(j > 0)
            def _():
                acc[:, cols] = acc[:, cols] + dot

    for_each(4, down)
    out_low[...] = acc[...].astype(LOW)
    save(out_low, out_o)
    for copy in saves:
        copy.wait()


def half_of(w, cols, comm):
    if comm:
        return w[..., cols].reshape(1024, HALF)
    return w[:, cols]


def forward_call(comm, first, second, tokens, feat, cosine, sine, seqs):
    n, width = tokens.shape
    vmem, hbm = pl.BlockSpec(memory_space=pltpu.VMEM), pl.BlockSpec(memory_space=pl.ANY)
    low = jax.ShapeDtypeStruct((n, width), LOW)
    wide = jax.ShapeDtypeStruct((n, width), WIDE)
    shape4 = jax.ShapeDtypeStruct((4, n, width), LOW)
    block = (4, 2, 2, 2, 32, width) if comm else (width, width)
    outs = [
        (jax.ShapeDtypeStruct((16, width), WIDE), vmem),
        (jax.ShapeDtypeStruct((feat.shape[0], width), WIDE), vmem),
    ] + [(s, hbm) for s in (low, low, low, low, low, wide, low, shape4, shape4)]
    if comm:
        outs = [(jax.ShapeDtypeStruct((BLOCKS,) + block, LOW), hbm)] + outs
        first = first.reshape(BLOCKS, 2, 2, 32, width)
    buffer = pltpu.VMEM((n, width), LOW)
    got = pl.pallas_call(
        functools.partial(forward_kernel, comm, seqs),
        out_shape=tuple(s for s, _ in outs),
        in_specs=[hbm, vmem, hbm, vmem, vmem, vmem],
        out_specs=tuple(m for _, m in outs),
        scratch_shapes=[
            buffer,
            pltpu.VMEM((2,) + block, LOW),
            buffer,
            buffer,
            buffer,
            buffer,
            buffer,
            pltpu.VMEM((n, width), WIDE),
            pltpu.VMEM((n, width), WIDE),
            pltpu.VMEM((4, n, width), LOW),
            pltpu.VMEM((4, n, width), LOW),
            pltpu.VMEM((n, HALF), WIDE),
            buffer,
            pltpu.SemaphoreType.DMA,
            pltpu.SemaphoreType.DMA((2,)),
            pltpu.SemaphoreType.DMA((9,)),
        ]
        + (GATHER_SCRATCH if comm else []),
        compiler_params=pltpu.CompilerParams(
            collective_id=0 if comm else None, has_side_effects=comm, vmem_limit_bytes=60 * 2**20
        ),
        name="forward",
    )(first, second, tokens, feat, cosine, sine)
    if not comm:
        return (first, second) + tuple(got[1:])
    return (got[0].reshape(BLOCKS, width, width),) + tuple(got[1:])


RING = 10


class Reduce:
    def __init__(self, slots, own, l0, out, *scratch):
        self.at = Place()
        self.slots, self.own, self.l0, self.out = slots, own, l0, out
        (self.held, self.s0, self.l1a, self.l1b, self.l2, self.l3, self.la, self.stage) = scratch[:8]
        (self.bsend, self.brecv, self.lsem, self.send, self.recv, self.osem) = scratch[8:14]
        x = self.at.x
        self.front, self.back = pl.ds(0, FRONT), pl.ds(FRONT, 1024 - FRONT)
        self.mine = pl.ds(pl.multiple_of(x * 16, 16), 16)
        self.theirs = pl.ds(pl.multiple_of((1 - x) * 16, 16), 16)

    def begin(self):
        at = self.at
        greet([at.across_core, at.across_x, at.diagonal] + at.group)

    def core_copy(self, b):
        src = self.slots.at[b % 2, :, :, 1 - self.at.core]
        return remote(src, self.l0.at[b], self.bsend.at[b], self.brecv.at[b], self.at.across_core)

    def own_copy(self, b):
        return pltpu.make_async_copy(self.slots.at[b % 2, :, :, self.at.core], self.own.at[b], self.lsem.at[b % 2])

    def loads(self, b):
        return (
            pltpu.make_async_copy(self.own.at[b], self.held.at[0], self.lsem.at[2]),
            pltpu.make_async_copy(self.l0.at[b], self.held.at[1], self.lsem.at[3]),
        )

    def free(self, b):
        pl.when(b >= 2)(lambda: self.core_copy(b - 2).wait_send())

    def produced(self, b):
        self.core_copy(b).start()
        self.own_copy(b).start()

    def load(self, b):
        self.own_copy(b).wait()
        self.core_copy(b).wait_recv()
        for copy in self.loads(b):
            copy.start()

    def feed(self, b):
        for copy in self.loads(b):
            copy.wait()

        def add(i):
            z, y, h = i // 4, (i // 2) % 2, i % 2
            piece = self.held[0, z, y, h].astype(WIDE) + self.held[1, z, y, h].astype(WIDE)
            self.s0[(2 * b + h) % RING, z, y] = piece.astype(LOW)

        for_each(16, add)
        for h in range(2):
            self.x_one(2 * b + h).start()
            self.y_one(2 * b + h).start()

    def pair(self, p, i, src, dst, peer):
        return remote(src, dst, self.send.at[p, i], self.recv.at[p, i], peer)

    def x_one(self, p):
        src = self.s0.at[p % RING, :, :, self.theirs, self.front]
        return self.pair(p, 0, src, self.l1a.at[p], self.at.across_x)

    def y_one(self, p):
        src = self.s0.at[p % RING, :, 1 - self.at.y, :, self.back]
        return self.pair(p, 1, src, self.l1b.at[p], self.at.across_y)

    def y_two(self, p):
        return self.pair(p, 2, self.l1a.at[p, :, 1 - self.at.y], self.l2.at[p, :, :, self.front], self.at.across_y)

    def x_two(self, p):
        return self.pair(p, 3, self.l1b.at[p, :, self.theirs], self.l2.at[p, :, :, self.back], self.at.across_x)

    def z_copy(self, p, k):
        return self.pair(p, 3 + k, self.l2.at[p, self.at.zs[k]], self.l3.at[p, k - 1], self.at.along_z[k])

    def x_back(self, p, x=None):
        piece = self.la.at[p, self.at.core, self.at.x if x is None else x]
        return self.pair(p, 7, piece, piece, self.at.across_x)

    def core_back(self, p, core=None):
        piece = self.la.at[p, self.at.core if core is None else core]
        return self.pair(p, 8, piece, piece, self.at.across_core)

    def store(self, p):
        return pltpu.make_async_copy(self.stage.at[p % 2], self.out.at[p // 2, :, p % 2], self.osem.at[p % 2])

    def drain(self, d):
        at = self.at

        @pl.when(d < PIECES)
        def _():
            p = d
            self.x_one(p).wait()

            def add(i):
                z, y = i // 2, i % 2
                more = self.s0[p % RING, z, y, self.mine, self.front].astype(WIDE)
                self.l1a[p, z, y] = (self.l1a[p, z, y].astype(WIDE) + more).astype(LOW)

            for_each(8, add)
            self.y_two(p).start()
            self.y_one(p).wait()

            def add_too(z):
                more = self.s0[p % RING, z, at.y, :, self.back].astype(WIDE)
                self.l1b[p, z] = (self.l1b[p, z].astype(WIDE) + more).astype(LOW)

            for_each(4, add_too)
            self.x_two(p).start()

        @pl.when(jnp.logical_and(d >= 1, d < PIECES + 1))
        def _():
            p = d - 1
            self.y_two(p).wait()
            self.x_two(p).wait()

            def add(z):
                one = self.l2[p, z, :, self.front].astype(WIDE) + self.l1a[p, z, at.y].astype(WIDE)
                two = self.l2[p, z, :, self.back].astype(WIDE) + self.l1b[p, z, self.mine].astype(WIDE)
                self.l2[p, z, :, self.front] = one.astype(LOW)
                self.l2[p, z, :, self.back] = two.astype(LOW)

            for_each(4, add)
            for k in range(1, 4):
                self.z_copy(p, k).start()

        @pl.when(jnp.logical_and(d >= 2, d < PIECES + 2))
        def _():
            p = d - 2
            total = self.l2[p, at.z].astype(WIDE)
            for k in range(1, 4):
                self.z_copy(p, k).wait()
            for k in range(3):
                total = total + self.l3[p, k].astype(WIDE)
            self.la[p, at.core, at.x] = total.astype(LOW)
            self.x_back(p).start()

        @pl.when(jnp.logical_and(d >= 3, d < PIECES + 3))
        def _():
            p = d - 3
            self.x_back(p, 1 - at.x).wait_recv()
            self.core_back(p).start()

        @pl.when(jnp.logical_and(d >= 4, d < PIECES + 4))
        def _():
            p = d - 4
            self.x_back(p).wait_send()
            self.core_back(p).wait_send()
            self.core_back(p, 1 - at.core).wait_recv()
            pl.when(p >= 2)(lambda: self.store(p - 2).wait())
            self.stage[p % 2] = self.la[p].astype(WIDE)
            self.store(p).start()

    drains = PIECES + 4

    def run(self, lo, hi):
        def one(d, carry):
            self.drain(d)
            return carry

        lax.fori_loop(lo, hi, one, 0)

    def end(self):
        self.core_copy(BLOCKS - 2).wait_send()
        self.core_copy(BLOCKS - 1).wait_send()
        self.store(PIECES - 2).wait()
        self.store(PIECES - 1).wait()


REDUCE_SCRATCH = [
    pltpu.VMEM((2, 4, 2, 2, 32, 1024), LOW),
    pltpu.VMEM((RING, 4, 2, 32, 1024), LOW),
    pltpu.VMEM((PIECES, 4, 2, 16, FRONT), LOW),
    pltpu.VMEM((PIECES, 4, 32, 1024 - FRONT), LOW),
    pltpu.VMEM((PIECES, 4, 16, 1024), LOW),
    pltpu.VMEM((PIECES, 3, 16, 1024), LOW),
    pltpu.VMEM((PIECES, 2, 2, 16, 1024), LOW),
    pltpu.VMEM((2, 2, 2, 16, 1024), WIDE),
    pltpu.SemaphoreType.DMA((BLOCKS,)),
    pltpu.SemaphoreType.DMA((BLOCKS,)),
    pltpu.SemaphoreType.DMA((4,)),
    pltpu.SemaphoreType.DMA((PIECES, 9)),
    pltpu.SemaphoreType.DMA((PIECES, 9)),
    pltpu.SemaphoreType.DMA((2,)),
]


def sum_vectors(at, parts, got, sums, out, send, recv):
    def part(i):
        return remote(parts.at[at.shards[i]], got.at[i], send.at[i], recv.at[i], at.group[i])

    reps = [at.across_x, at.across_core, at.diagonal]

    def rest(i):
        return remote(sums.at[3], sums.at[i], send.at[7 + i], recv.at[7 + i], reps[i])

    def start():
        for i in range(7):
            part(i).start()

    def middle():
        total = parts[at.f]
        for i in range(7):
            part(i).wait()
            total = total + got[i]
        sums[3] = total
        for i in range(3):
            rest(i).start()

    def end():
        total = sums[3]
        for i in range(3):
            rest(i).wait()
            total = total + sums[i]
        out[...] = total

    return start, middle, end


COT, NORMED2, PAIR, GRAD_UP, QUERY, KEY, VALUE, NORMED1, TOKENS = 0, 1, 2, 4, 5, 6, 7, 8, 9
GRAD_BRANCH, CONTEXT, GRAD_CONTEXT = 2, 3, 4


def backward_kernel(comm, seqs, *refs):
    refs = list(refs)
    take = lambda n: [refs.pop(0) for _ in range(n)]
    full, cot_h, activ_h, slope_h, normed2_h, mid_h, q_h, k_h, v_h, ctx_h, tokens_h = take(11)
    table, mods, feat, cosine, sine = take(5)
    if comm:
        out, vec_out, input_o, own, l0 = take(5)
    else:
        out, vec_out, input_o = take(3)
    pool, gn, mid, weights, slots, sums, gtab, sem_in, sem_pair, sem_w, sem_mid, sem_slot = take(12)
    if comm:
        parts, vgot, vsums, vsend, vrecv = take(5)
        red = Reduce(slots, own, l0, out, *refs)
    tokens_n = pool.shape[1]
    per = tokens_n // seqs

    def fetch(src, i):
        return pltpu.make_async_copy(src, pool.at[i], sem_in.at[i])

    def fetch_pair(src, j):
        return pltpu.make_async_copy(src.at[j], pool.at[PAIR + j % 2], sem_pair.at[j % 2])

    def fetch_w(c, slot):
        return pltpu.make_async_copy(full.at[c], weights.at[slot], sem_w.at[slot])

    mid_in = pltpu.make_async_copy(mid_h, mid, sem_mid)
    fetch(cot_h, COT).start()
    fetch_pair(activ_h, 0).start()
    fetch_pair(activ_h, 1).start()
    fetch(normed2_h, NORMED2).start()
    fetch_w(9, 0).start()
    fetch_w(5, 1).start()
    mid_in.start()
    for src, i in ((q_h, QUERY), (k_h, KEY), (v_h, VALUE), (tokens_h, TOKENS)):
        fetch(src, i).start()
    if comm:
        red.begin()
        run, load, feed = red.run, red.load, red.feed
    else:
        run = load = feed = lambda *a: None
    when = pl.when if comm else (lambda cond: lambda body: None)

    half_cols = lambda h: slice(h * HALF, (h + 1) * HALF)

    def half_rows(slot, h):
        if comm:
            return weights[slot, 2 * h : 2 * h + 2].reshape(HALF, 1024)
        return weights[slot, half_cols(h), :]

    def produce(b, lhs, rhs_of):
        if comm:
            red.free(b)
        else:
            pl.when(b >= 2)(lambda: pltpu.make_async_copy(slots.at[b % 2], out.at[b - 2], sem_slot.at[b % 2]).wait())
        for h in range(2):
            block = rhs_of(lhs, h).astype(LOW)
            if comm:
                slots[b % 2, :, :, :, :, :, half_cols(h)] = block.reshape(4, 2, 2, 2, 32, HALF)
            else:
                slots[b % 2, :, half_cols(h)] = block
        if comm:
            red.produced(b)
        else:
            pltpu.make_async_copy(slots.at[b % 2], out.at[b], sem_slot.at[b % 2]).start()

    def times(i):
        return lambda lhs, h: lax.dot_general(lhs[...], pool[i, :, half_cols(h)], TN, preferred_element_type=WIDE)

    ones = jnp.ones((8, tokens_n), LOW)

    def column_sums(i, row):
        gtab[pl.ds(row, 1), :] = jnp.dot(ones, pool[i], preferred_element_type=WIDE)[:1]

    fetch(cot_h, COT).wait()

    def down(j):
        fetch_pair(activ_h, j).wait()
        produce(j, pool.at[PAIR + j % 2], times(COT))

        @pl.when(j < 2)
        def _():
            fetch_pair(activ_h, j + 2).start()

        @pl.when(j >= 2)
        def _():
            fetch_pair(slope_h, j - 2).start()

        @when(j == 0)
        def _():
            load(0)
            feed(0)

        when(j == 2)(lambda: load(1))

        @when(j == 3)
        def _():
            feed(1)
            load(2)
            run(0, 1)

    for_each(4, down)
    column_sums(COT, BIAS_D)
    fetch(normed2_h, NORMED2).wait()

    def up(j):
        fetch_pair(slope_h, j).wait()
        fetch_w(9 + j, 0).wait()
        for h in range(2):
            grad = lax.dot_general(pool[COT], half_rows(0, h), NT, preferred_element_type=WIDE)
            grad = grad * pool[PAIR + j % 2, :, half_cols(h)].astype(WIDE)
            pool[GRAD_UP, :, half_cols(h)] = grad.astype(LOW)

        @pl.when(j < 3)
        def _():
            fetch_w(10 + j, 0).start()

        pl.when(j < 2)(lambda: fetch_pair(slope_h, j + 2).start())
        feed(2 + j)
        run(1 + 2 * j, 2 + 2 * j)
        column_sums(GRAD_UP, BIAS_U + j)
        produce(4 + j, pool.at[NORMED2], times(GRAD_UP))
        fetch_w(5 + j, 1).wait()
        for h in range(2):
            more = lax.dot_general(pool[GRAD_UP], half_rows(1, h), NT, preferred_element_type=WIDE)

            @pl.when(j == 0)
            def _():
                gn[:, half_cols(h)] = more

            @pl.when(j > 0)
            def _():
                gn[:, half_cols(h)] = gn[:, half_cols(h)] + more

        @pl.when(j < 3)
        def _():
            fetch_w(6 + j, 1).start()

        load(3 + j)
        run(2 + 2 * j, 3 + 2 * j)

    for_each(4, up)
    fetch_w(4, 0).start()
    fetch_w(1, 1).start()
    fetch(ctx_h, CONTEXT).start()

    sums[...] = jnp.zeros_like(sums)

    def norm_back(which, gain, value_of, done):
        def body(i):
            rows = rows_at(i)
            s = i // (per // TILE)
            at_scale, at_shift = 2 * which * seqs + s, (2 * which + 1) * seqs + s
            scale = table[gain : gain + 1, :] + row_of(mods, at_scale)
            normed, inverse = normalise(value_of(rows).astype(WIDE))
            grad = gn[rows, :]
            sums[pl.ds(at_scale, 1), :] += jnp.sum(grad * normed, axis=0, keepdims=True)
            sums[pl.ds(at_shift, 1), :] += jnp.sum(grad, axis=0, keepdims=True)
            hat = grad * scale
            done(rows, inverse * (hat - lane_mean(hat) - normed * lane_mean(hat * normed)))

        for_each(tokens_n // TILE, body)
        for n in range(2):
            at = (2 * which + n) * seqs
            gtab[gain + n : gain + n + 1, :] = jnp.sum(sums[at : at + seqs, :], axis=0, keepdims=True)

    mid_in.wait()

    def done2(rows, grad):
        total = pool[COT, rows, :].astype(WIDE) + grad
        mid[rows, :] = total
        pool[GRAD_BRANCH, rows, :] = total.astype(LOW)

    norm_back(1, GAIN2, lambda rows: mid[rows, :], done2)
    feed(6)
    load(7)
    run(9, 10)

    fetch(ctx_h, CONTEXT).wait()
    column_sums(GRAD_BRANCH, BIAS_O)
    produce(8, pool.at[CONTEXT], times(GRAD_BRANCH))
    fetch_w(4, 0).wait()
    for h in range(2):
        grad = lax.dot_general(pool[GRAD_BRANCH], half_rows(0, h), NT, preferred_element_type=WIDE)
        pool[GRAD_CONTEXT, :, half_cols(h)] = grad.astype(LOW)
    fetch_w(2, 0).start()
    feed(7)
    load(8)
    run(10, 11)

    for src, i in ((q_h, QUERY), (k_h, KEY), (v_h, VALUE), (tokens_h, TOKENS)):
        fetch(src, i).wait()
    modulated(pool.at[TOKENS], pool.at[NORMED1], table, mods, GAIN1, 0, seqs)
    feed(8)

    lane = lax.broadcasted_iota(jnp.int32, (1, 128), 1)
    first_head = (lane < 64).astype(WIDE)
    second_head = 1.0 - first_head

    def split(v):
        return jnp.concatenate([v * first_head.astype(LOW), v * second_head.astype(LOW)], axis=0)

    def unturned(v):
        return v * cosine[...] - swapped(v) * sine[...]

    def heads(n):
        cols = pl.ds(pl.multiple_of(n * 128, 128), 128)
        for s in range(seqs):
            rows = slice(s * per, (s + 1) * per)
            keys = pool[KEY, rows, cols]
            both = split(pool[QUERY, rows, cols])
            grads = split(pool[GRAD_CONTEXT, rows, cols])
            scores = lax.dot_general(both, keys, NT, preferred_element_type=WIDE)
            grown = jnp.exp(scores - jnp.max(scores, axis=-1, keepdims=True))
            probs = grown / jnp.sum(grown, axis=-1, keepdims=True)
            grad_probs = lax.dot_general(grads, pool[VALUE, rows, cols], NT, preferred_element_type=WIDE)
            inner = jnp.sum(grad_probs * probs, axis=-1, keepdims=True)
            grad_scores = (probs * (grad_probs - inner)).astype(LOW)
            grad_v = lax.dot_general(probs.astype(LOW), grads, TN, preferred_element_type=WIDE)
            grad_k = lax.dot_general(grad_scores, both, TN, preferred_element_type=WIDE)
            grad_q = jnp.dot(grad_scores, keys, preferred_element_type=WIDE)
            grad_q = (grad_q[:per] * first_head + grad_q[per:] * second_head) * 0.125
            pool[QUERY, rows, cols] = unturned(grad_q).astype(LOW)
            pool[KEY, rows, cols] = unturned(grad_k).astype(LOW)
            pool[VALUE, rows, cols] = grad_v.astype(LOW)
        when(n < 7)(lambda: run(11 + n, 12 + n))

    for_each(8, heads)

    def project(j):
        column_sums(QUERY + j, BIAS_P + j)
        produce(9 + j, pool.at[NORMED1], times(QUERY + j))
        when(j == 1)(lambda: load(9))

        @when(j == 2)
        def _():
            feed(9)
            load(10)

    for_each(3, project)

    def project_back(j):
        slot = (1 + j) % 2
        fetch_w(1 + j, slot).wait()
        for h in range(2):
            more = lax.dot_general(pool[QUERY + j], half_rows(slot, h), NT, preferred_element_type=WIDE)

            @pl.when(j == 0)
            def _():
                gn[:, half_cols(h)] = more

            @pl.when(j > 0)
            def _():
                gn[:, half_cols(h)] = gn[:, half_cols(h)] + more

        pl.when(j == 0)(lambda: fetch_w(3, 1).start())
        when(j < 2)(lambda: feed(10 + j))
        when(j == 0)(lambda: load(11))
        run(18 + j, 19 + j)

    for_each(3, project_back)

    def done1(rows, grad):
        mid[rows, :] = mid[rows, :] + grad

    norm_back(0, GAIN1, lambda rows: pool[TOKENS, rows, :], done1)
    input_copy = pltpu.make_async_copy(mid, input_o, sem_mid)
    input_copy.start()
    if comm:
        for f in range(8):
            for row in range(13):
                r, b = vector_spot(row, f)
                parts[f, row : row + 1, :] = gtab[r : r + 1, b * 128 : (b + 1) * 128]
            parts[f, 13:16, :] = jnp.zeros((3, 128), WIDE)
        start, middle, end = sum_vectors(red.at, parts, vgot, vsums, vec_out, vsend, vrecv)
        start()
    else:
        vec_out[...] = gtab[...]

    def outer(lhs, h):
        terms = sums[:, half_cols(h)]
        high = terms.astype(LOW)
        rest = (terms - high.astype(WIDE)).astype(LOW)
        return lax.dot_general(lhs[...], high, TN, preferred_element_type=WIDE) + lax.dot_general(
            lhs[...], rest, TN, preferred_element_type=WIDE
        )

    produce(12, feat, outer)
    load(12)
    feed(12)
    if comm:
        run(21, 24)
        middle()
        run(24, 28)
        end()
        run(28, red.drains)
        red.end()
    else:
        for b in (11, 12):
            pltpu.make_async_copy(slots.at[b % 2], out.at[b], sem_slot.at[b % 2]).wait()
    input_copy.wait()


def backward_call(comm, full, cot, saved, tokens, table, mods, feat, cosine, sine, seqs):
    n, width = tokens.shape
    vmem, hbm = pl.BlockSpec(memory_space=pltpu.VMEM), pl.BlockSpec(memory_space=pl.ANY)
    q, k, v, ctx, mid, normed2, activ, slope = saved
    block = (4, 2, 2, 2, 32, width) if comm else (width, width)
    outs = [
        (jax.ShapeDtypeStruct((BLOCKS, 2, 2, 2, 16, width) if comm else (BLOCKS, width, width), WIDE if comm else LOW), hbm),
        (jax.ShapeDtypeStruct((16, 128) if comm else (16, width), WIDE), vmem),
        (jax.ShapeDtypeStruct((n, width), WIDE), hbm),
    ]
    extra = []
    if comm:
        part = jax.ShapeDtypeStruct((BLOCKS, 4, 2, 2, 32, width), LOW)
        outs += [(part, hbm), (part, hbm)]
        extra = [
            pltpu.VMEM((8, 16, 128), WIDE),
            pltpu.VMEM((7, 16, 128), WIDE),
            pltpu.VMEM((4, 16, 128), WIDE),
            pltpu.SemaphoreType.DMA((10,)),
            pltpu.SemaphoreType.DMA((10,)),
        ] + REDUCE_SCRATCH
        full = full.reshape((BLOCKS,) + block)
    got = pl.pallas_call(
        functools.partial(backward_kernel, comm, seqs),
        out_shape=tuple(s for s, _ in outs),
        in_specs=[hbm] * 11 + [vmem] * 5,
        out_specs=tuple(m for _, m in outs),
        scratch_shapes=[
            pltpu.VMEM((10, n, width), LOW),
            pltpu.VMEM((n, width), WIDE),
            pltpu.VMEM((n, width), WIDE),
            pltpu.VMEM((2,) + block, LOW),
            pltpu.VMEM((2,) + block, LOW),
            pltpu.VMEM((feat.shape[0], width), WIDE),
            pltpu.VMEM((16, width), WIDE),
            pltpu.SemaphoreType.DMA((10,)),
            pltpu.SemaphoreType.DMA((2,)),
            pltpu.SemaphoreType.DMA((2,)),
            pltpu.SemaphoreType.DMA,
            pltpu.SemaphoreType.DMA((2,)),
        ]
        + extra,
        compiler_params=pltpu.CompilerParams(
            collective_id=1 if comm else None, has_side_effects=comm, vmem_limit_bytes=62 * 2**20
        ),
        name="backward",
    )(full, cot, activ, slope, normed2, mid, q, k, v, ctx, tokens, table, mods, feat, cosine, sine)
    return got[0], got[1], got[2]


def rotary_constants(length, head_dim):
    half_width = head_dim // 2
    inverse = np.exp(np.arange(half_width, dtype=np.float32) * np.float32(-math.log(10000.0) / half_width))
    angles = np.arange(length, dtype=np.float32)[:, None] * inverse[None, :]
    cosine, sine = np.cos(angles), np.sin(angles)
    pair = np.concatenate([cosine, cosine], axis=1), np.concatenate([-sine, sine], axis=1)
    return tuple(np.concatenate([t, t], axis=1).astype(np.float32) for t in pair)


def wide_features(noise_times, shards_of, width):
    each = TE // shards_of
    half_width = TE // 2
    column = np.arange(width)
    feature = column // (4 * each) * each + column % each
    part = column // each % 4
    rates = np.exp((feature % half_width).astype(np.float32) * np.float32(math.log(100.0) / half_width))
    phases = (jnp.log(noise_times) * 0.25)[:, None] * rates[None, :]
    feat = jnp.where((feature < half_width)[None, :], jnp.sin(phases), jnp.cos(phases))
    chosen = (part[None, :] == np.arange(4)[:, None])[:, None, :]
    feat = jnp.where(chosen, feat[None], 0.0).reshape(-1, width).astype(LOW)
    pad = -feat.shape[0] % 32
    return jnp.pad(feat, ((0, pad), (0, 0)))


def pack_local(weights):
    project, output, up, down, time1, time2 = weights
    rows, width = output.shape
    shards_of = width // rows
    up_blocks = up.reshape(rows, shards_of, 4, rows).transpose(2, 0, 1, 3).reshape(4, rows, width)
    times = jnp.stack([time1, time2]).reshape(2, -1, 2, width).transpose(0, 2, 1, 3)
    return jnp.concatenate(
        [
            times.reshape(1, rows, width),
            project.reshape(rows, 3, width).transpose(1, 0, 2),
            output[None],
            up_blocks,
            down.reshape(4, rows, width),
        ]
    )


def pieces_of(flat, sizes):
    at, got = 0, []
    for size in sizes:
        got.append(flat[..., at : at + size])
        at += size
    return got


def shards(
    inputs,
    noise_times,
    cotangent,
    norm1_gain,
    norm1_bias,
    norm1_time,
    project_weight,
    project_bias,
    output_weight,
    output_bias,
    norm2_gain,
    norm2_bias,
    norm2_time,
    up_weight,
    up_bias,
    down_weight,
    down_bias,
):
    seqs = noise_times.shape[0]
    tokens_n, width = inputs.shape
    rows = output_weight.shape[0]
    shards_of = width // rows
    comm = shards_of == 8
    feat = wide_features(noise_times, shards_of, width)
    cosine, sine = rotary_constants(tokens_n // seqs, width // HEADS)
    own = pack_local((project_weight, output_weight, up_weight, down_weight, norm1_time, norm2_time))
    vectors = (norm1_gain, norm1_bias, project_bias, output_bias, norm2_gain, norm2_bias, up_bias, down_bias)
    sizes = [v.shape[0] for v in vectors]
    vec = jnp.concatenate(vectors)
    if comm:
        first, second = own, jnp.pad(vec.reshape(13, 128), ((0, 3), (0, 0)))
    else:
        first = lax.all_gather(own, "fsdp", axis=1, tiled=True)
        whole = pieces_of(lax.all_gather(vec, "fsdp", axis=0), sizes)
        whole[6] = whole[6].reshape(shards_of, 4, rows).transpose(1, 0, 2)
        second = jnp.concatenate([w.reshape(-1, width) for w in whole]).astype(WIDE)
        second = jnp.pad(second, ((0, 3), (0, 0)))
    full, table, mods, layer_out, *saved = forward_call(comm, first, second, inputs, feat, cosine, sine, seqs)
    mine, mine_vec, input_grad = backward_call(
        comm, full, cotangent, saved, inputs, table, mods, feat, cosine, sine, seqs
    )
    if comm:
        mine = mine.reshape(BLOCKS, rows, width)
        mine_vec = mine_vec.reshape(-1)
    else:
        mine = lax.psum_scatter(mine, "fsdp", scatter_dimension=1, tiled=True)
        mine = lax.psum(mine, "rep").astype(WIDE)
        whole = pieces_of(mine_vec[:13].reshape(-1), [shards_of * size for size in sizes])
        whole[6] = whole[6].reshape(4, shards_of, rows).transpose(1, 0, 2)
        mine_vec = jnp.concatenate([w.reshape(shards_of, -1) for w in whole], axis=1)
        mine_vec = lax.psum(lax.psum_scatter(mine_vec, "fsdp", scatter_dimension=0, tiled=True)[0], "rep")
    got = pieces_of(mine_vec, sizes)
    my_down = mine[0:4].reshape(4 * rows, width)
    my_up = mine[4:8].reshape(4, rows, shards_of, rows).transpose(1, 2, 0, 3).reshape(rows, 4 * width)
    my_project = mine[9:12].transpose(1, 0, 2).reshape(rows, 3 * width)
    my_times = mine[12].reshape(2, 2, -1, width).transpose(0, 2, 1, 3).reshape(2, -1, 2 * width)
    return (
        layer_out,
        input_grad,
        got[0],
        got[1],
        my_times[0],
        my_project,
        got[2],
        mine[8],
        got[3],
        got[4],
        got[5],
        my_times[1],
        my_up,
        got[6],
        my_down,
        got[7],
    )


def solution(mesh):
    placed = (
        P(("rep", "fsdp"), None),
        P(("rep", "fsdp")),
        P(("rep", "fsdp"), None),
        P("fsdp"),
        P("fsdp"),
        P("fsdp", None),
        P("fsdp", None),
        P("fsdp"),
        P("fsdp", None),
        P("fsdp"),
        P("fsdp"),
        P("fsdp"),
        P("fsdp", None),
        P("fsdp", None),
        P("fsdp"),
        P("fsdp", None),
        P("fsdp"),
    )
    return jax.shard_map(
        shards,
        mesh=mesh,
        in_specs=placed,
        out_specs=(
            P(("rep", "fsdp"), None),
            P(("rep", "fsdp"), None),
            P("fsdp"),
            P("fsdp"),
            P("fsdp", None),
            P("fsdp", None),
            P("fsdp"),
            P("fsdp", None),
            P("fsdp"),
            P("fsdp"),
            P("fsdp"),
            P("fsdp", None),
            P("fsdp", None),
            P("fsdp"),
            P("fsdp", None),
            P("fsdp"),
        ),
        check_vma=False,
    )
```

```python
import functools
import math

import jax
import jax.numpy as jnp
import numpy as np
from jax import lax
from jax.experimental import pallas as pl
from jax.experimental.pallas import tpu as pltpu
from jax.sharding import PartitionSpec as P

HEADS = 16
TE = 256
epsilon = 1e-05


MESH = pl.DeviceIdType.MESH
LOW, WIDE = jnp.bfloat16, jnp.float32
FRONT = 384
BLOCKS = 13
PIECES = 2 * BLOCKS
NT = (((1,), (1,)), ((), ()))
TN = (((0,), (0,)), ((), ()))


class Place:
    def __init__(self):
        r, f = lax.axis_index("rep"), lax.axis_index("fsdp")
        self.r, self.f = r, f
        self.x, self.core = r // 2, r % 2
        self.z, self.y = f // 2, f % 2
        z = self.z
        self.zs = [z, z + 1 - 2 * (z % 2), (z + 2) % 4, 3 - z]
        self.same = [zk * 2 + self.y for zk in self.zs]
        self.other = [zk * 2 + 1 - self.y for zk in self.zs]
        self.across_x = ((1 - self.x) * 2 + self.core, f)
        self.across_y = (r, self.other[0])
        self.across_core = (self.x * 2 + 1 - self.core, f)
        self.diagonal = ((1 - self.x) * 2 + 1 - self.core, f)
        self.along_z = [(r, fk) for fk in self.same]
        self.shards = self.same[1:] + self.other
        self.group = [(r, fk) for fk in self.shards]


def greet(peers):
    barrier = pltpu.get_barrier_semaphore()
    for peer in peers:
        pl.semaphore_signal(barrier, inc=1, device_id=peer, device_id_type=MESH)
    pl.semaphore_wait(barrier, len(peers))


def remote(src, dst, send, recv, peer):
    return pltpu.make_async_remote_copy(
        src_ref=src, dst_ref=dst, send_sem=send, recv_sem=recv, device_id=peer, device_id_type=MESH
    )


class Gather:
    def __init__(self, own, vec, full, vecs, send, recv, vsend, vrecv, lsem):
        self.at = Place()
        self.own, self.full, self.send, self.recv, self.lsem = own, full, send, recv, lsem
        self.vec, self.vecs, self.vsend, self.vrecv = vec, vecs, vsend, vrecv
        x = self.at.x
        self.middle = jnp.logical_and(self.at.z >= 1, self.at.z <= 2)
        rest = 1024 - FRONT
        self.mine = pl.ds(pl.multiple_of(x * FRONT, 128), rest)
        self.xcols = pl.ds(pl.multiple_of(x * rest, 128), FRONT)
        self.xland = pl.ds(pl.multiple_of((1 - x) * rest, 128), FRONT)

    def spot(self, c, z, y, cols, core=None):
        core = self.at.core if core is None else core
        return self.full.at[c // 2, z, y, core, c % 2, :, cols]

    def pair(self, c, i, src, dst, peer):
        return remote(src, dst, self.send.at[c, i], self.recv.at[c, i], peer)

    def owned(self, c, cols):
        return self.own.at[c // 2, pl.ds(pl.multiple_of(self.at.core * 64 + c % 2 * 32, 32), 32), cols]

    def z_copy(self, c, k):
        at = self.at
        src = self.owned(c, self.mine)
        return self.pair(c, k - 1, src, self.spot(c, at.z, at.y, self.mine), at.along_z[k])

    def z_relay(self, c):
        dst = self.spot(c, self.at.zs[2], self.at.y, self.mine)
        return remote(dst, dst, self.send.at[c, 12], self.recv.at[c, 2], self.at.along_z[1])

    def z_land(self, c, k):
        dst = self.spot(c, self.at.zs[k], self.at.y, self.mine)
        return self.pair(c, k - 1, dst, dst, self.at.along_z[k])

    def y_copy(self, c, k):
        at = self.at
        dst = self.spot(c, at.zs[k], at.y, self.mine)
        src = self.owned(c, self.mine) if k == 0 else dst
        return self.pair(c, 3 + k, src, dst, at.across_y)

    def y_land(self, c, k):
        dst = self.spot(c, self.at.zs[k], 1 - self.at.y, self.mine)
        return self.pair(c, 3 + k, dst, dst, self.at.across_y)

    def x_place(self, c, k, cols):
        at = self.at
        if k < 3:
            return self.spot(c, at.zs[k + 1], at.y, cols)
        return self.spot(c, slice(None), 1 - at.y, cols)

    def x_copy(self, c, k):
        src = self.x_place(c, k, self.xcols)
        return self.pair(c, 7 + k, src, src, self.at.across_x)

    def x_land(self, c, k):
        dst = self.x_place(c, k, self.xland)
        return self.pair(c, 7 + k, dst, dst, self.at.across_x)

    def core_copy(self, c, core=None):
        part = self.spot(c, slice(None), slice(None), slice(None), core)
        return self.pair(c, 11, part, part, self.at.across_core)

    def local(self, c):
        at = self.at
        dst = self.spot(c, at.z, at.y, slice(None))
        return pltpu.make_async_copy(self.owned(c, slice(None)), dst, self.lsem.at[c])

    def first(self, c):
        for k in range(1, 3):
            self.z_copy(c, k).start()
        pl.when(self.middle)(lambda: self.z_copy(c, 3).start())
        self.y_copy(c, 0).start()
        self.local(c).start()

    ahead = 4

    def begin(self):
        at = self.at
        greet([at.across_core, at.across_x] + at.group)
        for i, peer in enumerate(at.group):
            remote(self.vec, self.vecs.at[at.f], self.vsend.at[i], self.vrecv.at[i], peer).start()

    def start(self):
        for c in range(self.ahead):
            self.first(c)

    def vectors(self):
        at = self.at
        self.vecs[at.f] = self.vec[...]
        for i, peer in enumerate(at.group):
            remote(self.vec, self.vecs.at[at.shards[i]], self.vsend.at[i], self.vrecv.at[i], peer).wait()

    lag_x, lag_core, lag_done = 2, 4, 5

    def step(self, t):
        lag_x, lag_core, lag_done = self.lag_x, self.lag_core, self.lag_done

        @pl.when(t + self.ahead < PIECES)
        def _():
            self.first(t + self.ahead)

        @pl.when(t < PIECES)
        def _():
            for k in (2, 1, 3):
                self.z_land(t, k).wait_recv()
                if k == 2:
                    pl.when(self.middle)(lambda: self.z_relay(t).start())
                self.y_copy(t, k).start()

        @pl.when(jnp.logical_and(t >= lag_x, t < PIECES + lag_x))
        def _():
            c = t - lag_x
            for k in range(4):
                if k == 3:
                    for j in range(4):
                        self.y_land(c, j).wait_recv()
                self.x_copy(c, k).start()

        @pl.when(jnp.logical_and(t >= lag_core, t < PIECES + lag_core))
        def _():
            c = t - lag_core
            self.local(c).wait()
            for k in range(4):
                self.x_land(c, k).wait_recv()
            self.core_copy(c).start()

        @pl.when(jnp.logical_and(t >= lag_done, t < PIECES + lag_done))
        def _():
            c = t - lag_done
            self.core_copy(c, 1 - self.at.core).wait_recv()
            for k in range(1, 3):
                self.z_copy(c, k).wait_send()

            @pl.when(self.middle)
            def _():
                self.z_copy(c, 3).wait_send()
                self.z_relay(c).wait_send()

            for k in range(4):
                self.y_copy(c, k).wait_send()
                self.x_copy(c, k).wait_send()
            self.core_copy(c).wait_send()

    steps = PIECES + lag_done

    def ready(self, block):
        return 2 * block + 2 + self.lag_done

    def run(self, lo, hi):
        def one(t, carry):
            self.step(t)
            return carry

        lax.fori_loop(lo, hi, one, 0)


GATHER_SCRATCH = [
    pltpu.VMEM((8, 16, 128), WIDE),
    pltpu.SemaphoreType.DMA((PIECES, 13)),
    pltpu.SemaphoreType.DMA((PIECES, 12)),
    pltpu.SemaphoreType.DMA((7,)),
    pltpu.SemaphoreType.DMA((7,)),
    pltpu.SemaphoreType.DMA((PIECES,)),
]


GAIN1, BIAS1, BIAS_P, BIAS_O, GAIN2, BIAS2, BIAS_U, BIAS_D = 0, 1, 2, 5, 6, 7, 8, 12
HALF = 512
TILE = 32


def vector_spot(row, f):
    for first, count in ((BIAS_P, 3), (BIAS_U, 4)):
        if first <= row < first + count:
            block = f * count + row - first
            return first + block // 8, block % 8
    return row, f


def for_each(count, body):
    def one(i, carry):
        body(i)
        return carry

    lax.fori_loop(0, count, one, 0)


def rows_at(i, size=TILE):
    return pl.ds(pl.multiple_of(i * size, size), size)


def lane_mean(v):
    return jnp.mean(v, axis=-1, keepdims=True)


def normalise(v):
    centred = v - lane_mean(v)
    inverse = lax.rsqrt(lane_mean(centred * centred) + epsilon)
    return centred * inverse, inverse


def row_of(ref, i):
    return ref[pl.ds(i, 1), :]


def modulated(ref, out, table, mods, gain, which, seqs):
    per = ref.shape[0] // seqs // TILE

    def body(i):
        s = i // per
        scale = table[gain : gain + 1, :] + row_of(mods, 2 * which * seqs + s)
        shift = table[gain + 1 : gain + 2, :] + row_of(mods, (2 * which + 1) * seqs + s)
        rows = rows_at(i)
        normed, _ = normalise(ref[rows, :].astype(WIDE))
        out[rows, :] = (normed * scale + shift).astype(LOW)

    for_each(ref.shape[0] // TILE, body)


def swapped(v):
    lane = lax.broadcasted_iota(jnp.int32, v.shape, 1)
    return jnp.where(lane % 64 < 32, pltpu.roll(v, 96, 1), pltpu.roll(v, 32, 1))


def pack(local, own, sems):
    project, output, up, down, time1, time2 = local
    pairs = [(t.at[:, pl.ds(1024 * h, 1024)], own.at[0, pl.ds(64 * n + 32 * h, 32)]) for n, t in enumerate((time1, time2)) for h in range(2)]
    pairs += [(project.at[:, pl.ds(1024 * j, 1024)], own.at[1 + j]) for j in range(3)] + [(output, own.at[4])]
    pairs += [(up.at[:, pl.ds(1024 * j, 1024)], own.at[5 + j]) for j in range(4)]
    pairs += [(down.at[pl.ds(128 * j, 128)], own.at[9 + j]) for j in range(4)]
    return [pltpu.make_async_copy(src, dst, sems.at[i]) for i, (src, dst) in enumerate(pairs)]


def forward_kernel(comm, seqs, *refs):
    refs = list(refs)
    take = lambda n: [refs.pop(0) for _ in range(n)]
    if comm:
        local, vec = take(6), take(1)[0]
    else:
        full_in, table_in = take(2)
    tokens_hbm, feat, cosine, sine = take(4)
    if comm:
        (full,) = take(1)
    else:
        full = full_in
    table, mods = take(2)
    out_o, q_o, k_o, v_o, ctx_o, mid_o, normed2_o, activ_o, slope_o = take(9)
    tokens, weights, normed, q, k, v, ctx, mid, acc, activ, slope, wide, out_low = take(13)
    sem_in, sem_w, sem_out = take(3)
    tokens_n = tokens.shape[0]
    per = tokens_n // seqs

    tokens_in = pltpu.make_async_copy(tokens_hbm, tokens, sem_in)
    tokens_in.start()
    if comm:
        own, sem_own = take(2)
        gather = Gather(own, vec, full, *refs)
        packing = pack(local, own, sem_own)
        for copy in packing:
            copy.start()
        gather.begin()
        for copy in packing:
            copy.wait()
        gather.start()
        gather.vectors()
        for f in range(8):
            block = gather.vecs[f]
            for row in range(13):
                r, b = vector_spot(row, f)
                table[r : r + 1, b * 128 : (b + 1) * 128] = block[row : row + 1, :]
        run = gather.run
    else:
        table[...] = table_in[...]
        run = lambda lo, hi: None

    def fetch(c):
        return pltpu.make_async_copy(full.at[c], weights.at[c % 2], sem_w.at[c % 2])

    def arrive(c, lo, hi):
        run(lo, hi)
        fetch(c).start()

    def weight(c):
        fetch(c).wait()
        return weights.at[c % 2]

    ready = Gather.lag_done + 2
    flat = (lambda w: w[...].reshape(1024, 1024)) if comm else (lambda w: w[...])

    saves = []

    def save(src, dst):
        copy = pltpu.make_async_copy(src, dst, sem_out.at[len(saves)])
        copy.start()
        saves.append(copy)

    arrive(0, 0, ready)
    w = weight(0)
    mods[...] = jnp.dot(feat[...], flat(w), preferred_element_type=WIDE)
    tokens_in.wait()
    arrive(1, ready, ready + 2)
    modulated(tokens, normed, table, mods, GAIN1, 0, seqs)

    for j, (dst, dst_o) in enumerate([(q, q_o), (k, k_o), (v, v_o)]):
        w = weight(1 + j)
        for h in range(2):
            cols = slice(h * HALF, (h + 1) * HALF)
            wide[...] = jnp.dot(normed[...], half_of(w, cols, comm), preferred_element_type=WIDE)
            run(ready + 2 + 2 * j + h, ready + 3 + 2 * j + h)
            if h == 1:
                fetch(2 + j).start()
            bias = table[BIAS_P + j : BIAS_P + j + 1, cols]

            def body(i, h=h, bias=bias, dst=dst, j=j):
                rows = rows_at(i)
                where = pl.ds(pl.multiple_of((i % (per // TILE)) * TILE, TILE), TILE)
                piece = wide[rows, :] + bias
                if j == 2:
                    dst[rows, h * HALF : (h + 1) * HALF] = piece.astype(LOW)
                    return
                for n in range(HALF // 128):
                    part = piece[:, n * 128 : (n + 1) * 128]
                    turned = part * cosine[where, :] + swapped(part) * sine[where, :]
                    if j == 0:
                        turned = turned * 0.125
                    at = h * HALF + n * 128
                    dst[rows, at : at + 128] = turned.astype(LOW)

            for_each(tokens_n // TILE, body)
        save(dst, dst_o)

    lane = lax.broadcasted_iota(jnp.int32, (1, 128), 1)
    first_head = (lane < 64).astype(WIDE)
    second_head = 1.0 - first_head

    def heads(n):
        cols = pl.ds(pl.multiple_of(n * 128, 128), 128)
        for s in range(seqs):
            rows = slice(s * per, (s + 1) * per)
            qs = q[rows, cols]
            both = jnp.concatenate([qs * first_head.astype(LOW), qs * second_head.astype(LOW)], axis=0)
            scores = lax.dot_general(both, k[rows, cols], NT, preferred_element_type=WIDE)
            grown = jnp.exp(scores - jnp.max(scores, axis=-1, keepdims=True))
            probs = (grown / jnp.sum(grown, axis=-1, keepdims=True)).astype(LOW)
            mixed = jnp.dot(probs, v[rows, cols], preferred_element_type=WIDE)
            ctx[rows, cols] = (mixed[:per] * first_head + mixed[per:] * second_head).astype(LOW)
        if comm:
            pl.when(n >= 2)(lambda: gather.step(ready + 6 + n))

    for_each(8, heads)
    save(ctx, ctx_o)

    w = weight(4)
    for h in range(2):
        cols = slice(h * HALF, (h + 1) * HALF)
        dot = jnp.dot(ctx[...], half_of(w, cols, comm), preferred_element_type=WIDE)
        mid[:, cols] = tokens[:, cols].astype(WIDE) + (dot + table[BIAS_O : BIAS_O + 1, cols])
    arrive(5, ready + 14, ready + 15)
    save(mid, mid_o)
    modulated(mid, normed, table, mods, GAIN2, 1, seqs)
    save(normed, normed2_o)

    def up(j):
        w = weight(5 + j)
        for h in range(2):
            cols = slice(h * HALF, (h + 1) * HALF)
            wide[...] = jnp.dot(normed[...], half_of(w, cols, comm), preferred_element_type=WIDE)
            if h == 0:
                once = ready + 15 + 2 * j - jnp.maximum(j - 2, 0)
                run(once, once + 1)
            else:
                run(ready + 16 + 2 * j, ready + 16 + 2 * j + (j < 2).astype(jnp.int32))
                fetch(6 + j).start()

            def body(i, h=h, cols=cols):
                rows = rows_at(i)
                u = wide[rows, :] + table[pl.ds(BIAS_U + j, 1), cols]
                phi = 0.5 + 0.5 * lax.erf(u * (0.5**0.5))
                bell = jnp.exp(-0.5 * (u * u)) * (1.0 / math.sqrt(2.0 * math.pi))
                result, grow = (u * phi).astype(LOW), (phi + u * bell).astype(LOW)
                place = pl.ds(pl.multiple_of((2 * j + h) * 128, 128), 128)
                for n in range(4):
                    activ[n, rows, place] = result[:, n * 128 : (n + 1) * 128]
                    slope[n, rows, place] = grow[:, n * 128 : (n + 1) * 128]

            for_each(tokens_n // TILE, body)

    for_each(4, up)
    save(activ, activ_o)
    save(slope, slope_o)

    def down(j):
        w = weight(9 + j)
        for h in range(2):
            cols = slice(h * HALF, (h + 1) * HALF)
            dot = jnp.dot(activ[j], half_of(w, cols, comm), preferred_element_type=WIDE)

            @pl.when(j == 0)
            def _():
                acc[:, cols] = mid[:, cols] + table[BIAS_D : BIAS_D + 1, cols] + dot

            @pl.when(j > 0)
            def _():
                acc[:, cols] = acc[:, cols] + dot

            if h == 0:
                pl.when(j < 3)(lambda: arrive(10 + j, ready + 21 + j, ready + 22 + j))

    for_each(4, down)
    out_low[...] = acc[...].astype(LOW)
    save(out_low, out_o)
    for copy in saves:
        copy.wait()


def half_of(w, cols, comm):
    if comm:
        return w[..., cols].reshape(1024, HALF)
    return w[:, cols]


def forward_call(comm, weights, vectors, tokens, feat, cosine, sine, seqs):
    n, width = tokens.shape
    vmem, hbm = pl.BlockSpec(memory_space=pltpu.VMEM), pl.BlockSpec(memory_space=pl.ANY)
    low = jax.ShapeDtypeStruct((n, width), LOW)
    wide = jax.ShapeDtypeStruct((n, width), WIDE)
    shape4 = jax.ShapeDtypeStruct((4, n, width), LOW)
    block = (4, 2, 2, 2, 32, width) if comm else (width, width)
    outs = [
        (jax.ShapeDtypeStruct((16, width), WIDE), vmem),
        (jax.ShapeDtypeStruct((feat.shape[0], width), WIDE), vmem),
    ] + [(s, hbm) for s in (low, low, low, low, low, wide, low, shape4, shape4)]
    extra = []
    if comm:
        outs = [(jax.ShapeDtypeStruct((BLOCKS,) + block, LOW), hbm)] + outs
        extra = [pltpu.VMEM((BLOCKS, 128, width), LOW), pltpu.SemaphoreType.DMA((16,))] + GATHER_SCRATCH
    buffer = pltpu.VMEM((n, width), LOW)
    got = pl.pallas_call(
        functools.partial(forward_kernel, comm, seqs),
        out_shape=tuple(s for s, _ in outs),
        in_specs=[hbm] * len(weights) + [vmem, hbm, vmem, vmem, vmem],
        out_specs=tuple(m for _, m in outs),
        scratch_shapes=[
            buffer,
            pltpu.VMEM((2,) + block, LOW),
            buffer,
            buffer,
            buffer,
            buffer,
            buffer,
            pltpu.VMEM((n, width), WIDE),
            pltpu.VMEM((n, width), WIDE),
            pltpu.VMEM((4, n, width), LOW),
            pltpu.VMEM((4, n, width), LOW),
            pltpu.VMEM((n, HALF), WIDE),
            buffer,
            pltpu.SemaphoreType.DMA,
            pltpu.SemaphoreType.DMA((2,)),
            pltpu.SemaphoreType.DMA((9,)),
        ]
        + extra,
        compiler_params=pltpu.CompilerParams(
            collective_id=0 if comm else None, has_side_effects=comm, vmem_limit_bytes=60 * 2**20
        ),
        name="forward",
    )(*weights, vectors, tokens, feat, cosine, sine)
    if not comm:
        return (weights[0], vectors) + tuple(got[1:])
    return (got[0].reshape(BLOCKS, width, width),) + tuple(got[1:])


RING = 10


class Reduce:
    def __init__(self, slots, own, l0, outs, *scratch):
        self.at = Place()
        self.slots, self.own, self.l0, self.outs = slots, own, l0, outs
        (self.held, self.s0, self.l1a, self.l1b, self.l2, self.l3, self.la) = scratch[:7]
        (self.bsend, self.brecv, self.lsem, self.send, self.recv, self.osem) = scratch[7:13]
        x = self.at.x
        self.front, self.back = pl.ds(0, FRONT), pl.ds(FRONT, 1024 - FRONT)
        self.mine = pl.ds(pl.multiple_of(x * 16, 16), 16)
        self.theirs = pl.ds(pl.multiple_of((1 - x) * 16, 16), 16)

    def begin(self):
        at = self.at
        greet([at.across_core, at.across_x, at.diagonal] + at.group)

    def core_copy(self, b):
        src = self.slots.at[b % 2, :, :, 1 - self.at.core]
        return remote(src, self.l0.at[b], self.bsend.at[b], self.brecv.at[b], self.at.across_core)

    def own_copy(self, b):
        return pltpu.make_async_copy(self.slots.at[b % 2, :, :, self.at.core], self.own.at[b], self.lsem.at[b % 2])

    def loads(self, b):
        return (
            pltpu.make_async_copy(self.own.at[b], self.held.at[0], self.lsem.at[2]),
            pltpu.make_async_copy(self.l0.at[b], self.held.at[1], self.lsem.at[3]),
        )

    def free(self, b):
        pl.when(b >= 2)(lambda: self.core_copy(b - 2).wait_send())

    def produced(self, b):
        self.core_copy(b).start()
        self.own_copy(b).start()

    def load(self, b):
        self.own_copy(b).wait()
        self.core_copy(b).wait_recv()
        for copy in self.loads(b):
            copy.start()

    def feed(self, b):
        for copy in self.loads(b):
            copy.wait()

        def add(i):
            z, y, h = i // 4, (i // 2) % 2, i % 2
            piece = self.held[0, z, y, h].astype(WIDE) + self.held[1, z, y, h].astype(WIDE)
            self.s0[(2 * b + h) % RING, z, y] = piece.astype(LOW)

        for_each(16, add)
        for h in range(2):
            self.x_one(2 * b + h).start()
            self.y_one(2 * b + h).start()

    def pair(self, p, i, src, dst, peer):
        return remote(src, dst, self.send.at[p, i], self.recv.at[p, i], peer)

    def x_one(self, p):
        src = self.s0.at[p % RING, :, :, self.theirs, self.front]
        return self.pair(p, 0, src, self.l1a.at[p], self.at.across_x)

    def y_one(self, p):
        src = self.s0.at[p % RING, :, 1 - self.at.y, :, self.back]
        return self.pair(p, 1, src, self.l1b.at[p], self.at.across_y)

    def y_two(self, p):
        return self.pair(p, 2, self.l1a.at[p, :, 1 - self.at.y], self.l2.at[p, :, :, self.front], self.at.across_y)

    def x_two(self, p):
        return self.pair(p, 3, self.l1b.at[p, :, self.theirs], self.l2.at[p, :, :, self.back], self.at.across_x)

    def z_copy(self, p, k):
        return self.pair(p, 3 + k, self.l2.at[p, self.at.zs[k]], self.l3.at[p, k - 1], self.at.along_z[k])

    def x_back(self, p, x=None):
        piece = self.la.at[p, self.at.core, pl.ds(pl.multiple_of((self.at.x if x is None else x) * 16, 16), 16)]
        return self.pair(p, 7, piece, piece, self.at.across_x)

    def core_back(self, p, core=None):
        piece = self.la.at[p, self.at.core if core is None else core]
        return self.pair(p, 8, piece, piece, self.at.across_core)

    def store(self, p, dsts):
        for core, dst in enumerate(dsts):
            pltpu.make_async_copy(self.la.at[p, core], dst, self.osem.at[p, core]).start()

    def store_all(self, p):
        project, output, up, down, *times = self.outs
        b, h = p // 2, p % 2

        def rows(core, first=0):
            return pl.ds(pl.multiple_of(first + core * 64 + h * 32, 32), 32)

        def cols(j):
            return pl.ds(pl.multiple_of(j * 1024, 1024), 1024)

        pl.when(b < 4)(lambda: self.store(p, [down.at[rows(c, b * 128)] for c in range(2)]))
        pl.when(jnp.logical_and(b >= 4, b < 8))(lambda: self.store(p, [up.at[rows(c), cols(b - 4)] for c in range(2)]))
        pl.when(b == 8)(lambda: self.store(p, [output.at[rows(c)] for c in range(2)]))
        pl.when(jnp.logical_and(b >= 9, b < 12))(lambda: self.store(p, [project.at[rows(c), cols(b - 9)] for c in range(2)]))
        pl.when(b == 12)(lambda: self.store(p, [t.at[:, cols(h)] for t in times]))

    lags = (2, 3, 5, 6)

    def drain(self, d):
        at, lags = self.at, self.lags

        @pl.when(d < PIECES)
        def _():
            p = d
            self.x_one(p).wait()

            def add(i):
                z, y = i // 2, i % 2
                more = self.s0[p % RING, z, y, self.mine, self.front].astype(WIDE)
                self.l1a[p, z, y] = (self.l1a[p, z, y].astype(WIDE) + more).astype(LOW)

            for_each(8, add)
            self.y_two(p).start()
            self.y_one(p).wait()

            def add_too(z):
                more = self.s0[p % RING, z, at.y, :, self.back].astype(WIDE)
                self.l1b[p, z] = (self.l1b[p, z].astype(WIDE) + more).astype(LOW)

            for_each(4, add_too)
            self.x_two(p).start()

        @pl.when(jnp.logical_and(d >= lags[0], d < PIECES + lags[0]))
        def _():
            p = d - lags[0]
            self.y_two(p).wait()
            self.x_two(p).wait()

            def add(z):
                one = self.l2[p, z, :, self.front].astype(WIDE) + self.l1a[p, z, at.y].astype(WIDE)
                two = self.l2[p, z, :, self.back].astype(WIDE) + self.l1b[p, z, self.mine].astype(WIDE)
                self.l2[p, z, :, self.front] = one.astype(LOW)
                self.l2[p, z, :, self.back] = two.astype(LOW)

            for_each(4, add)
            for k in range(1, 4):
                self.z_copy(p, k).start()

        @pl.when(jnp.logical_and(d >= lags[1], d < PIECES + lags[1]))
        def _():
            p = d - lags[1]
            total = self.l2[p, at.z].astype(WIDE)
            for k in range(1, 4):
                self.z_copy(p, k).wait()
            for k in range(3):
                total = total + self.l3[p, k].astype(WIDE)
            self.la[p, at.core, self.mine] = total.astype(LOW)
            self.x_back(p).start()

        @pl.when(jnp.logical_and(d >= lags[2], d < PIECES + lags[2]))
        def _():
            p = d - lags[2]
            self.x_back(p, 1 - at.x).wait_recv()
            self.core_back(p).start()

        @pl.when(jnp.logical_and(d >= lags[3], d < PIECES + lags[3]))
        def _():
            p = d - lags[3]
            self.x_back(p).wait_send()
            self.core_back(p).wait_send()
            self.core_back(p, 1 - at.core).wait_recv()
            self.store_all(p)

    drains = PIECES + lags[3]

    def run(self, lo, hi):
        def one(d, carry):
            self.drain(d)
            return carry

        lax.fori_loop(lo, hi, one, 0)

    def end(self):
        self.core_copy(BLOCKS - 2).wait_send()
        self.core_copy(BLOCKS - 1).wait_send()

        def stored(p):
            for core in range(2):
                pltpu.make_async_copy(self.la.at[p, core], self.outs[1].at[pl.ds(0, 32)], self.osem.at[p, core]).wait()

        for_each(PIECES, stored)


REDUCE_SCRATCH = [
    pltpu.VMEM((2, 4, 2, 2, 32, 1024), LOW),
    pltpu.VMEM((RING, 4, 2, 32, 1024), LOW),
    pltpu.VMEM((PIECES, 4, 2, 16, FRONT), LOW),
    pltpu.VMEM((PIECES, 4, 32, 1024 - FRONT), LOW),
    pltpu.VMEM((PIECES, 4, 16, 1024), LOW),
    pltpu.VMEM((PIECES, 3, 16, 1024), LOW),
    pltpu.VMEM((PIECES, 2, 32, 1024), LOW),
    pltpu.SemaphoreType.DMA((BLOCKS,)),
    pltpu.SemaphoreType.DMA((BLOCKS,)),
    pltpu.SemaphoreType.DMA((4,)),
    pltpu.SemaphoreType.DMA((PIECES, 9)),
    pltpu.SemaphoreType.DMA((PIECES, 9)),
    pltpu.SemaphoreType.DMA((PIECES, 2)),
]


def sum_vectors(at, parts, got, sums, out, send, recv):
    def part(i):
        return remote(parts.at[at.shards[i]], got.at[i], send.at[i], recv.at[i], at.group[i])

    reps = [at.across_x, at.across_core, at.diagonal]

    def rest(i):
        return remote(sums.at[3], sums.at[i], send.at[7 + i], recv.at[7 + i], reps[i])

    def start():
        for i in range(7):
            part(i).start()

    def middle():
        total = parts[at.f]
        for i in range(7):
            part(i).wait()
            total = total + got[i]
        sums[3] = total
        for i in range(3):
            rest(i).start()

    def end():
        total = sums[3]
        for i in range(3):
            rest(i).wait()
            total = total + sums[i]
        out[...] = total

    return start, middle, end


COT, NORMED2, PAIR, GRAD_UP, TOKENS, NORMED1 = 0, 1, 2, 4, 8, 9
GRAD_BRANCH, CONTEXT, QUERY, KEY, VALUE, GRAD_CONTEXT = 2, 3, 4, 5, 6, 7


def backward_kernel(comm, seqs, *refs):
    refs = list(refs)
    take = lambda n: [refs.pop(0) for _ in range(n)]
    full, cot_h, activ_h, slope_h, normed2_h, mid_h, q_h, k_h, v_h, ctx_h, tokens_h = take(11)
    table, mods, feat, cosine, sine = take(5)
    outs = take(6 if comm else 1)
    vec_out, input_o = take(2)
    if comm:
        own, l0 = take(2)
    else:
        (out,) = outs
    pool, gn, mid, weights, slots, sums, gtab, sem_in, sem_pair, sem_w, sem_mid, sem_slot = take(12)
    if comm:
        parts, vgot, vsums, vsend, vrecv = take(5)
        red = Reduce(slots, own, l0, outs, *refs)
    tokens_n = pool.shape[1]
    per = tokens_n // seqs

    def fetch(src, i):
        return pltpu.make_async_copy(src, pool.at[i], sem_in.at[i])

    def fetch_pair(src, j):
        return pltpu.make_async_copy(src.at[j], pool.at[PAIR + j % 2], sem_pair.at[j % 2])

    def fetch_w(c, slot):
        return pltpu.make_async_copy(full.at[c], weights.at[slot], sem_w.at[slot])

    mid_in = pltpu.make_async_copy(mid_h, mid, sem_mid)
    fetch(cot_h, COT).start()
    fetch_pair(activ_h, 0).start()
    fetch_pair(activ_h, 1).start()
    fetch(normed2_h, NORMED2).start()
    fetch_w(9, 0).start()
    fetch_w(10, 1).start()
    mid_in.start()
    fetch(tokens_h, TOKENS).start()
    if comm:
        red.begin()
        run, load, feed = red.run, red.load, red.feed
    else:
        run = load = feed = lambda *a: None
    when = pl.when if comm else (lambda cond: lambda body: None)

    half_cols = lambda h: slice(h * HALF, (h + 1) * HALF)

    def half_rows(slot, h):
        if comm:
            return weights[slot, 2 * h : 2 * h + 2].reshape(HALF, 1024)
        return weights[slot, half_cols(h), :]

    def produce(b, lhs, rhs_of):
        if comm:
            red.free(b)
        else:
            pl.when(b >= 2)(lambda: pltpu.make_async_copy(slots.at[b % 2], out.at[b - 2], sem_slot.at[b % 2]).wait())
        for h in range(2):
            block = rhs_of(lhs, h).astype(LOW)
            if comm:
                slots[b % 2, :, :, :, :, :, half_cols(h)] = block.reshape(4, 2, 2, 2, 32, HALF)
            else:
                slots[b % 2, :, half_cols(h)] = block
        if comm:
            red.produced(b)
        else:
            pltpu.make_async_copy(slots.at[b % 2], out.at[b], sem_slot.at[b % 2]).start()

    def times(i):
        return lambda lhs, h: lax.dot_general(lhs[...], pool[i, :, half_cols(h)], TN, preferred_element_type=WIDE)

    ones = jnp.ones((8, tokens_n), LOW)

    def column_sums(i, row):
        gtab[pl.ds(row, 1), :] = jnp.dot(ones, pool[i], preferred_element_type=WIDE)[:1]

    fetch(cot_h, COT).wait()

    def down(j):
        fetch_pair(activ_h, j).wait()
        produce(j, pool.at[PAIR + j % 2], times(COT))

        @pl.when(j < 2)
        def _():
            fetch_pair(activ_h, j + 2).start()

        @pl.when(j >= 2)
        def _():
            fetch_pair(slope_h, j - 2).start()

        @when(j == 0)
        def _():
            load(0)
            feed(0)

        when(j == 2)(lambda: load(1))

        @when(j == 3)
        def _():
            feed(1)
            load(2)
            run(0, 1)

    for_each(4, down)
    column_sums(COT, BIAS_D)
    fetch(normed2_h, NORMED2).wait()

    def activ_back(j):
        fetch_pair(slope_h, j).wait()
        fetch_w(9 + j, j % 2).wait()
        for h in range(2):
            grad = lax.dot_general(pool[COT], half_rows(j % 2, h), NT, preferred_element_type=WIDE)
            grad = (grad * pool[PAIR + j % 2, :, half_cols(h)].astype(WIDE)).astype(LOW)
            for n in range(4):
                f = 4 * h + n
                place = pl.ds(pl.multiple_of((f % 2 * 4 + j) * 128, 128), 128)
                pool[GRAD_UP + f // 2, :, place] = grad[:, n * 128 : (n + 1) * 128]

        pl.when(j < 2)(lambda: fetch_w(11 + j, j % 2).start())
        pl.when(j >= 2)(lambda: fetch_w(3 + j, j % 2).start())
        pl.when(j < 2)(lambda: fetch_pair(slope_h, j + 2).start())

        @when(j == 0)
        def _():
            feed(2)
            load(3)

        when(j == 1)(lambda: feed(3))
        run(1 + j, 2 + j)

    for_each(4, activ_back)

    def up(j):
        column_sums(GRAD_UP + j, BIAS_U + j)
        produce(4 + j, pool.at[NORMED2], times(GRAD_UP + j))
        fetch_w(5 + j, j % 2).wait()
        when(j >= 1)(lambda: feed(3 + j))
        run(5 + j, 6 + j)
        for h in range(2):
            more = lax.dot_general(pool[GRAD_UP + j], half_rows(j % 2, h), NT, preferred_element_type=WIDE)

            @pl.when(j == 0)
            def _():
                gn[:, half_cols(h)] = more

            @pl.when(j > 0)
            def _():
                gn[:, half_cols(h)] = gn[:, half_cols(h)] + more

        pl.when(j < 2)(lambda: fetch_w(7 + j, j % 2).start())
        load(4 + j)

    for_each(4, up)
    fetch_w(4, 0).start()
    fetch_w(1, 1).start()
    for src, i in ((ctx_h, CONTEXT), (q_h, QUERY), (k_h, KEY), (v_h, VALUE)):
        fetch(src, i).start()

    sums[...] = jnp.zeros_like(sums)

    def norm_back(which, gain, value_of, done):
        def body(i):
            rows = rows_at(i)
            s = i // (per // TILE)
            at_scale, at_shift = 2 * which * seqs + s, (2 * which + 1) * seqs + s
            scale = table[gain : gain + 1, :] + row_of(mods, at_scale)
            normed, inverse = normalise(value_of(rows).astype(WIDE))
            grad = gn[rows, :]
            sums[pl.ds(at_scale, 1), :] += jnp.sum(grad * normed, axis=0, keepdims=True)
            sums[pl.ds(at_shift, 1), :] += jnp.sum(grad, axis=0, keepdims=True)
            hat = grad * scale
            done(rows, inverse * (hat - lane_mean(hat) - normed * lane_mean(hat * normed)))

        for_each(tokens_n // TILE, body)
        for n in range(2):
            at = (2 * which + n) * seqs
            gtab[gain + n : gain + n + 1, :] = jnp.sum(sums[at : at + seqs, :], axis=0, keepdims=True)

    mid_in.wait()

    def done2(rows, grad):
        total = pool[COT, rows, :].astype(WIDE) + grad
        mid[rows, :] = total
        pool[GRAD_BRANCH, rows, :] = total.astype(LOW)

    norm_back(1, GAIN2, lambda rows: mid[rows, :], done2)
    feed(7)
    run(9, 10)

    fetch(ctx_h, CONTEXT).wait()
    column_sums(GRAD_BRANCH, BIAS_O)
    produce(8, pool.at[CONTEXT], times(GRAD_BRANCH))
    fetch_w(4, 0).wait()
    for h in range(2):
        grad = lax.dot_general(pool[GRAD_BRANCH], half_rows(0, h), NT, preferred_element_type=WIDE)
        pool[GRAD_CONTEXT, :, half_cols(h)] = grad.astype(LOW)
    fetch_w(2, 0).start()
    load(8)
    run(10, 11)

    for src, i in ((q_h, QUERY), (k_h, KEY), (v_h, VALUE), (tokens_h, TOKENS)):
        fetch(src, i).wait()

    modulated(pool.at[TOKENS], pool.at[NORMED1], table, mods, GAIN1, 0, seqs)
    feed(8)

    lane = lax.broadcasted_iota(jnp.int32, (1, 128), 1)
    first_head = (lane < 64).astype(WIDE)
    second_head = 1.0 - first_head

    def split(v):
        return jnp.concatenate([v * first_head.astype(LOW), v * second_head.astype(LOW)], axis=0)

    def unturned(v):
        return v * cosine[...] - swapped(v) * sine[...]

    def heads(n):
        cols = pl.ds(pl.multiple_of(n * 128, 128), 128)
        for s in range(seqs):
            rows = slice(s * per, (s + 1) * per)
            keys = pool[KEY, rows, cols]
            both = split(pool[QUERY, rows, cols])
            grads = split(pool[GRAD_CONTEXT, rows, cols])
            scores = lax.dot_general(both, keys, NT, preferred_element_type=WIDE)
            grown = jnp.exp(scores - jnp.max(scores, axis=-1, keepdims=True))
            probs = grown / jnp.sum(grown, axis=-1, keepdims=True)
            grad_probs = lax.dot_general(grads, pool[VALUE, rows, cols], NT, preferred_element_type=WIDE)
            inner = jnp.sum(grad_probs * probs, axis=-1, keepdims=True)
            grad_scores = (probs * (grad_probs - inner)).astype(LOW)
            grad_v = lax.dot_general(probs.astype(LOW), grads, TN, preferred_element_type=WIDE)
            grad_k = lax.dot_general(grad_scores, both, TN, preferred_element_type=WIDE)
            grad_q = jnp.dot(grad_scores, keys, preferred_element_type=WIDE)
            grad_q = (grad_q[:per] * first_head + grad_q[per:] * second_head) * 0.125
            pool[QUERY, rows, cols] = unturned(grad_q).astype(LOW)
            pool[KEY, rows, cols] = unturned(grad_k).astype(LOW)
            pool[VALUE, rows, cols] = grad_v.astype(LOW)
        when(n < 7)(lambda: run(11 + n, 12 + n))

    for_each(8, heads)

    def project(j):
        column_sums(QUERY + j, BIAS_P + j)
        produce(9 + j, pool.at[NORMED1], times(QUERY + j))
        when(j == 1)(lambda: load(9))

        @when(j == 2)
        def _():
            feed(9)
            load(10)

    for_each(3, project)

    def project_back(j):
        slot = (1 + j) % 2
        fetch_w(1 + j, slot).wait()
        for h in range(2):
            more = lax.dot_general(pool[QUERY + j], half_rows(slot, h), NT, preferred_element_type=WIDE)

            @pl.when(j == 0)
            def _():
                gn[:, half_cols(h)] = more

            @pl.when(j > 0)
            def _():
                gn[:, half_cols(h)] = gn[:, half_cols(h)] + more

        pl.when(j == 0)(lambda: fetch_w(3, 1).start())
        when(j < 2)(lambda: feed(10 + j))
        when(j == 0)(lambda: load(11))
        run(18 + j, 19 + j)

    for_each(3, project_back)

    def done1(rows, grad):
        mid[rows, :] = mid[rows, :] + grad

    norm_back(0, GAIN1, lambda rows: pool[TOKENS, rows, :], done1)
    input_copy = pltpu.make_async_copy(mid, input_o, sem_mid)
    input_copy.start()
    if comm:
        for f in range(8):
            for row in range(13):
                r, b = vector_spot(row, f)
                parts[f, row : row + 1, :] = gtab[r : r + 1, b * 128 : (b + 1) * 128]
            parts[f, 13:16, :] = jnp.zeros((3, 128), WIDE)
        start, middle, end = sum_vectors(red.at, parts, vgot, vsums, vec_out, vsend, vrecv)
        start()
    else:
        vec_out[...] = gtab[...]

    def outer(lhs, h):
        terms = sums[:, half_cols(h)]
        high = terms.astype(LOW)
        rest = (terms - high.astype(WIDE)).astype(LOW)
        return lax.dot_general(lhs[...], high, TN, preferred_element_type=WIDE) + lax.dot_general(
            lhs[...], rest, TN, preferred_element_type=WIDE
        )

    produce(12, feat, outer)
    load(12)
    feed(12)
    if comm:
        run(21, 24)
        middle()
        run(24, 28)
        end()
        run(28, red.drains)
        red.end()
    else:
        for b in (11, 12):
            pltpu.make_async_copy(slots.at[b % 2], out.at[b], sem_slot.at[b % 2]).wait()
    input_copy.wait()


def backward_call(comm, full, cot, saved, tokens, table, mods, feat, cosine, sine, seqs):
    n, width = tokens.shape
    vmem, hbm = pl.BlockSpec(memory_space=pltpu.VMEM), pl.BlockSpec(memory_space=pl.ANY)
    q, k, v, ctx, mid, normed2, activ, slope = saved
    block = (4, 2, 2, 2, 32, width) if comm else (width, width)
    rows = width // 8
    if comm:
        shapes = [(rows, 3 * width), (rows, width), (rows, 4 * width), (4 * rows, width), (TE // 8, 2 * width), (TE // 8, 2 * width)]
    else:
        shapes = [(BLOCKS, width, width)]
    outs = [(jax.ShapeDtypeStruct(shape, LOW), hbm) for shape in shapes] + [
        (jax.ShapeDtypeStruct((16, 128) if comm else (16, width), WIDE), vmem),
        (jax.ShapeDtypeStruct((n, width), WIDE), hbm),
    ]
    extra = []
    if comm:
        part = jax.ShapeDtypeStruct((BLOCKS, 4, 2, 2, 32, width), LOW)
        outs += [(part, hbm), (part, hbm)]
        extra = [
            pltpu.VMEM((8, 16, 128), WIDE),
            pltpu.VMEM((7, 16, 128), WIDE),
            pltpu.VMEM((4, 16, 128), WIDE),
            pltpu.SemaphoreType.DMA((10,)),
            pltpu.SemaphoreType.DMA((10,)),
        ] + REDUCE_SCRATCH
        full = full.reshape((BLOCKS,) + block)
    got = pl.pallas_call(
        functools.partial(backward_kernel, comm, seqs),
        out_shape=tuple(s for s, _ in outs),
        in_specs=[hbm] * 11 + [vmem] * 5,
        out_specs=tuple(m for _, m in outs),
        scratch_shapes=[
            pltpu.VMEM((10, n, width), LOW),
            pltpu.VMEM((n, width), WIDE),
            pltpu.VMEM((n, width), WIDE),
            pltpu.VMEM((2,) + block, LOW),
            pltpu.VMEM((2,) + block, LOW),
            pltpu.VMEM((feat.shape[0], width), WIDE),
            pltpu.VMEM((16, width), WIDE),
            pltpu.SemaphoreType.DMA((10,)),
            pltpu.SemaphoreType.DMA((2,)),
            pltpu.SemaphoreType.DMA((2,)),
            pltpu.SemaphoreType.DMA,
            pltpu.SemaphoreType.DMA((2,)),
        ]
        + extra,
        compiler_params=pltpu.CompilerParams(
            collective_id=1 if comm else None, has_side_effects=comm, vmem_limit_bytes=62 * 2**20
        ),
        name="backward",
    )(full, cot, activ, slope, normed2, mid, q, k, v, ctx, tokens, table, mods, feat, cosine, sine)
    return got[: len(shapes) + 2]


def rotary_constants(length, head_dim):
    half_width = head_dim // 2
    inverse = np.exp(np.arange(half_width, dtype=np.float32) * np.float32(-math.log(10000.0) / half_width))
    angles = np.arange(length, dtype=np.float32)[:, None] * inverse[None, :]
    cosine, sine = np.cos(angles), np.sin(angles)
    pair = np.concatenate([cosine, cosine], axis=1), np.concatenate([-sine, sine], axis=1)
    return tuple(np.concatenate([t, t], axis=1).astype(np.float32) for t in pair)


def wide_features(noise_times, width):
    seqs = noise_times.shape[0]
    half_width = TE // 2
    column = np.arange(width)
    feature = column // 128 * 32 + column % 32
    rates = np.exp((feature % half_width).astype(np.float32) * np.float32(math.log(100.0) / half_width))
    row = np.arange(-(-4 * seqs // 32) * 32)
    times = jnp.ones(row.shape, WIDE)
    for s in range(seqs):
        times = jnp.where(row % seqs == s, noise_times[s], times)
    phases = (jnp.log(times) * 0.25)[:, None] * rates[None, :]
    feat = jnp.where((feature < half_width)[None, :], jnp.sin(phases), jnp.cos(phases))
    return jnp.where((column // 32 % 4)[None, :] == (row // seqs)[:, None], feat, 0.0).astype(LOW)


def gather_plain(weights, vectors):
    project, output, up, down, time1, time2 = weights
    rows, width = output.shape
    each = time1.shape[0]
    columns = lambda w: w.reshape(rows, -1, width).transpose(1, 0, 2)
    times = jnp.stack([time1, time2]).reshape(2, each, 2, width).transpose(0, 2, 1, 3)
    own = jnp.concatenate(
        [times.reshape(1, rows, width), columns(project), output[None], columns(up), down.reshape(4, rows, width)]
    )
    full = lax.all_gather(own, "fsdp", axis=1, tiled=True)
    times = full[0].reshape(-1, 2, 2, each, width).transpose(1, 2, 0, 3, 4).reshape(2, 2, 8, 32, width)
    down = full[9:].reshape(4, -1, rows, width).transpose(1, 0, 2, 3).reshape(8, 4, 128, width)
    full = jnp.concatenate(
        [
            times.transpose(2, 0, 1, 3, 4).reshape(1, width, width),
            full[1:9],
            down.transpose(1, 0, 2, 3).reshape(4, width, width),
        ]
    )
    sizes = [v.shape[0] for v in vectors]
    whole = pieces_of(lax.all_gather(jnp.concatenate(vectors), "fsdp", axis=0), sizes)
    table = jnp.concatenate([w.reshape(-1, width) for w in whole]).astype(WIDE)
    return full, jnp.pad(table, ((0, 3), (0, 0)))


def reduce_plain(parts, table, sizes, shards_of):
    width = parts.shape[-1]
    rows, each = width // shards_of, TE // shards_of
    down = parts[:4].reshape(4, 8, 128, width).transpose(1, 0, 2, 3).reshape(shards_of, 4, rows, width)
    times = parts[12].reshape(8, 2, 2, 32, width).transpose(1, 2, 0, 3, 4).reshape(2, 2, shards_of, each, width)
    own = jnp.concatenate(
        [
            down.transpose(1, 0, 2, 3).reshape(4, width, width),
            parts[4:12],
            times.transpose(2, 0, 1, 3, 4).reshape(1, width, width),
        ]
    )
    mine = lax.psum(lax.psum_scatter(own, "fsdp", scatter_dimension=1, tiled=True), "rep")
    whole = pieces_of(table[:13].reshape(-1), [shards_of * size for size in sizes])
    vec = jnp.concatenate([w.reshape(shards_of, -1) for w in whole], axis=1)
    vec = lax.psum(lax.psum_scatter(vec, "fsdp", scatter_dimension=0, tiled=True)[0], "rep")
    columns = lambda w: w.transpose(1, 0, 2).reshape(rows, -1)
    times = mine[12].reshape(2, 2, each, width).transpose(0, 2, 1, 3).reshape(2, each, 2 * width)
    return columns(mine[9:12]), mine[8], columns(mine[4:8]), mine[:4].reshape(-1, width), times[0], times[1], vec


def pieces_of(flat, sizes):
    at, got = 0, []
    for size in sizes:
        got.append(flat[..., at : at + size])
        at += size
    return got


def shards(
    inputs,
    noise_times,
    cotangent,
    norm1_gain,
    norm1_bias,
    norm1_time,
    project_weight,
    project_bias,
    output_weight,
    output_bias,
    norm2_gain,
    norm2_bias,
    norm2_time,
    up_weight,
    up_bias,
    down_weight,
    down_bias,
):
    seqs = noise_times.shape[0]
    tokens_n, width = inputs.shape
    rows = output_weight.shape[0]
    shards_of = width // rows
    comm = shards_of == 8
    feat = wide_features(noise_times, width)
    cosine, sine = rotary_constants(tokens_n // seqs, width // HEADS)
    weights = (project_weight, output_weight, up_weight, down_weight, norm1_time, norm2_time)
    vectors = (norm1_gain, norm1_bias, project_bias, output_bias, norm2_gain, norm2_bias, up_bias, down_bias)
    sizes = [v.shape[0] for v in vectors]
    if comm:
        at, table = 0, jnp.zeros((16, 128), WIDE)
        for v in vectors:
            lines = v.astype(WIDE).reshape(-1, 128)
            table = table + jnp.pad(lines, ((at, 16 - at - lines.shape[0]), (0, 0)))
            at += lines.shape[0]
    else:
        full, table = gather_plain(weights, vectors)
        weights = (full,)
    full, table, mods, layer_out, *saved = forward_call(comm, weights, table, inputs, feat, cosine, sine, seqs)
    *sums, input_grad = backward_call(comm, full, cotangent, saved, inputs, table, mods, feat, cosine, sine, seqs)
    if not comm:
        sums = reduce_plain(*sums, sizes, shards_of)
    project, output, up, down, time1, time2 = [s.astype(WIDE) for s in sums[:6]]
    got = pieces_of(sums[6].reshape(-1), sizes)
    return (
        layer_out,
        input_grad,
        got[0],
        got[1],
        time1,
        project,
        got[2],
        output,
        got[3],
        got[4],
        got[5],
        time2,
        up,
        got[6],
        down,
        got[7],
    )


def solution(mesh):
    placed = (
        P(("rep", "fsdp"), None),
        P(("rep", "fsdp")),
        P(("rep", "fsdp"), None),
        P("fsdp"),
        P("fsdp"),
        P("fsdp", None),
        P("fsdp", None),
        P("fsdp"),
        P("fsdp", None),
        P("fsdp"),
        P("fsdp"),
        P("fsdp"),
        P("fsdp", None),
        P("fsdp", None),
        P("fsdp"),
        P("fsdp", None),
        P("fsdp"),
    )
    return jax.shard_map(
        shards,
        mesh=mesh,
        in_specs=placed,
        out_specs=(
            P(("rep", "fsdp"), None),
            P(("rep", "fsdp"), None),
            P("fsdp"),
            P("fsdp"),
            P("fsdp", None),
            P("fsdp", None),
            P("fsdp"),
            P("fsdp", None),
            P("fsdp"),
            P("fsdp"),
            P("fsdp"),
            P("fsdp", None),
            P("fsdp", None),
            P("fsdp"),
            P("fsdp", None),
            P("fsdp"),
        ),
        check_vma=False,
    )
```

```python
import functools
import math

import jax
import jax.numpy as jnp
import numpy as np
from jax import lax
from jax.experimental import pallas as pl
from jax.experimental.pallas import tpu as pltpu
from jax.sharding import PartitionSpec as P

HEADS = 16
TE = 256
epsilon = 1e-05


MESH = pl.DeviceIdType.MESH
LOW, WIDE = jnp.bfloat16, jnp.float32
FRONT = 384
BLOCKS = 13
PIECES = 2 * BLOCKS
NT = (((1,), (1,)), ((), ()))
TN = (((0,), (0,)), ((), ()))


class Place:
    def __init__(self):
        r, f = lax.axis_index("rep"), lax.axis_index("fsdp")
        self.r, self.f = r, f
        self.x, self.core = r // 2, r % 2
        self.z, self.y = f // 2, f % 2
        z = self.z
        self.zs = [z, z + 1 - 2 * (z % 2), (z + 2) % 4, 3 - z]
        self.same = [zk * 2 + self.y for zk in self.zs]
        self.other = [zk * 2 + 1 - self.y for zk in self.zs]
        self.across_x = ((1 - self.x) * 2 + self.core, f)
        self.across_y = (r, self.other[0])
        self.across_core = (self.x * 2 + 1 - self.core, f)
        self.diagonal = ((1 - self.x) * 2 + 1 - self.core, f)
        self.along_z = [(r, fk) for fk in self.same]
        self.shards = self.same[1:] + self.other
        self.group = [(r, fk) for fk in self.shards]


def greet(peers):
    barrier = pltpu.get_barrier_semaphore()
    for peer in peers:
        pl.semaphore_signal(barrier, inc=1, device_id=peer, device_id_type=MESH)
    pl.semaphore_wait(barrier, len(peers))


def remote(src, dst, send, recv, peer):
    return pltpu.make_async_remote_copy(
        src_ref=src, dst_ref=dst, send_sem=send, recv_sem=recv, device_id=peer, device_id_type=MESH
    )


class Gather:
    def __init__(self, own, vec, full, vecs, send, recv, vsend, vrecv, lsem):
        self.at = Place()
        self.own, self.full, self.send, self.recv, self.lsem = own, full, send, recv, lsem
        self.vec, self.vecs, self.vsend, self.vrecv = vec, vecs, vsend, vrecv
        x = self.at.x
        self.middle = jnp.logical_and(self.at.z >= 1, self.at.z <= 2)
        rest = 1024 - FRONT
        self.mine = pl.ds(pl.multiple_of(x * FRONT, 128), rest)
        self.xcols = pl.ds(pl.multiple_of(x * rest, 128), FRONT)
        self.xland = pl.ds(pl.multiple_of((1 - x) * rest, 128), FRONT)

    def spot(self, c, z, y, cols, core=None):
        core = self.at.core if core is None else core
        return self.full.at[c // 2, z, y, core, c % 2, :, cols]

    def pair(self, c, i, src, dst, peer):
        return remote(src, dst, self.send.at[c, i], self.recv.at[c, i], peer)

    def owned(self, c, cols):
        return self.own.at[c // 2, pl.ds(pl.multiple_of(self.at.core * 64 + c % 2 * 32, 32), 32), cols]

    def z_copy(self, c, k):
        at = self.at
        src = self.owned(c, self.mine)
        return self.pair(c, k - 1, src, self.spot(c, at.z, at.y, self.mine), at.along_z[k])

    def z_relay(self, c):
        dst = self.spot(c, self.at.zs[2], self.at.y, self.mine)
        return remote(dst, dst, self.send.at[c, 12], self.recv.at[c, 2], self.at.along_z[1])

    def z_land(self, c, k):
        dst = self.spot(c, self.at.zs[k], self.at.y, self.mine)
        return self.pair(c, k - 1, dst, dst, self.at.along_z[k])

    def y_copy(self, c, k):
        at = self.at
        dst = self.spot(c, at.zs[k], at.y, self.mine)
        src = self.owned(c, self.mine) if k == 0 else dst
        return self.pair(c, 3 + k, src, dst, at.across_y)

    def y_land(self, c, k):
        dst = self.spot(c, self.at.zs[k], 1 - self.at.y, self.mine)
        return self.pair(c, 3 + k, dst, dst, self.at.across_y)

    def x_place(self, c, k, cols):
        at = self.at
        if k < 3:
            return self.spot(c, at.zs[k + 1], at.y, cols)
        return self.spot(c, slice(None), 1 - at.y, cols)

    def x_copy(self, c, k):
        src = self.x_place(c, k, self.xcols)
        return self.pair(c, 7 + k, src, src, self.at.across_x)

    def x_land(self, c, k):
        dst = self.x_place(c, k, self.xland)
        return self.pair(c, 7 + k, dst, dst, self.at.across_x)

    def core_copy(self, c, core=None):
        part = self.spot(c, slice(None), slice(None), slice(None), core)
        return self.pair(c, 11, part, part, self.at.across_core)

    def local(self, c):
        at = self.at
        dst = self.spot(c, at.z, at.y, slice(None))
        return pltpu.make_async_copy(self.owned(c, slice(None)), dst, self.lsem.at[c])

    def first(self, c):
        for k in range(1, 3):
            self.z_copy(c, k).start()
        pl.when(self.middle)(lambda: self.z_copy(c, 3).start())
        self.y_copy(c, 0).start()
        self.local(c).start()

    ahead = 4

    def begin(self):
        at = self.at
        greet([at.across_core, at.across_x] + at.group)
        for i, peer in enumerate(at.group):
            remote(self.vec, self.vecs.at[at.f], self.vsend.at[i], self.vrecv.at[i], peer).start()

    def start(self):
        for c in range(self.ahead):
            self.first(c)

    def vectors(self):
        at = self.at
        self.vecs[at.f] = self.vec[...]
        for i, peer in enumerate(at.group):
            remote(self.vec, self.vecs.at[at.shards[i]], self.vsend.at[i], self.vrecv.at[i], peer).wait()

    lag_x, lag_core, lag_done = 3, 6, 7

    def step(self, t):
        lag_x, lag_core, lag_done = self.lag_x, self.lag_core, self.lag_done

        @pl.when(t + self.ahead < PIECES)
        def _():
            self.first(t + self.ahead)

        @pl.when(t < PIECES)
        def _():
            for k in (2, 1, 3):
                self.z_land(t, k).wait_recv()
                if k == 2:
                    pl.when(self.middle)(lambda: self.z_relay(t).start())
                self.y_copy(t, k).start()

        @pl.when(jnp.logical_and(t >= lag_x, t < PIECES + lag_x))
        def _():
            c = t - lag_x
            for k in range(4):
                if k == 3:
                    for j in range(4):
                        self.y_land(c, j).wait_recv()
                self.x_copy(c, k).start()

        @pl.when(jnp.logical_and(t >= lag_core, t < PIECES + lag_core))
        def _():
            c = t - lag_core
            self.local(c).wait()
            for k in range(4):
                self.x_land(c, k).wait_recv()
            self.core_copy(c).start()

        @pl.when(jnp.logical_and(t >= lag_done, t < PIECES + lag_done))
        def _():
            c = t - lag_done
            self.core_copy(c, 1 - self.at.core).wait_recv()
            for k in range(1, 3):
                self.z_copy(c, k).wait_send()

            @pl.when(self.middle)
            def _():
                self.z_copy(c, 3).wait_send()
                self.z_relay(c).wait_send()

            for k in range(4):
                self.y_copy(c, k).wait_send()
                self.x_copy(c, k).wait_send()
            self.core_copy(c).wait_send()

    steps = PIECES + lag_done

    def ready(self, block):
        return 2 * block + 2 + self.lag_done

    def run(self, lo, hi):
        def one(t, carry):
            self.step(t)
            return carry

        lax.fori_loop(lo, hi, one, 0)


GATHER_SCRATCH = [
    pltpu.VMEM((8, 16, 128), WIDE),
    pltpu.SemaphoreType.DMA((PIECES, 13)),
    pltpu.SemaphoreType.DMA((PIECES, 12)),
    pltpu.SemaphoreType.DMA((7,)),
    pltpu.SemaphoreType.DMA((7,)),
    pltpu.SemaphoreType.DMA((PIECES,)),
]


GAIN1, BIAS1, BIAS_P, BIAS_O, GAIN2, BIAS2, BIAS_U, BIAS_D = 0, 1, 2, 5, 6, 7, 8, 12
HALF = 512
TILE = 32


def vector_spot(row, f):
    for first, count in ((BIAS_P, 3), (BIAS_U, 4)):
        if first <= row < first + count:
            block = f * count + row - first
            return first + block // 8, block % 8
    return row, f


def for_each(count, body):
    def one(i, carry):
        body(i)
        return carry

    lax.fori_loop(0, count, one, 0)


def rows_at(i, size=TILE):
    return pl.ds(pl.multiple_of(i * size, size), size)


def lane_mean(v):
    return jnp.mean(v, axis=-1, keepdims=True)


def normalise(v):
    centred = v - lane_mean(v)
    inverse = lax.rsqrt(lane_mean(centred * centred) + epsilon)
    return centred * inverse, inverse


def row_of(ref, i):
    return ref[pl.ds(i, 1), :]


def modulated(ref, out, table, mods, gain, which, seqs):
    per = ref.shape[0] // seqs // TILE

    def body(i):
        s = i // per
        scale = table[gain : gain + 1, :] + row_of(mods, 2 * which * seqs + s)
        shift = table[gain + 1 : gain + 2, :] + row_of(mods, (2 * which + 1) * seqs + s)
        rows = rows_at(i)
        normed, _ = normalise(ref[rows, :].astype(WIDE))
        out[rows, :] = (normed * scale + shift).astype(LOW)

    for_each(ref.shape[0] // TILE, body)


def swapped(v):
    lane = lax.broadcasted_iota(jnp.int32, v.shape, 1)
    return jnp.where(lane % 64 < 32, pltpu.roll(v, 96, 1), pltpu.roll(v, 32, 1))


def pack(local, own, sems):
    project, output, up, down, time1, time2 = local
    pairs = [(t.at[:, pl.ds(1024 * h, 1024)], own.at[0, pl.ds(64 * n + 32 * h, 32)]) for n, t in enumerate((time1, time2)) for h in range(2)]
    pairs += [(project.at[:, pl.ds(1024 * j, 1024)], own.at[1 + j]) for j in range(3)] + [(output, own.at[4])]
    pairs += [(up.at[:, pl.ds(1024 * j, 1024)], own.at[5 + j]) for j in range(4)]
    pairs += [(down.at[pl.ds(128 * j, 128)], own.at[9 + j]) for j in range(4)]
    return [pltpu.make_async_copy(src, dst, sems.at[i]) for i, (src, dst) in enumerate(pairs)]


def forward_kernel(comm, seqs, *refs):
    refs = list(refs)
    take = lambda n: [refs.pop(0) for _ in range(n)]
    if comm:
        local, vec = take(6), take(1)[0]
    else:
        full_in, table_in = take(2)
    tokens_hbm, cot_hbm, feat, cosine, sine = take(5)
    if comm:
        (full,) = take(1)
    else:
        full = full_in
    table, mods = take(2)
    out_o, grad_o, q_o, k_o, v_o, ctx_o, mid_o, normed1_o, normed2_o, slope_o, probs_o = take(11)
    tokens, cot, weights, normed, normed2, q, k, v, ctx, mid, acc, activ, slope, wide, out_low, probs, grads = take(17)
    sem_in, sem_w, sem_out, sem_grad = take(4)
    tokens_n = tokens.shape[0]
    per = tokens_n // seqs

    tokens_in = pltpu.make_async_copy(tokens_hbm, tokens, sem_in.at[0])
    tokens_in.start()
    cot_in = pltpu.make_async_copy(cot_hbm, cot, sem_in.at[1])
    cot_in.start()
    if comm:
        own, sem_own = take(2)
        gather = Gather(own, vec, full, *refs)
        packing = pack(local, own, sem_own)
        for copy in packing:
            copy.start()
        gather.begin()
        for copy in packing:
            copy.wait()
        gather.start()
        gather.vectors()
        for f in range(8):
            block = gather.vecs[f]
            for row in range(13):
                r, b = vector_spot(row, f)
                table[r : r + 1, b * 128 : (b + 1) * 128] = block[row : row + 1, :]
        run = gather.run
    else:
        table[...] = table_in[...]
        run = lambda lo, hi: None

    def fetch(c):
        return pltpu.make_async_copy(full.at[c], weights.at[c % 2], sem_w.at[c % 2])

    def arrive(c, lo, hi):
        run(lo, hi)
        fetch(c).start()

    def weight(c):
        fetch(c).wait()
        return weights.at[c % 2]

    ready = Gather.lag_done + 2
    flat = (lambda w: w[...].reshape(1024, 1024)) if comm else (lambda w: w[...])

    saves = []

    def save(src, dst):
        copy = pltpu.make_async_copy(src, dst, sem_out.at[len(saves)])
        copy.start()
        saves.append(copy)

    arrive(0, 0, ready)
    w = weight(0)
    mods[...] = jnp.dot(feat[...], flat(w), preferred_element_type=WIDE)
    tokens_in.wait()
    arrive(1, ready, ready + 2)
    modulated(tokens, normed, table, mods, GAIN1, 0, seqs)
    save(normed, normed1_o)

    for j, (dst, dst_o) in enumerate([(q, q_o), (k, k_o), (v, v_o)]):
        w = weight(1 + j)
        for h in range(2):
            cols = slice(h * HALF, (h + 1) * HALF)
            wide[...] = jnp.dot(normed[...], half_of(w, cols, comm), preferred_element_type=WIDE)
            run(ready + 2 + 2 * j + h, ready + 3 + 2 * j + h)
            if h == 1:
                fetch(2 + j).start()
            bias = table[BIAS_P + j : BIAS_P + j + 1, cols]

            def body(i, h=h, bias=bias, dst=dst, j=j):
                rows = rows_at(i)
                where = pl.ds(pl.multiple_of((i % (per // TILE)) * TILE, TILE), TILE)
                piece = wide[rows, :] + bias
                if j == 2:
                    dst[rows, h * HALF : (h + 1) * HALF] = piece.astype(LOW)
                    return
                for n in range(HALF // 128):
                    part = piece[:, n * 128 : (n + 1) * 128]
                    turned = part * cosine[where, :] + swapped(part) * sine[where, :]
                    if j == 0:
                        turned = turned * 0.125
                    at = h * HALF + n * 128
                    dst[rows, at : at + 128] = turned.astype(LOW)

            for_each(tokens_n // TILE, body)
        save(dst, dst_o)

    lane = lax.broadcasted_iota(jnp.int32, (1, 128), 1)
    first_head = (lane < 64).astype(WIDE)
    second_head = 1.0 - first_head

    def heads(n):
        cols = pl.ds(pl.multiple_of(n * 128, 128), 128)
        for s in range(seqs):
            rows = slice(s * per, (s + 1) * per)
            qs = q[rows, cols]
            both = jnp.concatenate([qs * first_head.astype(LOW), qs * second_head.astype(LOW)], axis=0)
            scores = lax.dot_general(both, k[rows, cols], NT, preferred_element_type=WIDE)
            grown = jnp.exp(scores - jnp.max(scores, axis=-1, keepdims=True))
            share = (grown / jnp.sum(grown, axis=-1, keepdims=True)).astype(LOW)
            probs[n, 2 * s * per : 2 * (s + 1) * per, :] = share
            mixed = jnp.dot(share, v[rows, cols], preferred_element_type=WIDE)
            ctx[rows, cols] = (mixed[:per] * first_head + mixed[per:] * second_head).astype(LOW)
        if comm:
            pl.when(n >= 2)(lambda: gather.step(ready + 6 + n))

    for_each(8, heads)
    save(ctx, ctx_o)
    save(probs, probs_o)

    w = weight(4)
    for h in range(2):
        cols = slice(h * HALF, (h + 1) * HALF)
        dot = jnp.dot(ctx[...], half_of(w, cols, comm), preferred_element_type=WIDE)
        mid[:, cols] = tokens[:, cols].astype(WIDE) + (dot + table[BIAS_O : BIAS_O + 1, cols])
    arrive(5, ready + 14, ready + 15)
    save(mid, mid_o)
    modulated(mid, normed2, table, mods, GAIN2, 1, seqs)
    save(normed2, normed2_o)

    def up(j):
        w = weight(5 + j)
        for h in range(2):
            cols = slice(h * HALF, (h + 1) * HALF)
            wide[...] = jnp.dot(normed2[...], half_of(w, cols, comm), preferred_element_type=WIDE)
            if h == 0:
                once = ready + 15 + 2 * j - jnp.maximum(j - 2, 0)
                run(once, once + 1)
            else:
                run(ready + 16 + 2 * j, ready + 16 + 2 * j + (j < 2).astype(jnp.int32))
                fetch(6 + j).start()

            def body(i, h=h, cols=cols):
                rows = rows_at(i)
                u = wide[rows, :] + table[pl.ds(BIAS_U + j, 1), cols]
                phi = 0.5 + 0.5 * lax.erf(u * (0.5**0.5))
                bell = jnp.exp(-0.5 * (u * u)) * (1.0 / math.sqrt(2.0 * math.pi))
                result, grow = (u * phi).astype(LOW), (phi + u * bell).astype(LOW)
                place = pl.ds(pl.multiple_of((2 * j + h) * 128, 128), 128)
                for n in range(4):
                    activ[n, rows, place] = result[:, n * 128 : (n + 1) * 128]
                    slope[n, rows, place] = grow[:, n * 128 : (n + 1) * 128]

            for_each(tokens_n // TILE, body)

    for_each(4, up)
    save(slope, slope_o)

    cot_in.wait()

    def grad_copy(j):
        return pltpu.make_async_copy(grads.at[j % 2], grad_o.at[j], sem_grad.at[j % 2])

    def down(j):
        pl.when(j >= 2)(lambda: grad_copy(j - 2).wait())
        for h in range(2):
            cols = slice(h * HALF, (h + 1) * HALF)
            block = lax.dot_general(activ[j], cot[:, cols], TN, preferred_element_type=WIDE).astype(LOW)
            if comm:
                grads[j % 2, :, :, :, :, :, cols] = block.reshape(4, 2, 2, 2, 32, HALF)
            else:
                grads[j % 2, :, cols] = block
        grad_copy(j).start()
        w = weight(9 + j)
        for h in range(2):
            cols = slice(h * HALF, (h + 1) * HALF)
            dot = jnp.dot(activ[j], half_of(w, cols, comm), preferred_element_type=WIDE)

            @pl.when(j == 0)
            def _():
                acc[:, cols] = mid[:, cols] + table[BIAS_D : BIAS_D + 1, cols] + dot

            @pl.when(j > 0)
            def _():
                acc[:, cols] = acc[:, cols] + dot

            if h == 0:
                pl.when(j < 3)(lambda: arrive(10 + j, ready + 21 + j, ready + 22 + j))

    for_each(4, down)
    out_low[...] = acc[...].astype(LOW)
    save(out_low, out_o)
    grad_copy(2).wait()
    grad_copy(3).wait()
    for copy in saves:
        copy.wait()


def half_of(w, cols, comm):
    if comm:
        return w[..., cols].reshape(1024, HALF)
    return w[:, cols]


def forward_call(comm, weights, vectors, tokens, cot, feat, cosine, sine, seqs):
    n, width = tokens.shape
    vmem, hbm = pl.BlockSpec(memory_space=pltpu.VMEM), pl.BlockSpec(memory_space=pl.ANY)
    low = jax.ShapeDtypeStruct((n, width), LOW)
    wide = jax.ShapeDtypeStruct((n, width), WIDE)
    shape4 = jax.ShapeDtypeStruct((4, n, width), LOW)
    block = (4, 2, 2, 2, 32, width) if comm else (width, width)
    outs = [
        (jax.ShapeDtypeStruct((16, width), WIDE), vmem),
        (jax.ShapeDtypeStruct((feat.shape[0], width), WIDE), vmem),
    ]
    share = (8, 2 * n, 128)
    saved = (jax.ShapeDtypeStruct((4,) + block, LOW), low, low, low, low, wide, low, low, shape4)
    outs += [(s, hbm) for s in (low,) + saved + (jax.ShapeDtypeStruct(share, LOW),)]
    extra = []
    if comm:
        outs = [(jax.ShapeDtypeStruct((BLOCKS,) + block, LOW), hbm)] + outs
        extra = [pltpu.VMEM((BLOCKS, 128, width), LOW), pltpu.SemaphoreType.DMA((16,))] + GATHER_SCRATCH
    buffer = pltpu.VMEM((n, width), LOW)
    got = pl.pallas_call(
        functools.partial(forward_kernel, comm, seqs),
        out_shape=tuple(s for s, _ in outs),
        in_specs=[hbm] * len(weights) + [vmem, hbm, hbm, vmem, vmem, vmem],
        out_specs=tuple(m for _, m in outs),
        scratch_shapes=[
            buffer,
            buffer,
            pltpu.VMEM((2,) + block, LOW),
            buffer,
            buffer,
            buffer,
            buffer,
            buffer,
            buffer,
            pltpu.VMEM((n, width), WIDE),
            pltpu.VMEM((n, width), WIDE),
            pltpu.VMEM((4, n, width), LOW),
            pltpu.VMEM((4, n, width), LOW),
            pltpu.VMEM((n, HALF), WIDE),
            buffer,
            pltpu.VMEM(share, LOW),
            pltpu.VMEM((2,) + block, LOW),
            pltpu.SemaphoreType.DMA((2,)),
            pltpu.SemaphoreType.DMA((2,)),
            pltpu.SemaphoreType.DMA((10,)),
            pltpu.SemaphoreType.DMA((2,)),
        ]
        + extra,
        compiler_params=pltpu.CompilerParams(
            collective_id=0 if comm else None, has_side_effects=comm, vmem_limit_bytes=60 * 2**20
        ),
        name="forward",
    )(*weights, vectors, tokens, cot, feat, cosine, sine)
    if not comm:
        return (weights[0], vectors) + tuple(got[1:])
    return (got[0].reshape(BLOCKS, width, width),) + tuple(got[1:])


RING = 10
READY = 4


class Reduce:
    def __init__(self, ready, slots, own, l0, outs, *scratch):
        self.at = Place()
        self.ready, self.slots, self.own, self.l0, self.outs = ready, slots, own, l0, outs
        (self.held, self.s0, self.l1a, self.l1b, self.l2, self.l3, self.la) = scratch[:7]
        (self.bsend, self.brecv, self.lsem, self.send, self.recv, self.osem) = scratch[7:13]
        x = self.at.x
        self.front, self.back = pl.ds(0, FRONT), pl.ds(FRONT, 1024 - FRONT)
        self.mine = pl.ds(pl.multiple_of(x * 16, 16), 16)
        self.theirs = pl.ds(pl.multiple_of((1 - x) * 16, 16), 16)

    def begin(self):
        at = self.at
        greet([at.across_core, at.across_x, at.diagonal] + at.group)
        for b in range(READY):
            src = self.ready.at[b, :, :, 1 - at.core]
            remote(src, self.l0.at[b], self.bsend.at[b], self.brecv.at[b], at.across_core).start()

    def core_copy(self, b):
        src = self.slots.at[b % 2, :, :, 1 - self.at.core]
        return remote(src, self.l0.at[b], self.bsend.at[b], self.brecv.at[b], self.at.across_core)

    def own_copy(self, b):
        return pltpu.make_async_copy(self.slots.at[b % 2, :, :, self.at.core], self.own.at[b - READY], self.lsem.at[b % 2])

    def loads(self, b, ready=False):
        src = self.ready.at[b, :, :, self.at.core] if ready else self.own.at[b - READY]
        return (
            pltpu.make_async_copy(src, self.held.at[0], self.lsem.at[2]),
            pltpu.make_async_copy(self.l0.at[b], self.held.at[1], self.lsem.at[3]),
        )

    def free(self, b):
        self.core_copy(b - 2).wait_send()

    def produced(self, b):
        self.core_copy(b).start()
        self.own_copy(b).start()

    def load(self, b):
        self.core_copy(b).wait_recv()
        if isinstance(b, int) and b < READY:
            for copy in self.loads(b, True):
                copy.start()
            return
        self.own_copy(b).wait()
        for copy in self.loads(b):
            copy.start()

    def feed(self, b):
        for copy in self.loads(READY):
            copy.wait()

        def add(z):
            for h in range(2):
                self.s0[(2 * b + h) % RING, z] = self.held[0, z, :, h] + self.held[1, z, :, h]

        for_each(4, add)
        for h in range(2):
            self.x_one(2 * b + h).start()
            self.y_one(2 * b + h).start()

    def pair(self, p, i, src, dst, peer):
        return remote(src, dst, self.send.at[p, i], self.recv.at[p, i], peer)

    def x_one(self, p):
        src = self.s0.at[p % RING, :, :, self.theirs, self.front]
        return self.pair(p, 0, src, self.l1a.at[p], self.at.across_x)

    def y_one(self, p):
        src = self.s0.at[p % RING, :, 1 - self.at.y, :, self.back]
        return self.pair(p, 1, src, self.l1b.at[p], self.at.across_y)

    def y_two(self, p):
        return self.pair(p, 2, self.l1a.at[p, :, 1 - self.at.y], self.l2.at[p, :, :, self.front], self.at.across_y)

    def x_two(self, p):
        return self.pair(p, 3, self.l1b.at[p, :, self.theirs], self.l2.at[p, :, :, self.back], self.at.across_x)

    def z_copy(self, p, k):
        return self.pair(p, 3 + k, self.l2.at[p, self.at.zs[k]], self.l3.at[p, k - 1], self.at.along_z[k])

    def x_back(self, p, x=None):
        piece = self.la.at[p, self.at.core, pl.ds(pl.multiple_of((self.at.x if x is None else x) * 16, 16), 16)]
        return self.pair(p, 7, piece, piece, self.at.across_x)

    def core_back(self, p, core=None):
        piece = self.la.at[p, self.at.core if core is None else core]
        return self.pair(p, 8, piece, piece, self.at.across_core)

    def store(self, p, dsts):
        for core, dst in enumerate(dsts):
            pltpu.make_async_copy(self.la.at[p, core], dst, self.osem.at[p, core]).start()

    def store_all(self, p):
        project, output, up, down, *times = self.outs
        b, h = p // 2, p % 2

        def rows(core, first=0):
            return pl.ds(pl.multiple_of(first + core * 64 + h * 32, 32), 32)

        def cols(j):
            return pl.ds(pl.multiple_of(j * 1024, 1024), 1024)

        pl.when(b < 4)(lambda: self.store(p, [down.at[rows(c, b * 128)] for c in range(2)]))
        pl.when(jnp.logical_and(b >= 4, b < 8))(lambda: self.store(p, [up.at[rows(c), cols(b - 4)] for c in range(2)]))
        pl.when(b == 8)(lambda: self.store(p, [output.at[rows(c)] for c in range(2)]))
        pl.when(jnp.logical_and(b >= 9, b < 12))(lambda: self.store(p, [project.at[rows(c), cols(b - 9)] for c in range(2)]))
        pl.when(b == 12)(lambda: self.store(p, [t.at[:, cols(h)] for t in times]))

    lags = (4, 6, 10, 11)

    def drain(self, d):
        at, lags = self.at, self.lags

        @pl.when(d < PIECES)
        def _():
            p = d
            self.x_one(p).wait()

            self.l1a[p] = self.l1a[p] + self.s0[p % RING, :, :, self.mine, self.front]
            self.y_two(p).start()
            self.y_one(p).wait()
            self.l1b[p] = self.l1b[p] + self.s0[p % RING, :, at.y, :, self.back]
            self.x_two(p).start()

        @pl.when(jnp.logical_and(d >= lags[0], d < PIECES + lags[0]))
        def _():
            p = d - lags[0]
            self.y_two(p).wait()
            self.x_two(p).wait()

            self.l2[p, :, :, self.front] = self.l2[p, :, :, self.front] + self.l1a[p, :, at.y]
            self.l2[p, :, :, self.back] = self.l2[p, :, :, self.back] + self.l1b[p, :, self.mine]
            for k in range(1, 4):
                self.z_copy(p, k).start()

        @pl.when(jnp.logical_and(d >= lags[1], d < PIECES + lags[1]))
        def _():
            p = d - lags[1]
            total = self.l2[p, at.z].astype(WIDE)
            for k in range(1, 4):
                self.z_copy(p, k).wait()
            for k in range(3):
                total = total + self.l3[p, k].astype(WIDE)
            self.la[p, at.core, self.mine] = total.astype(LOW)
            self.x_back(p).start()

        @pl.when(jnp.logical_and(d >= lags[2], d < PIECES + lags[2]))
        def _():
            p = d - lags[2]
            self.x_back(p, 1 - at.x).wait_recv()
            self.core_back(p).start()

        @pl.when(jnp.logical_and(d >= lags[3], d < PIECES + lags[3]))
        def _():
            p = d - lags[3]
            self.x_back(p).wait_send()
            self.core_back(p).wait_send()
            self.core_back(p, 1 - at.core).wait_recv()
            self.store_all(p)

    drains = PIECES + lags[3]

    def run(self, lo, hi):
        def one(d, carry):
            self.drain(d)
            return carry

        lax.fori_loop(lo, hi, one, 0)

    def end(self):
        for b in range(READY - 2):
            self.core_copy(b).wait_send()
        self.core_copy(BLOCKS - 2).wait_send()
        self.core_copy(BLOCKS - 1).wait_send()

        def stored(p):
            for core in range(2):
                pltpu.make_async_copy(self.la.at[p, core], self.outs[1].at[pl.ds(0, 32)], self.osem.at[p, core]).wait()

        for_each(PIECES, stored)


REDUCE_SCRATCH = [
    pltpu.VMEM((2, 4, 2, 2, 32, 1024), LOW),
    pltpu.VMEM((RING, 4, 2, 32, 1024), LOW),
    pltpu.VMEM((PIECES, 4, 2, 16, FRONT), LOW),
    pltpu.VMEM((PIECES, 4, 32, 1024 - FRONT), LOW),
    pltpu.VMEM((PIECES, 4, 16, 1024), LOW),
    pltpu.VMEM((PIECES, 3, 16, 1024), LOW),
    pltpu.VMEM((PIECES, 2, 32, 1024), LOW),
    pltpu.SemaphoreType.DMA((BLOCKS,)),
    pltpu.SemaphoreType.DMA((BLOCKS,)),
    pltpu.SemaphoreType.DMA((4,)),
    pltpu.SemaphoreType.DMA((PIECES, 9)),
    pltpu.SemaphoreType.DMA((PIECES, 9)),
    pltpu.SemaphoreType.DMA((PIECES, 2)),
]


def sum_vectors(at, parts, got, sums, out, send, recv):
    def part(i):
        return remote(parts.at[at.shards[i]], got.at[i], send.at[i], recv.at[i], at.group[i])

    reps = [at.across_x, at.across_core, at.diagonal]

    def rest(i):
        return remote(sums.at[3], sums.at[i], send.at[7 + i], recv.at[7 + i], reps[i])

    def start():
        for i in range(7):
            part(i).start()

    def middle():
        total = parts[at.f]
        for i in range(7):
            part(i).wait()
            total = total + got[i]
        sums[3] = total
        for i in range(3):
            rest(i).start()

    def end():
        total = sums[3]
        for i in range(3):
            rest(i).wait()
            total = total + sums[i]
        out[...] = total

    return start, middle, end


COT, NORMED2, PAIR, GRAD_UP, TOKENS, NORMED1 = 0, 1, 2, 4, 8, 9
QUERY, KEY, VALUE, GRAD_CONTEXT, GRAD_BRANCH, CONTEXT = 2, 3, 4, 5, 10, 11


def backward_kernel(comm, seqs, *refs):
    refs = list(refs)
    take = lambda n: [refs.pop(0) for _ in range(n)]
    full, cot_h, slope_h, normed1_h, normed2_h, mid_h, q_h, k_h, v_h, ctx_h, probs_h, tokens_h, ready = take(13)
    table, mods, feat, cosine, sine = take(5)
    outs = take(6 if comm else 1)
    vec_out, input_o = take(2)
    if comm:
        own, l0 = take(2)
    else:
        (out,) = outs
    pool, gn, mid, weights, slots, shares, sums, gtab, sem_in, sem_pair, sem_w, sem_mid, sem_slot, sem_share = take(14)
    if comm:
        parts, vgot, vsums, vsend, vrecv = take(5)
        red = Reduce(ready, slots, own, l0, outs, *refs)
    tokens_n = pool.shape[1]
    per = tokens_n // seqs

    def fetch(src, i):
        return pltpu.make_async_copy(src, pool.at[i], sem_in.at[i])

    def fetch_slope(j):
        return pltpu.make_async_copy(slope_h.at[j], pool.at[PAIR + j % 2], sem_pair.at[j % 2])

    def fetch_share(n):
        return pltpu.make_async_copy(probs_h.at[n], shares.at[n % 2], sem_share.at[n % 2])

    def fetch_w(c, slot):
        return pltpu.make_async_copy(full.at[c], weights.at[slot], sem_w.at[slot])

    mid_in = pltpu.make_async_copy(mid_h, mid, sem_mid)
    fetch(cot_h, COT).start()
    fetch_slope(0).start()
    fetch_slope(1).start()
    fetch(normed2_h, NORMED2).start()
    fetch_w(9, 0).start()
    fetch_w(10, 1).start()
    mid_in.start()
    for src, i in ((tokens_h, TOKENS), (normed1_h, NORMED1), (ctx_h, CONTEXT)):
        fetch(src, i).start()
    if comm:
        red.begin()
        run, load, feed = red.run, red.load, red.feed
    else:
        run = load = feed = lambda *a: None
    when = pl.when if comm else (lambda cond: lambda body: None)

    half_cols = lambda h: slice(h * HALF, (h + 1) * HALF)

    def half_rows(slot, h):
        if comm:
            return weights[slot, 2 * h : 2 * h + 2].reshape(HALF, 1024)
        return weights[slot, half_cols(h), :]

    def produce(b, lhs, rhs_of):
        if comm:
            red.free(b)
        else:
            pl.when(b >= READY + 2)(
                lambda: pltpu.make_async_copy(slots.at[b % 2], out.at[b - READY - 2], sem_slot.at[b % 2]).wait()
            )
        for h in range(2):
            block = rhs_of(lhs, h).astype(LOW)
            if comm:
                slots[b % 2, :, :, :, :, :, half_cols(h)] = block.reshape(4, 2, 2, 2, 32, HALF)
            else:
                slots[b % 2, :, half_cols(h)] = block
        if comm:
            red.produced(b)
        else:
            pltpu.make_async_copy(slots.at[b % 2], out.at[b - READY], sem_slot.at[b % 2]).start()

    def times(i):
        return lambda lhs, h: lax.dot_general(lhs[...], pool[i, :, half_cols(h)], TN, preferred_element_type=WIDE)

    ones = jnp.ones((8, tokens_n), LOW)

    def column_sums(i, row):
        gtab[pl.ds(row, 1), :] = jnp.dot(ones, pool[i], preferred_element_type=WIDE)[:1]

    def up(j):
        produce(4 + j, pool.at[NORMED2], times(GRAD_UP + j))

    fetch(cot_h, COT).wait()
    load(0)
    feed(0)
    column_sums(COT, BIAS_D)

    def activ_back(j):
        fetch_slope(j).wait()
        fetch_w(9 + j, j % 2).wait()
        for h in range(2):
            grad = lax.dot_general(pool[COT], half_rows(j % 2, h), NT, preferred_element_type=WIDE)
            grad = (grad * pool[PAIR + j % 2, :, half_cols(h)].astype(WIDE)).astype(LOW)
            for n in range(4):
                f = 4 * h + n
                place = pl.ds(pl.multiple_of((f % 2 * 4 + j) * 128, 128), 128)
                pool[GRAD_UP + f // 2, :, place] = grad[:, n * 128 : (n + 1) * 128]

        pl.when(j < 2)(lambda: fetch_w(11 + j, j % 2).start())
        pl.when(j >= 2)(lambda: fetch_w(3 + j, j % 2).start())
        pl.when(j < 2)(lambda: fetch_slope(j + 2).start())
        when(j >= 1)(lambda: feed(j))
        when(j == 0)(lambda: load(1))
        when(j == 1)(lambda: load(2))
        when(j == 2)(lambda: load(3))
        when(j >= 1)(lambda: run(j - 1, j))

    for_each(4, activ_back)
    fetch(q_h, QUERY).start()
    fetch(k_h, KEY).start()
    fetch(normed2_h, NORMED2).wait()

    def up_back(j):
        fetch_w(5 + j, j % 2).wait()
        for h in range(2):
            more = lax.dot_general(pool[GRAD_UP + j], half_rows(j % 2, h), NT, preferred_element_type=WIDE)

            @pl.when(j == 0)
            def _():
                gn[:, half_cols(h)] = more

            @pl.when(j > 0)
            def _():
                gn[:, half_cols(h)] = gn[:, half_cols(h)] + more

        pl.when(j < 2)(lambda: fetch_w(7 + j, j % 2).start())
        pl.when(j == 2)(lambda: fetch_w(4, 0).start())
        pl.when(j == 3)(lambda: fetch_w(1, 1).start())
        column_sums(GRAD_UP + j, BIAS_U + j)
        when(j == 2)(lambda: load(4))
        when(j == 3)(lambda: feed(4))
        pl.when(j % 2 == 1)(lambda: up(j // 2))
        when(j % 2 == 0)(lambda: run(3 + j // 2, 4 + j // 2))

    for_each(4, up_back)
    fetch(v_h, VALUE).start()
    fetch_share(0).start()
    fetch_share(1).start()

    sums[...] = jnp.zeros_like(sums)

    def norm_back(which, gain, value_of, done):
        def body(i):
            rows = rows_at(i)
            s = i // (per // TILE)
            at_scale, at_shift = 2 * which * seqs + s, (2 * which + 1) * seqs + s
            scale = table[gain : gain + 1, :] + row_of(mods, at_scale)
            normed, inverse = normalise(value_of(rows).astype(WIDE))
            grad = gn[rows, :]
            sums[pl.ds(at_scale, 1), :] += jnp.sum(grad * normed, axis=0, keepdims=True)
            sums[pl.ds(at_shift, 1), :] += jnp.sum(grad, axis=0, keepdims=True)
            hat = grad * scale
            done(rows, inverse * (hat - lane_mean(hat) - normed * lane_mean(hat * normed)))

        for_each(tokens_n // TILE, body)
        for n in range(2):
            at = (2 * which + n) * seqs
            gtab[gain + n : gain + n + 1, :] = jnp.sum(sums[at : at + seqs, :], axis=0, keepdims=True)

    mid_in.wait()

    def done2(rows, grad):
        total = pool[COT, rows, :].astype(WIDE) + grad
        mid[rows, :] = total
        pool[GRAD_BRANCH, rows, :] = total.astype(LOW)

    norm_back(1, GAIN2, lambda rows: mid[rows, :], done2)
    load(5)
    run(5, 7)

    column_sums(GRAD_BRANCH, BIAS_O)
    fetch_w(4, 0).wait()
    for h in range(2):
        grad = lax.dot_general(pool[GRAD_BRANCH], half_rows(0, h), NT, preferred_element_type=WIDE)
        pool[GRAD_CONTEXT, :, half_cols(h)] = grad.astype(LOW)
    fetch_w(2, 0).start()
    feed(5)
    up(2)
    run(7, 8)
    for src, i in ((q_h, QUERY), (k_h, KEY), (v_h, VALUE), (ctx_h, CONTEXT), (tokens_h, TOKENS), (normed1_h, NORMED1)):
        fetch(src, i).wait()

    lane = lax.broadcasted_iota(jnp.int32, (1, 128), 1)
    first_head = (lane < 64).astype(WIDE)
    second_head = 1.0 - first_head

    def split(v):
        return jnp.concatenate([v * first_head.astype(LOW), v * second_head.astype(LOW)], axis=0)

    def unturned(v):
        return v * cosine[...] - swapped(v) * sine[...]

    def heads(n):
        cols = pl.ds(pl.multiple_of(n * 128, 128), 128)
        fetch_share(n).wait()
        for s in range(seqs):
            rows = slice(s * per, (s + 1) * per)
            keys = pool[KEY, rows, cols]
            both = split(pool[QUERY, rows, cols])
            grads = split(pool[GRAD_CONTEXT, rows, cols])
            share = shares[n % 2, 2 * s * per : 2 * (s + 1) * per, :]
            probs = share.astype(WIDE)
            grad_probs = lax.dot_general(grads, pool[VALUE, rows, cols], NT, preferred_element_type=WIDE)
            inner = jnp.sum(grad_probs * probs, axis=-1, keepdims=True)
            grad_scores = (probs * (grad_probs - inner)).astype(LOW)
            grad_v = lax.dot_general(share, grads, TN, preferred_element_type=WIDE)
            grad_k = lax.dot_general(grad_scores, both, TN, preferred_element_type=WIDE)
            grad_q = jnp.dot(grad_scores, keys, preferred_element_type=WIDE)
            grad_q = (grad_q[:per] * first_head + grad_q[per:] * second_head) * 0.125
            pool[QUERY, rows, cols] = unturned(grad_q).astype(LOW)
            pool[KEY, rows, cols] = unturned(grad_k).astype(LOW)
            pool[VALUE, rows, cols] = grad_v.astype(LOW)

        pl.when(n < 6)(lambda: fetch_share(n + 2).start())
        when(n % 3 == 0)(lambda: load(6 + n // 3))
        when(jnp.logical_and(n % 3 == 1, n < 7))(lambda: feed(6 + n // 3))
        when(n == 7)(lambda: feed(8))

        @pl.when(jnp.logical_or(n == 2, n == 5))
        def _():
            lhs = jnp.where(n == 2, NORMED2, CONTEXT)
            rhs = jnp.where(n == 2, GRAD_UP + 3, GRAD_BRANCH)
            produce(6 + (n + 1) // 3, pool.at[lhs], times(rhs))

        done = 8 + n - (n + 2) // 3
        when(n % 3 != 0)(lambda: run(done, done + 1))

    for_each(8, heads)

    def project(j):
        column_sums(QUERY + j, BIAS_P + j)
        when(j == 2)(lambda: feed(9))
        produce(9 + j, pool.at[NORMED1], times(QUERY + j))
        when(j >= 1)(lambda: load(8 + j))
        run(13 + j, 14 + j)

    for_each(3, project)

    def project_back(j):
        slot = (1 + j) % 2
        fetch_w(1 + j, slot).wait()
        for h in range(2):
            more = lax.dot_general(pool[QUERY + j], half_rows(slot, h), NT, preferred_element_type=WIDE)

            @pl.when(j == 0)
            def _():
                gn[:, half_cols(h)] = more

            @pl.when(j > 0)
            def _():
                gn[:, half_cols(h)] = gn[:, half_cols(h)] + more

        pl.when(j == 0)(lambda: fetch_w(3, 1).start())
        when(j < 2)(lambda: feed(10 + j))
        when(j == 0)(lambda: load(11))
        when(j < 2)(lambda: run(16 + j, 17 + j))

    for_each(3, project_back)

    def done1(rows, grad):
        mid[rows, :] = mid[rows, :] + grad

    norm_back(0, GAIN1, lambda rows: pool[TOKENS, rows, :], done1)
    input_copy = pltpu.make_async_copy(mid, input_o, sem_mid)
    input_copy.start()
    run(18, 20)
    if comm:
        for f in range(8):
            for row in range(13):
                r, b = vector_spot(row, f)
                parts[f, row : row + 1, :] = gtab[r : r + 1, b * 128 : (b + 1) * 128]
            parts[f, 13:16, :] = jnp.zeros((3, 128), WIDE)
        start, middle, end = sum_vectors(red.at, parts, vgot, vsums, vec_out, vsend, vrecv)
        start()
    else:
        vec_out[...] = gtab[...]

    def outer(lhs, h):
        terms = sums[:, half_cols(h)]
        high = terms.astype(LOW)
        rest = (terms - high.astype(WIDE)).astype(LOW)
        return lax.dot_general(lhs[...], high, TN, preferred_element_type=WIDE) + lax.dot_general(
            lhs[...], rest, TN, preferred_element_type=WIDE
        )

    produce(12, feat, outer)
    load(12)
    feed(12)
    if comm:
        run(20, 24)
        middle()
        run(24, 28)
        end()
        run(28, red.drains)
        red.end()
    else:
        for b in (11, 12):
            pltpu.make_async_copy(slots.at[b % 2], out.at[b - READY], sem_slot.at[b % 2]).wait()
    input_copy.wait()


def backward_call(comm, full, cot, saved, tokens, table, mods, feat, cosine, sine, seqs):
    n, width = tokens.shape
    vmem, hbm = pl.BlockSpec(memory_space=pltpu.VMEM), pl.BlockSpec(memory_space=pl.ANY)
    ready, q, k, v, ctx, mid, normed1, normed2, slope, probs = saved
    block = (4, 2, 2, 2, 32, width) if comm else (width, width)
    rows = width // 8
    if comm:
        shapes = [(rows, 3 * width), (rows, width), (rows, 4 * width), (4 * rows, width), (TE // 8, 2 * width), (TE // 8, 2 * width)]
    else:
        shapes = [(BLOCKS - READY, width, width)]
    outs = [(jax.ShapeDtypeStruct(shape, LOW), hbm) for shape in shapes] + [
        (jax.ShapeDtypeStruct((16, 128) if comm else (16, width), WIDE), vmem),
        (jax.ShapeDtypeStruct((n, width), WIDE), hbm),
    ]
    extra = []
    if comm:
        part = lambda count: (jax.ShapeDtypeStruct((count, 4, 2, 2, 32, width), LOW), hbm)
        outs += [part(BLOCKS - READY), part(BLOCKS)]
        extra = [
            pltpu.VMEM((8, 16, 128), WIDE),
            pltpu.VMEM((7, 16, 128), WIDE),
            pltpu.VMEM((4, 16, 128), WIDE),
            pltpu.SemaphoreType.DMA((10,)),
            pltpu.SemaphoreType.DMA((10,)),
        ] + REDUCE_SCRATCH
        full = full.reshape((BLOCKS,) + block)
    got = pl.pallas_call(
        functools.partial(backward_kernel, comm, seqs),
        out_shape=tuple(s for s, _ in outs),
        in_specs=[hbm] * 13 + [vmem] * 5,
        out_specs=tuple(m for _, m in outs),
        scratch_shapes=[
            pltpu.VMEM((12, n, width), LOW),
            pltpu.VMEM((n, width), WIDE),
            pltpu.VMEM((n, width), WIDE),
            pltpu.VMEM((2,) + block, LOW),
            pltpu.VMEM((2,) + block, LOW),
            pltpu.VMEM((2,) + probs.shape[1:], LOW),
            pltpu.VMEM((feat.shape[0], width), WIDE),
            pltpu.VMEM((16, width), WIDE),
            pltpu.SemaphoreType.DMA((12,)),
            pltpu.SemaphoreType.DMA((2,)),
            pltpu.SemaphoreType.DMA((2,)),
            pltpu.SemaphoreType.DMA,
            pltpu.SemaphoreType.DMA((2,)),
            pltpu.SemaphoreType.DMA((2,)),
        ]
        + extra,
        compiler_params=pltpu.CompilerParams(
            collective_id=1 if comm else None, has_side_effects=comm, vmem_limit_bytes=62 * 2**20
        ),
        name="backward",
    )(full, cot, slope, normed1, normed2, mid, q, k, v, ctx, probs, tokens, ready, table, mods, feat, cosine, sine)
    return got[: len(shapes) + 2]


def widen(arrays, vec, sizes):
    count = len(arrays)

    def kernel(vec_in, *refs):
        srcs, dsts, lines = refs[:count], refs[count : 2 * count], refs[2 * count : 2 * count + len(sizes)]
        rest = refs[2 * count + len(sizes) :]
        lows, wides, sems = rest[:count], rest[count : 2 * count], rest[-1]
        ins = [pltpu.make_async_copy(s, v, sems.at[i]) for i, (s, v) in enumerate(zip(srcs, lows))]
        outs = [pltpu.make_async_copy(v, d, sems.at[i]) for i, (v, d) in enumerate(zip(wides, dsts))]
        for copy in ins:
            copy.start()
        row = 0
        for line, size in zip(lines, sizes):
            for k in range(size // 128):
                line[pl.ds(128 * k, 128)] = vec_in[row, :]
                row += 1
        for i in range(count):
            ins[i].wait()

            def body(n, i=i):
                at = pl.ds(pl.multiple_of(n * 16, 16), 16)
                wides[i][at, :] = lows[i][at, :].astype(WIDE)

            for_each(lows[i].shape[0] // 16, body)
            outs[i].start()
        for copy in outs:
            copy.wait()

    hbm, vmem = pl.BlockSpec(memory_space=pl.ANY), pl.BlockSpec(memory_space=pltpu.VMEM)
    got = pl.pallas_call(
        kernel,
        out_shape=tuple(jax.ShapeDtypeStruct(a.shape, WIDE) for a in arrays)
        + tuple(jax.ShapeDtypeStruct((size,), WIDE) for size in sizes),
        in_specs=[vmem] + [hbm] * count,
        out_specs=(hbm,) * count + (vmem,) * len(sizes),
        scratch_shapes=[pltpu.VMEM(a.shape, LOW) for a in arrays]
        + [pltpu.VMEM(a.shape, WIDE) for a in arrays]
        + [pltpu.SemaphoreType.DMA((count,))],
        compiler_params=pltpu.CompilerParams(vmem_limit_bytes=60 * 2**20),
        name="widen",
    )(vec, *arrays)
    return got[:count], got[count:]


def rotary_constants(length, head_dim):
    half_width = head_dim // 2
    inverse = np.exp(np.arange(half_width, dtype=np.float32) * np.float32(-math.log(10000.0) / half_width))
    angles = np.arange(length, dtype=np.float32)[:, None] * inverse[None, :]
    cosine, sine = np.cos(angles), np.sin(angles)
    pair = np.concatenate([cosine, cosine], axis=1), np.concatenate([-sine, sine], axis=1)
    return tuple(np.concatenate([t, t], axis=1).astype(np.float32) for t in pair)


def wide_features(noise_times, width):
    seqs = noise_times.shape[0]
    half_width = TE // 2
    column = np.arange(width)
    feature = column // 128 * 32 + column % 32
    rates = np.exp((feature % half_width).astype(np.float32) * np.float32(math.log(100.0) / half_width))
    row = np.arange(-(-4 * seqs // 32) * 32)
    times = jnp.sum(jnp.where(row[:, None] % seqs == np.arange(seqs)[None, :], noise_times[None, :], 0.0), axis=1)
    phases = (jnp.log(times) * 0.25)[:, None] * rates[None, :]
    feat = jnp.where((feature < half_width)[None, :], jnp.sin(phases), jnp.cos(phases))
    return jnp.where((column // 32 % 4)[None, :] == (row // seqs)[:, None], feat, 0.0).astype(LOW)


def gather_plain(weights, vectors):
    project, output, up, down, time1, time2 = weights
    rows, width = output.shape
    each = time1.shape[0]
    columns = lambda w: w.reshape(rows, -1, width).transpose(1, 0, 2)
    times = jnp.stack([time1, time2]).reshape(2, each, 2, width).transpose(0, 2, 1, 3)
    own = jnp.concatenate(
        [times.reshape(1, rows, width), columns(project), output[None], columns(up), down.reshape(4, rows, width)]
    )
    full = lax.all_gather(own, "fsdp", axis=1, tiled=True)
    times = full[0].reshape(-1, 2, 2, each, width).transpose(1, 2, 0, 3, 4).reshape(2, 2, 8, 32, width)
    down = full[9:].reshape(4, -1, rows, width).transpose(1, 0, 2, 3).reshape(8, 4, 128, width)
    full = jnp.concatenate(
        [
            times.transpose(2, 0, 1, 3, 4).reshape(1, width, width),
            full[1:9],
            down.transpose(1, 0, 2, 3).reshape(4, width, width),
        ]
    )
    sizes = [v.shape[0] for v in vectors]
    whole = pieces_of(lax.all_gather(jnp.concatenate(vectors), "fsdp", axis=0), sizes)
    table = jnp.concatenate([w.reshape(-1, width) for w in whole]).astype(WIDE)
    return full, jnp.pad(table, ((0, 3), (0, 0)))


def reduce_plain(parts, table, sizes, shards_of):
    width = parts.shape[-1]
    rows, each = width // shards_of, TE // shards_of
    down = parts[:4].reshape(4, 8, 128, width).transpose(1, 0, 2, 3).reshape(shards_of, 4, rows, width)
    times = parts[12].reshape(8, 2, 2, 32, width).transpose(1, 2, 0, 3, 4).reshape(2, 2, shards_of, each, width)
    own = jnp.concatenate(
        [
            down.transpose(1, 0, 2, 3).reshape(4, width, width),
            parts[4:12],
            times.transpose(2, 0, 1, 3, 4).reshape(1, width, width),
        ]
    )
    mine = lax.psum(lax.psum_scatter(own, "fsdp", scatter_dimension=1, tiled=True), "rep")
    whole = pieces_of(table[:13].reshape(-1), [shards_of * size for size in sizes])
    vec = jnp.concatenate([w.reshape(shards_of, -1) for w in whole], axis=1)
    vec = lax.psum(lax.psum_scatter(vec, "fsdp", scatter_dimension=0, tiled=True)[0], "rep")
    columns = lambda w: w.transpose(1, 0, 2).reshape(rows, -1)
    times = mine[12].reshape(2, 2, each, width).transpose(0, 2, 1, 3).reshape(2, each, 2 * width)
    return columns(mine[9:12]), mine[8], columns(mine[4:8]), mine[:4].reshape(-1, width), times[0], times[1], vec


def pieces_of(flat, sizes):
    at, got = 0, []
    for size in sizes:
        got.append(flat[..., at : at + size])
        at += size
    return got


def shards(
    inputs,
    noise_times,
    cotangent,
    norm1_gain,
    norm1_bias,
    norm1_time,
    project_weight,
    project_bias,
    output_weight,
    output_bias,
    norm2_gain,
    norm2_bias,
    norm2_time,
    up_weight,
    up_bias,
    down_weight,
    down_bias,
):
    seqs = noise_times.shape[0]
    tokens_n, width = inputs.shape
    rows = output_weight.shape[0]
    shards_of = width // rows
    comm = shards_of == 8
    feat = wide_features(noise_times, width)
    cosine, sine = rotary_constants(tokens_n // seqs, width // HEADS)
    weights = (project_weight, output_weight, up_weight, down_weight, norm1_time, norm2_time)
    vectors = (norm1_gain, norm1_bias, project_bias, output_bias, norm2_gain, norm2_bias, up_bias, down_bias)
    sizes = [v.shape[0] for v in vectors]
    if comm:
        at, table = 0, jnp.zeros((16, 128), WIDE)
        for v in vectors:
            lines = v.astype(WIDE).reshape(-1, 128)
            table = table + jnp.pad(lines, ((at, 16 - at - lines.shape[0]), (0, 0)))
            at += lines.shape[0]
    else:
        full, table = gather_plain(weights, vectors)
        weights = (full,)
    full, table, mods, layer_out, *saved = forward_call(
        comm, weights, table, inputs, cotangent, feat, cosine, sine, seqs
    )
    *sums, input_grad = backward_call(comm, full, cotangent, saved, inputs, table, mods, feat, cosine, sine, seqs)
    if not comm:
        sums = reduce_plain(jnp.concatenate([saved[0], sums[0]]), sums[1], sizes, shards_of)
    if comm:
        wide, got = widen(sums[:6], sums[6], sizes)
    else:
        wide, got = [s.astype(WIDE) for s in sums[:6]], pieces_of(sums[6], sizes)
    project, output, up, down, time1, time2 = wide
    return (
        layer_out,
        input_grad,
        got[0],
        got[1],
        time1,
        project,
        got[2],
        output,
        got[3],
        got[4],
        got[5],
        time2,
        up,
        got[6],
        down,
        got[7],
    )


def solution(mesh):
    placed = (
        P(("rep", "fsdp"), None),
        P(("rep", "fsdp")),
        P(("rep", "fsdp"), None),
        P("fsdp"),
        P("fsdp"),
        P("fsdp", None),
        P("fsdp", None),
        P("fsdp"),
        P("fsdp", None),
        P("fsdp"),
        P("fsdp"),
        P("fsdp"),
        P("fsdp", None),
        P("fsdp", None),
        P("fsdp"),
        P("fsdp", None),
        P("fsdp"),
    )
    return jax.shard_map(
        shards,
        mesh=mesh,
        in_specs=placed,
        out_specs=(
            P(("rep", "fsdp"), None),
            P(("rep", "fsdp"), None),
            P("fsdp"),
            P("fsdp"),
            P("fsdp", None),
            P("fsdp", None),
            P("fsdp"),
            P("fsdp", None),
            P("fsdp"),
            P("fsdp"),
            P("fsdp"),
            P("fsdp", None),
            P("fsdp", None),
            P("fsdp"),
            P("fsdp", None),
            P("fsdp"),
        ),
        check_vma=False,
    )
```

```python
import functools
import math

import jax
import jax.numpy as jnp
import numpy as np
from jax import lax
from jax.experimental import pallas as pl
from jax.experimental.pallas import tpu as pltpu
from jax.sharding import PartitionSpec as P

HEADS = 16
TE = 256
epsilon = 1e-05


MESH = pl.DeviceIdType.MESH
LOW, WIDE = jnp.bfloat16, jnp.float32
FRONT = 384
BLOCKS = 13
PIECES = 2 * BLOCKS
NT = (((1,), (1,)), ((), ()))
TN = (((0,), (0,)), ((), ()))


class Place:
    def __init__(self):
        r, f = lax.axis_index("rep"), lax.axis_index("fsdp")
        self.r, self.f = r, f
        self.x, self.core = r // 2, r % 2
        self.z, self.y = f // 2, f % 2
        z = self.z
        self.zs = [z, z + 1 - 2 * (z % 2), (z + 2) % 4, 3 - z]
        self.same = [zk * 2 + self.y for zk in self.zs]
        self.other = [zk * 2 + 1 - self.y for zk in self.zs]
        self.across_x = ((1 - self.x) * 2 + self.core, f)
        self.across_y = (r, self.other[0])
        self.across_core = (self.x * 2 + 1 - self.core, f)
        self.diagonal = ((1 - self.x) * 2 + 1 - self.core, f)
        self.along_z = [(r, fk) for fk in self.same]
        self.shards = self.same[1:] + self.other
        self.group = [(r, fk) for fk in self.shards]


def greet(peers):
    barrier = pltpu.get_barrier_semaphore()
    for peer in peers:
        pl.semaphore_signal(barrier, inc=1, device_id=peer, device_id_type=MESH)
    pl.semaphore_wait(barrier, len(peers))


def remote(src, dst, send, recv, peer):
    return pltpu.make_async_remote_copy(
        src_ref=src, dst_ref=dst, send_sem=send, recv_sem=recv, device_id=peer, device_id_type=MESH
    )


class Gather:
    def __init__(self, own, vec, full, vecs, send, recv, vsend, vrecv, lsem):
        self.at = Place()
        self.own, self.full, self.send, self.recv, self.lsem = own, full, send, recv, lsem
        self.vec, self.vecs, self.vsend, self.vrecv = vec, vecs, vsend, vrecv
        x = self.at.x
        self.middle = jnp.logical_and(self.at.z >= 1, self.at.z <= 2)
        rest = 1024 - FRONT
        self.mine = pl.ds(pl.multiple_of(x * FRONT, 128), rest)
        self.xcols = pl.ds(pl.multiple_of(x * rest, 128), FRONT)
        self.xland = pl.ds(pl.multiple_of((1 - x) * rest, 128), FRONT)

    def spot(self, c, z, y, cols, core=None):
        core = self.at.core if core is None else core
        return self.full.at[c // 2, z, y, core, c % 2, :, cols]

    def pair(self, c, i, src, dst, peer):
        return remote(src, dst, self.send.at[c, i], self.recv.at[c, i], peer)

    def owned(self, c, cols):
        return self.own.at[c // 2, pl.ds(pl.multiple_of(self.at.core * 64 + c % 2 * 32, 32), 32), cols]

    def z_copy(self, c, k):
        at = self.at
        src = self.owned(c, self.mine)
        return self.pair(c, k - 1, src, self.spot(c, at.z, at.y, self.mine), at.along_z[k])

    def z_relay(self, c):
        dst = self.spot(c, self.at.zs[2], self.at.y, self.mine)
        return remote(dst, dst, self.send.at[c, 12], self.recv.at[c, 2], self.at.along_z[1])

    def z_land(self, c, k):
        dst = self.spot(c, self.at.zs[k], self.at.y, self.mine)
        return self.pair(c, k - 1, dst, dst, self.at.along_z[k])

    def y_copy(self, c, k):
        at = self.at
        dst = self.spot(c, at.zs[k], at.y, self.mine)
        src = self.owned(c, self.mine) if k == 0 else dst
        return self.pair(c, 3 + k, src, dst, at.across_y)

    def y_land(self, c, k):
        dst = self.spot(c, self.at.zs[k], 1 - self.at.y, self.mine)
        return self.pair(c, 3 + k, dst, dst, self.at.across_y)

    def x_place(self, c, k, cols):
        at = self.at
        if k < 3:
            return self.spot(c, at.zs[k + 1], at.y, cols)
        return self.spot(c, slice(None), 1 - at.y, cols)

    def x_copy(self, c, k):
        src = self.x_place(c, k, self.xcols)
        return self.pair(c, 7 + k, src, src, self.at.across_x)

    def x_land(self, c, k):
        dst = self.x_place(c, k, self.xland)
        return self.pair(c, 7 + k, dst, dst, self.at.across_x)

    def core_copy(self, c, core=None):
        part = self.spot(c, slice(None), slice(None), slice(None), core)
        return self.pair(c, 11, part, part, self.at.across_core)

    def local(self, c):
        at = self.at
        dst = self.spot(c, at.z, at.y, slice(None))
        return pltpu.make_async_copy(self.owned(c, slice(None)), dst, self.lsem.at[c])

    def first(self, c):
        for k in range(1, 3):
            self.z_copy(c, k).start()
        pl.when(self.middle)(lambda: self.z_copy(c, 3).start())
        self.y_copy(c, 0).start()
        self.local(c).start()

    ahead = 4

    def begin(self):
        at = self.at
        greet([at.across_core, at.across_x] + at.group)
        for i, peer in enumerate(at.group):
            remote(self.vec, self.vecs.at[at.f], self.vsend.at[i], self.vrecv.at[i], peer).start()

    def start(self):
        for c in range(self.ahead):
            self.first(c)

    def vectors(self):
        at = self.at
        self.vecs[at.f] = self.vec[...]
        for i, peer in enumerate(at.group):
            remote(self.vec, self.vecs.at[at.shards[i]], self.vsend.at[i], self.vrecv.at[i], peer).wait()

    lag_x, lag_core, lag_done = 2, 4, 5

    def step(self, t):
        lag_x, lag_core, lag_done = self.lag_x, self.lag_core, self.lag_done

        @pl.when(t + self.ahead < PIECES)
        def _():
            self.first(t + self.ahead)

        @pl.when(t < PIECES)
        def _():
            for k in (2, 1, 3):
                self.z_land(t, k).wait_recv()
                if k == 2:
                    pl.when(self.middle)(lambda: self.z_relay(t).start())
                self.y_copy(t, k).start()

        @pl.when(jnp.logical_and(t >= lag_x, t < PIECES + lag_x))
        def _():
            c = t - lag_x
            for k in range(4):
                if k == 3:
                    for j in range(4):
                        self.y_land(c, j).wait_recv()
                self.x_copy(c, k).start()

        @pl.when(jnp.logical_and(t >= lag_core, t < PIECES + lag_core))
        def _():
            c = t - lag_core
            self.local(c).wait()
            for k in range(4):
                self.x_land(c, k).wait_recv()
            self.core_copy(c).start()

        @pl.when(jnp.logical_and(t >= lag_done, t < PIECES + lag_done))
        def _():
            c = t - lag_done
            self.core_copy(c, 1 - self.at.core).wait_recv()
            for k in range(1, 3):
                self.z_copy(c, k).wait_send()

            @pl.when(self.middle)
            def _():
                self.z_copy(c, 3).wait_send()
                self.z_relay(c).wait_send()

            for k in range(4):
                self.y_copy(c, k).wait_send()
                self.x_copy(c, k).wait_send()
            self.core_copy(c).wait_send()

    steps = PIECES + lag_done

    def ready(self, block):
        return 2 * block + 2 + self.lag_done

    def run(self, lo, hi):
        def one(t, carry):
            self.step(t)
            return carry

        lax.fori_loop(lo, hi, one, 0)


GATHER_SCRATCH = [
    pltpu.VMEM((8, 16, 128), WIDE),
    pltpu.SemaphoreType.DMA((PIECES, 13)),
    pltpu.SemaphoreType.DMA((PIECES, 12)),
    pltpu.SemaphoreType.DMA((7,)),
    pltpu.SemaphoreType.DMA((7,)),
    pltpu.SemaphoreType.DMA((PIECES,)),
]


GAIN1, BIAS1, BIAS_P, BIAS_O, GAIN2, BIAS2, BIAS_U, BIAS_D = 0, 1, 2, 5, 6, 7, 8, 12
HALF = 512
TILE = 64


def vector_spot(row, f):
    for first, count in ((BIAS_P, 3), (BIAS_U, 4)):
        if first <= row < first + count:
            block = f * count + row - first
            return first + block // 8, block % 8
    return row, f


def for_each(count, body):
    def one(i, carry):
        body(i)
        return carry

    lax.fori_loop(0, count, one, 0)


def rows_at(i, size=TILE):
    return pl.ds(pl.multiple_of(i * size, size), size)


def lane_mean(v):
    return jnp.mean(v, axis=-1, keepdims=True)


def normalise(v):
    centred = v - lane_mean(v)
    inverse = lax.rsqrt(lane_mean(centred * centred) + epsilon)
    return centred * inverse, inverse


def row_of(ref, i):
    return ref[pl.ds(i, 1), :]


def part_of(norm, shift, seqs):
    return norm * (-(-2 * seqs // 16) * 16) + shift * seqs


def modulated(ref, out, table, mods, gain, which, seqs):
    per = ref.shape[0] // seqs // TILE

    def body(i):
        s = i // per
        scale = table[gain : gain + 1, :] + row_of(mods, part_of(which, 0, seqs) + s)
        shift = table[gain + 1 : gain + 2, :] + row_of(mods, part_of(which, 1, seqs) + s)
        rows = rows_at(i)
        normed, _ = normalise(ref[rows, :].astype(WIDE))
        out[rows, :] = (normed * scale + shift).astype(LOW)

    for_each(ref.shape[0] // TILE, body)


def swapped(v):
    lane = lax.broadcasted_iota(jnp.int32, v.shape, 1)
    return jnp.where(lane % 64 < 32, pltpu.roll(v, 96, 1), pltpu.roll(v, 32, 1))


def pack(local, own, sems):
    project, output, up, down, time1, time2 = local
    pairs = [(t.at[:, pl.ds(1024 * h, 1024)], own.at[0, pl.ds(64 * n + 32 * h, 32)]) for n, t in enumerate((time1, time2)) for h in range(2)]
    pairs += [(project.at[:, pl.ds(1024 * j, 1024)], own.at[1 + j]) for j in range(3)] + [(output, own.at[4])]
    pairs += [(up.at[:, pl.ds(1024 * j, 1024)], own.at[5 + j]) for j in range(4)]
    pairs += [(down.at[pl.ds(128 * j, 128)], own.at[9 + j]) for j in range(4)]
    return [pltpu.make_async_copy(src, dst, sems.at[i]) for i, (src, dst) in enumerate(pairs)]


def forward_kernel(comm, seqs, *refs):
    refs = list(refs)
    take = lambda n: [refs.pop(0) for _ in range(n)]
    if comm:
        local, vec = take(6), take(1)[0]
    else:
        full_in, table_in = take(2)
    tokens_hbm, cot_hbm, feat, cosine, sine = take(5)
    if comm:
        (full,) = take(1)
    else:
        full = full_in
    table, mods = take(2)
    grad_o, q_o, k_o, v_o, ctx_o, mid_o, normed1_o, normed2_o, activ_o, slope_o, probs_o = take(11)
    tokens, cot, weights, normed, normed2, q, k, v, ctx, mid, activ, slope, wide, probs, grads = take(15)
    sem_in, sem_w, sem_out, sem_grad = take(4)
    tokens_n = tokens.shape[0]
    per = tokens_n // seqs

    tokens_in = pltpu.make_async_copy(tokens_hbm, tokens, sem_in.at[0])
    tokens_in.start()
    cot_in = pltpu.make_async_copy(cot_hbm, cot, sem_in.at[1])
    cot_in.start()
    if comm:
        own, sem_own = take(2)
        gather = Gather(own, vec, full, *refs)
        packing = pack(local, own, sem_own)
        for copy in packing:
            copy.start()
        gather.begin()
        for copy in packing:
            copy.wait()
        gather.start()
        gather.vectors()
        for f in range(8):
            block = gather.vecs[f]
            for row in range(13):
                r, b = vector_spot(row, f)
                table[r : r + 1, b * 128 : (b + 1) * 128] = block[row : row + 1, :]
        run = gather.run
    else:
        table[...] = table_in[...]
        run = lambda lo, hi: None

    def fetch(c):
        return pltpu.make_async_copy(full.at[c], weights.at[c % 2], sem_w.at[c % 2])

    def arrive(c, lo, hi):
        run(lo, hi)
        fetch(c).start()

    def weight(c):
        fetch(c).wait()
        return weights.at[c % 2]

    ready = Gather.lag_done + 2
    flat = (lambda w: w[...].reshape(1024, 1024)) if comm else (lambda w: w[...])

    saves = []

    def save(src, dst):
        copy = pltpu.make_async_copy(src, dst, sem_out.at[len(saves)])
        copy.start()
        saves.append(copy)

    arrive(0, 0, ready)
    w = weight(0)
    mods[...] = jnp.dot(feat[...], flat(w), preferred_element_type=WIDE)
    tokens_in.wait()
    arrive(1, ready, ready + 2)
    modulated(tokens, normed, table, mods, GAIN1, 0, seqs)
    save(normed, normed1_o)

    for j, (dst, dst_o) in enumerate([(q, q_o), (k, k_o), (v, v_o)]):
        w = weight(1 + j)
        for h in range(2):
            cols = slice(h * HALF, (h + 1) * HALF)
            wide[...] = jnp.dot(normed[...], half_of(w, cols, comm), preferred_element_type=WIDE)
            run(ready + 2 + 2 * j + h, ready + 3 + 2 * j + h)
            if h == 1:
                fetch(2 + j).start()
            bias = table[BIAS_P + j : BIAS_P + j + 1, cols]

            def body(i, h=h, bias=bias, dst=dst, j=j):
                rows = rows_at(i)
                where = pl.ds(pl.multiple_of((i % (per // TILE)) * TILE, TILE), TILE)
                piece = wide[rows, :] + bias
                if j == 2:
                    dst[rows, h * HALF : (h + 1) * HALF] = piece.astype(LOW)
                    return
                for n in range(HALF // 128):
                    part = piece[:, n * 128 : (n + 1) * 128]
                    turned = part * cosine[where, :] + swapped(part) * sine[where, :]
                    if j == 0:
                        turned = turned * 0.125
                    at = h * HALF + n * 128
                    dst[rows, at : at + 128] = turned.astype(LOW)

            for_each(tokens_n // TILE, body)
        save(dst, dst_o)

    lane = lax.broadcasted_iota(jnp.int32, (1, 128), 1)
    first_head = (lane < 64).astype(WIDE)
    second_head = 1.0 - first_head

    def heads(n):
        cols = pl.ds(pl.multiple_of(n * 128, 128), 128)
        for s in range(seqs):
            rows = slice(s * per, (s + 1) * per)
            qs = q[rows, cols]
            both = jnp.concatenate([qs * first_head.astype(LOW), qs * second_head.astype(LOW)], axis=0)
            scores = lax.dot_general(both, k[rows, cols], NT, preferred_element_type=WIDE)
            grown = jnp.exp(scores - jnp.max(scores, axis=-1, keepdims=True))
            share = (grown / jnp.sum(grown, axis=-1, keepdims=True)).astype(LOW)
            probs[n, 2 * s * per : 2 * (s + 1) * per, :] = share
            mixed = jnp.dot(share, v[rows, cols], preferred_element_type=WIDE)
            ctx[rows, cols] = (mixed[:per] * first_head + mixed[per:] * second_head).astype(LOW)
        if comm:
            pl.when(n >= 2)(lambda: gather.step(ready + 6 + n))

    for_each(8, heads)
    save(ctx, ctx_o)
    save(probs, probs_o)

    w = weight(4)
    for h in range(2):
        cols = slice(h * HALF, (h + 1) * HALF)
        dot = jnp.dot(ctx[...], half_of(w, cols, comm), preferred_element_type=WIDE)
        mid[:, cols] = tokens[:, cols].astype(WIDE) + (dot + table[BIAS_O : BIAS_O + 1, cols])
    arrive(5, ready + 14, ready + 15)
    save(mid, mid_o)
    modulated(mid, normed2, table, mods, GAIN2, 1, seqs)
    save(normed2, normed2_o)

    def up(j):
        w = weight(5 + j)
        for h in range(2):
            cols = slice(h * HALF, (h + 1) * HALF)
            wide[...] = jnp.dot(normed2[...], half_of(w, cols, comm), preferred_element_type=WIDE)
            if h == 0:
                once = ready + 15 + 2 * j - jnp.maximum(j - 2, 0)
                run(once, once + 1)
            else:
                run(ready + 16 + 2 * j, ready + 16 + 2 * j + (j < 2).astype(jnp.int32))
                pl.when(j < 3)(lambda: fetch(6 + j).start())

            def body(i, h=h, cols=cols):
                rows = rows_at(i)
                u = wide[rows, :] + table[pl.ds(BIAS_U + j, 1), cols]
                phi = 0.5 + 0.5 * lax.erf(u * (0.5**0.5))
                bell = jnp.exp(-0.5 * (u * u)) * (1.0 / math.sqrt(2.0 * math.pi))
                result, grow = (u * phi).astype(LOW), (phi + u * bell).astype(LOW)
                place = pl.ds(pl.multiple_of((2 * j + h) * 128, 128), 128)
                for n in range(4):
                    activ[n, rows, place] = result[:, n * 128 : (n + 1) * 128]
                    slope[n, rows, place] = grow[:, n * 128 : (n + 1) * 128]

            for_each(tokens_n // TILE, body)

    for_each(4, up)
    save(activ, activ_o)
    save(slope, slope_o)

    cot_in.wait()

    def grad_copy(j):
        return pltpu.make_async_copy(grads.at[j % 2], grad_o.at[j], sem_grad.at[j % 2])

    def down(j):
        pl.when(j >= 2)(lambda: grad_copy(j - 2).wait())
        for h in range(2):
            cols = slice(h * HALF, (h + 1) * HALF)
            block = lax.dot_general(activ[j], cot[:, cols], TN, preferred_element_type=WIDE).astype(LOW)
            if comm:
                grads[j % 2, :, :, :, :, :, cols] = block.reshape(4, 2, 2, 2, 32, HALF)
            else:
                grads[j % 2, :, cols] = block
        grad_copy(j).start()
        if comm:
            pl.when(j < 3)(lambda: run(ready + 21 + j, ready + 22 + j))

    for_each(4, down)
    grad_copy(2).wait()
    grad_copy(3).wait()
    for copy in saves:
        copy.wait()


def half_of(w, cols, comm):
    if comm:
        return w[..., cols].reshape(1024, HALF)
    return w[:, cols]


def forward_call(comm, weights, vectors, tokens, cot, feat, cosine, sine, seqs):
    n, width = tokens.shape
    vmem, hbm = pl.BlockSpec(memory_space=pltpu.VMEM), pl.BlockSpec(memory_space=pl.ANY)
    low = jax.ShapeDtypeStruct((n, width), LOW)
    wide = jax.ShapeDtypeStruct((n, width), WIDE)
    shape4 = jax.ShapeDtypeStruct((4, n, width), LOW)
    block = (4, 2, 2, 2, 32, width) if comm else (width, width)
    outs = [
        (jax.ShapeDtypeStruct((16, width), WIDE), vmem),
        (jax.ShapeDtypeStruct((feat.shape[0], width), WIDE), vmem),
    ]
    share = (8, 2 * n, 128)
    saved = (jax.ShapeDtypeStruct((4,) + block, LOW), low, low, low, low, wide, low, low, shape4, shape4)
    outs += [(s, hbm) for s in saved + (jax.ShapeDtypeStruct(share, LOW),)]
    extra = []
    if comm:
        outs = [(jax.ShapeDtypeStruct((BLOCKS,) + block, LOW), hbm)] + outs
        extra = [pltpu.VMEM((BLOCKS, 128, width), LOW), pltpu.SemaphoreType.DMA((16,))] + GATHER_SCRATCH
    buffer = pltpu.VMEM((n, width), LOW)
    got = pl.pallas_call(
        functools.partial(forward_kernel, comm, seqs),
        out_shape=tuple(s for s, _ in outs),
        in_specs=[hbm] * len(weights) + [vmem, hbm, hbm, vmem, vmem, vmem],
        out_specs=tuple(m for _, m in outs),
        scratch_shapes=[
            buffer,
            buffer,
            pltpu.VMEM((2,) + block, LOW),
            buffer,
            buffer,
            buffer,
            buffer,
            buffer,
            buffer,
            pltpu.VMEM((n, width), WIDE),
            pltpu.VMEM((4, n, width), LOW),
            pltpu.VMEM((4, n, width), LOW),
            pltpu.VMEM((n, HALF), WIDE),
            pltpu.VMEM(share, LOW),
            pltpu.VMEM((2,) + block, LOW),
            pltpu.SemaphoreType.DMA((2,)),
            pltpu.SemaphoreType.DMA((2,)),
            pltpu.SemaphoreType.DMA((10,)),
            pltpu.SemaphoreType.DMA((2,)),
        ]
        + extra,
        compiler_params=pltpu.CompilerParams(
            collective_id=0 if comm else None, has_side_effects=comm, vmem_limit_bytes=60 * 2**20
        ),
        name="forward",
    )(*weights, vectors, tokens, cot, feat, cosine, sine)
    if not comm:
        return (weights[0], vectors) + tuple(got[1:])
    return (got[0].reshape(BLOCKS, width, width),) + tuple(got[1:])


RING = 10
REDUCED = 12
PARTS = 2 * REDUCED
READY = 4


class Reduce:
    def __init__(self, ready, slots, own, l0, outs, *scratch):
        self.at = Place()
        self.ready, self.slots, self.own, self.l0, self.outs = ready, slots, own, l0, outs
        (self.held, self.s0, self.l1a, self.l1b, self.l2, self.l3, self.la) = scratch[:7]
        (self.bsend, self.brecv, self.lsem, self.send, self.recv, self.osem) = scratch[7:13]
        x = self.at.x
        self.front, self.back = pl.ds(0, FRONT), pl.ds(FRONT, 1024 - FRONT)
        self.mine = pl.ds(pl.multiple_of(x * 16, 16), 16)
        self.theirs = pl.ds(pl.multiple_of((1 - x) * 16, 16), 16)

    def begin(self):
        at = self.at
        greet([at.across_core, at.across_x, at.diagonal] + at.group)
        for b in range(READY):
            src = self.ready.at[b, :, :, 1 - at.core]
            remote(src, self.l0.at[b], self.bsend.at[b], self.brecv.at[b], at.across_core).start()

    def core_copy(self, b):
        src = self.slots.at[b % 2, :, :, 1 - self.at.core]
        return remote(src, self.l0.at[b], self.bsend.at[b], self.brecv.at[b], self.at.across_core)

    def own_copy(self, b):
        return pltpu.make_async_copy(self.slots.at[b % 2, :, :, self.at.core], self.own.at[b - READY], self.lsem.at[b % 2])

    def loads(self, b, ready=False):
        src = self.ready.at[b, :, :, self.at.core] if ready else self.own.at[b - READY]
        return (
            pltpu.make_async_copy(src, self.held.at[0], self.lsem.at[2]),
            pltpu.make_async_copy(self.l0.at[b], self.held.at[1], self.lsem.at[3]),
        )

    def free(self, b):
        self.core_copy(b - 2).wait_send()

    def produced(self, b):
        self.core_copy(b).start()
        self.own_copy(b).start()

    def load(self, b):
        self.core_copy(b).wait_recv()
        if isinstance(b, int) and b < READY:
            for copy in self.loads(b, True):
                copy.start()
            return
        self.own_copy(b).wait()
        for copy in self.loads(b):
            copy.start()

    def feed(self, b):
        for copy in self.loads(READY):
            copy.wait()

        def add(z):
            for h in range(2):
                self.s0[(2 * b + h) % RING, z] = self.held[0, z, :, h] + self.held[1, z, :, h]

        for_each(4, add)
        for h in range(2):
            self.x_one(2 * b + h).start()
            self.y_one(2 * b + h).start()

    def pair(self, p, i, src, dst, peer):
        return remote(src, dst, self.send.at[p, i], self.recv.at[p, i], peer)

    def x_one(self, p):
        src = self.s0.at[p % RING, :, :, self.theirs, self.front]
        return self.pair(p, 0, src, self.l1a.at[p], self.at.across_x)

    def y_one(self, p):
        src = self.s0.at[p % RING, :, 1 - self.at.y, :, self.back]
        return self.pair(p, 1, src, self.l1b.at[p], self.at.across_y)

    def y_two(self, p):
        return self.pair(p, 2, self.l1a.at[p, :, 1 - self.at.y], self.l2.at[p, :, :, self.front], self.at.across_y)

    def x_two(self, p):
        return self.pair(p, 3, self.l1b.at[p, :, self.theirs], self.l2.at[p, :, :, self.back], self.at.across_x)

    def z_copy(self, p, k):
        return self.pair(p, 3 + k, self.l2.at[p, self.at.zs[k]], self.l3.at[p, k - 1], self.at.along_z[k])

    def x_back(self, p, x=None):
        piece = self.la.at[p, self.at.core, pl.ds(pl.multiple_of((self.at.x if x is None else x) * 16, 16), 16)]
        return self.pair(p, 7, piece, piece, self.at.across_x)

    def core_back(self, p, core=None):
        piece = self.la.at[p, self.at.core if core is None else core]
        return self.pair(p, 8, piece, piece, self.at.across_core)

    def store(self, p, dsts):
        for core, dst in enumerate(dsts):
            pltpu.make_async_copy(self.la.at[p, core], dst, self.osem.at[p, core]).start()

    def store_all(self, p):
        project, output, up, down = self.outs[:4]
        b, h = p // 2, p % 2

        def rows(core, first=0):
            return pl.ds(pl.multiple_of(first + core * 64 + h * 32, 32), 32)

        def cols(j):
            return pl.ds(pl.multiple_of(j * 1024, 1024), 1024)

        pl.when(b < 4)(lambda: self.store(p, [down.at[rows(c, b * 128)] for c in range(2)]))
        pl.when(jnp.logical_and(b >= 4, b < 8))(lambda: self.store(p, [up.at[rows(c), cols(b - 4)] for c in range(2)]))
        pl.when(b == 8)(lambda: self.store(p, [output.at[rows(c)] for c in range(2)]))
        pl.when(jnp.logical_and(b >= 9, b < 12))(lambda: self.store(p, [project.at[rows(c), cols(b - 9)] for c in range(2)]))

    lags = (4, 6, 10, 11)

    def drain(self, d):
        at, lags = self.at, self.lags

        @pl.when(d < PARTS)
        def _():
            p = d
            self.x_one(p).wait()

            self.l1a[p] = self.l1a[p] + self.s0[p % RING, :, :, self.mine, self.front]
            self.y_two(p).start()
            self.y_one(p).wait()
            self.l1b[p] = self.l1b[p] + self.s0[p % RING, :, at.y, :, self.back]
            self.x_two(p).start()

        @pl.when(jnp.logical_and(d >= lags[0], d < PARTS + lags[0]))
        def _():
            p = d - lags[0]
            self.y_two(p).wait()
            self.x_two(p).wait()

            self.l2[p, :, :, self.front] = self.l2[p, :, :, self.front] + self.l1a[p, :, at.y]
            self.l2[p, :, :, self.back] = self.l2[p, :, :, self.back] + self.l1b[p, :, self.mine]
            for k in range(1, 4):
                self.z_copy(p, k).start()

        @pl.when(jnp.logical_and(d >= lags[1], d < PARTS + lags[1]))
        def _():
            p = d - lags[1]
            total = self.l2[p, at.z].astype(WIDE)
            for k in range(1, 4):
                self.z_copy(p, k).wait()
            for k in range(3):
                total = total + self.l3[p, k].astype(WIDE)
            self.la[p, at.core, self.mine] = total.astype(LOW)
            self.x_back(p).start()

        @pl.when(jnp.logical_and(d >= lags[2], d < PARTS + lags[2]))
        def _():
            p = d - lags[2]
            self.x_back(p, 1 - at.x).wait_recv()
            self.core_back(p).start()

        @pl.when(jnp.logical_and(d >= lags[3], d < PARTS + lags[3]))
        def _():
            p = d - lags[3]
            self.x_back(p).wait_send()
            self.core_back(p).wait_send()
            self.core_back(p, 1 - at.core).wait_recv()
            self.store_all(p)

    drains = PARTS + lags[3]

    def run(self, lo, hi):
        def one(d, carry):
            self.drain(d)
            return carry

        lax.fori_loop(lo, hi, one, 0)

    def end(self):
        for b in range(READY - 2):
            self.core_copy(b).wait_send()
        self.core_copy(REDUCED - 2).wait_send()
        self.core_copy(REDUCED - 1).wait_send()

        def stored(p):
            for core in range(2):
                pltpu.make_async_copy(self.la.at[p, core], self.outs[1].at[pl.ds(0, 32)], self.osem.at[p, core]).wait()

        for_each(PARTS, stored)


REDUCE_SCRATCH = [
    pltpu.VMEM((2, 4, 2, 2, 32, 1024), LOW),
    pltpu.VMEM((RING, 4, 2, 32, 1024), LOW),
    pltpu.VMEM((PARTS, 4, 2, 16, FRONT), LOW),
    pltpu.VMEM((PARTS, 4, 32, 1024 - FRONT), LOW),
    pltpu.VMEM((PARTS, 4, 16, 1024), LOW),
    pltpu.VMEM((PARTS, 3, 16, 1024), LOW),
    pltpu.VMEM((PARTS, 2, 32, 1024), LOW),
    pltpu.SemaphoreType.DMA((REDUCED,)),
    pltpu.SemaphoreType.DMA((REDUCED,)),
    pltpu.SemaphoreType.DMA((4,)),
    pltpu.SemaphoreType.DMA((PARTS, 9)),
    pltpu.SemaphoreType.DMA((PARTS, 9)),
    pltpu.SemaphoreType.DMA((PARTS, 2)),
]


class TimeSums:
    def __init__(self, at, feat, outs, featg, sumg, part, core_in, x_in, final, send, recv, sems):
        self.at, self.outs, self.feat = at, outs, feat
        self.featg, self.sumg, self.part, self.core_in, self.x_in, self.final = featg, sumg, part, core_in, x_in, final
        self.send, self.recv, self.sems = send, recv, sems
        self.half = pl.ds(pl.multiple_of(at.core * 64, 64), 64)
        self.rows = sumg.shape[1] // 2

    def feat_copy(self, i):
        src = self.feat.at[:, pl.ds(pl.multiple_of(self.at.shards[i] * 128, 128), 128)]
        return remote(src, self.featg.at[i], self.send.at[i], self.recv.at[i], self.at.group[i])

    def begin(self):
        for i in range(7):
            self.feat_copy(i).start()
        self.featg[7] = self.feat[:, pl.ds(pl.multiple_of(self.at.f * 128, 128), 128)]

    def sum_copy(self, norm, i):
        rows = pl.ds(norm * self.rows, self.rows)
        sem = 7 + 7 * norm + i
        return remote(
            self.sumg.at[7, rows], self.sumg.at[i, rows], self.send.at[sem], self.recv.at[sem], self.at.group[i]
        )

    def share(self, norm, sums):
        rows = slice(norm * self.rows, (norm + 1) * self.rows)
        self.sumg[7, rows, :] = sums[rows, :].astype(LOW)
        for i in range(7):
            self.sum_copy(norm, i).start()

    def core_copy(self):
        src = self.part.at[pl.ds(pl.multiple_of((1 - self.at.core) * 64, 64), 64)]
        return remote(src, self.core_in, self.send.at[21], self.recv.at[21], self.at.across_core)

    def quarter(self, x):
        return pl.ds(pl.multiple_of(self.at.core * 64 + x * 32, 32), 32)

    def x_copy(self):
        src = self.part.at[self.quarter(1 - self.at.x)]
        return remote(src, self.x_in, self.send.at[22], self.recv.at[22], self.at.across_x)

    def x_back(self, x):
        piece = self.final.at[self.quarter(x)]
        return remote(piece, piece, self.send.at[23], self.recv.at[23], self.at.across_x)

    def core_back(self, core):
        piece = self.final.at[pl.ds(pl.multiple_of(core * 64, 64), 64)]
        return remote(piece, piece, self.send.at[24], self.recv.at[24], self.at.across_core)

    def combine(self):
        for i in range(7):
            self.feat_copy(i).wait()
            for norm in range(2):
                self.sum_copy(norm, i).wait()
        rows = 8 * self.sumg.shape[1]
        for h in range(2):
            cols = slice(h * HALF, (h + 1) * HALF)
            terms = self.sumg[:, :, cols].reshape(rows, HALF)
            total = lax.dot_general(self.featg[...].reshape(rows, 128), terms, TN, preferred_element_type=WIDE)
            self.part[:, cols] = total.astype(LOW)
        self.core_copy().start()

    def cross(self):
        self.core_copy().wait()
        self.part[self.half, :] = self.part[self.half, :] + self.core_in[...]
        self.x_copy().start()

    def finish(self):
        at = self.at
        self.x_copy().wait()
        mine = self.quarter(at.x)
        self.final[mine, :] = self.part[mine, :] + self.x_in[...]
        self.x_back(at.x).start()

    def give(self):
        at = self.at
        self.x_back(at.x).wait_send()
        self.x_back(1 - at.x).wait_recv()
        self.core_back(at.core).start()

    def end(self):
        at = self.at
        self.core_back(at.core).wait_send()
        self.core_back(1 - at.core).wait_recv()
        copies = [
            pltpu.make_async_copy(
                self.final.at[pl.ds(64 * n + 32 * h, 32)], self.outs[n].at[:, pl.ds(1024 * h, 1024)], self.sems.at[2 * n + h]
            )
            for n in range(2)
            for h in range(2)
        ]
        for copy in copies:
            copy.start()
        for copy in copies:
            copy.wait()


def sum_vectors(at, parts, got, sums, out, send, recv):
    def part(i):
        return remote(parts.at[at.shards[i]], got.at[i], send.at[i], recv.at[i], at.group[i])

    reps = [at.across_x, at.across_core, at.diagonal]

    def rest(i):
        return remote(sums.at[3], sums.at[i], send.at[7 + i], recv.at[7 + i], reps[i])

    def start():
        for i in range(7):
            part(i).start()

    def middle():
        total = parts[at.f]
        for i in range(7):
            part(i).wait()
            total = total + got[i]
        sums[3] = total
        for i in range(3):
            rest(i).start()

    def end():
        total = sums[3]
        for i in range(3):
            rest(i).wait()
            total = total + sums[i]
        out[...] = total

    return start, middle, end


COT, NORMED2, PAIR, GRAD_UP, TOKENS, NORMED1 = 0, 1, 2, 4, 8, 9
QUERY, KEY, VALUE, GRAD_CONTEXT, GRAD_BRANCH, CONTEXT = 2, 3, 4, 5, 10, 11
LAST = (5, 6, 7, 1)


def backward_kernel(comm, seqs, *refs):
    refs = list(refs)
    take = lambda n: [refs.pop(0) for _ in range(n)]
    full, cot_h, activ_h, slope_h, normed1_h, normed2_h, mid_h, q_h, k_h, v_h, ctx_h, probs_h, tokens_h, ready = take(14)
    table, mods, feat, cosine, sine = take(5)
    outs = take(6 if comm else 1)
    vec_out, input_o, layer_o = take(3)
    if comm:
        own, l0 = take(2)
    else:
        (out,) = outs
    pool, gn, mid, weights, slots, shares, sums, gtab, sem_in, sem_pair, sem_w, sem_mid, sem_slot, sem_share, sem_out = take(15)
    if comm:
        parts, vgot, vsums, vsend, vrecv = take(5)
        time_scratch = take(9)
        red = Reduce(ready, slots, own, l0, outs, *refs)
    tokens_n = pool.shape[1]
    per = tokens_n // seqs

    def fetch(src, i):
        return pltpu.make_async_copy(src, pool.at[i], sem_in.at[i])

    def fetch_slope(j):
        return pltpu.make_async_copy(slope_h.at[j], pool.at[PAIR + j % 2], sem_pair.at[j % 2])

    def fetch_share(n):
        return pltpu.make_async_copy(probs_h.at[n], shares.at[n % 2], sem_share.at[n % 2])

    def fetch_w(c, slot):
        return pltpu.make_async_copy(full.at[c], weights.at[slot], sem_w.at[slot])

    mid_in = pltpu.make_async_copy(mid_h, mid, sem_mid)
    fetch(cot_h, COT).start()
    fetch_slope(0).start()
    fetch_slope(1).start()
    fetch(normed2_h, NORMED2).start()
    fetch_w(9, 0).start()
    fetch_w(10, 1).start()
    mid_in.start()
    for src, i in ((tokens_h, TOKENS), (normed1_h, NORMED1), (ctx_h, CONTEXT)):
        fetch(src, i).start()
    if comm:
        red.begin()
        time_sums = TimeSums(red.at, feat, outs[4:], *time_scratch)
        time_sums.begin()
        run, load, feed = red.run, red.load, red.feed
    else:
        run = load = feed = lambda *a: None
    when = pl.when if comm else (lambda cond: lambda body: None)

    half_cols = lambda h: slice(h * HALF, (h + 1) * HALF)

    def half_rows(slot, h):
        if comm:
            return weights[slot, 2 * h : 2 * h + 2].reshape(HALF, 1024)
        return weights[slot, half_cols(h), :]

    def produce(b, lhs, rhs_of):
        if comm:
            red.free(b)
        else:
            pl.when(b >= READY + 2)(
                lambda: pltpu.make_async_copy(slots.at[b % 2], out.at[b - READY - 2], sem_slot.at[b % 2]).wait()
            )
        for h in range(2):
            block = rhs_of(lhs, h).astype(LOW)
            if comm:
                slots[b % 2, :, :, :, :, :, half_cols(h)] = block.reshape(4, 2, 2, 2, 32, HALF)
            else:
                slots[b % 2, :, half_cols(h)] = block
        if comm:
            red.produced(b)
        else:
            pltpu.make_async_copy(slots.at[b % 2], out.at[b - READY], sem_slot.at[b % 2]).start()

    def times(i):
        return lambda lhs, h: lax.dot_general(lhs[...], pool[i, :, half_cols(h)], TN, preferred_element_type=WIDE)

    ones = jnp.ones((8, tokens_n), LOW)

    def column_sums(i, row):
        gtab[pl.ds(row, 1), :] = jnp.dot(ones, pool[i], preferred_element_type=WIDE)[:1]

    def up(j):
        produce(4 + j, pool.at[NORMED2], times(GRAD_UP + j))

    fetch(cot_h, COT).wait()
    load(0)
    feed(0)
    column_sums(COT, BIAS_D)

    def activ_back(j):
        fetch_slope(j).wait()
        fetch_w(9 + j, j % 2).wait()
        for h in range(2):
            grad = lax.dot_general(pool[COT], half_rows(j % 2, h), NT, preferred_element_type=WIDE)
            grad = (grad * pool[PAIR + j % 2, :, half_cols(h)].astype(WIDE)).astype(LOW)
            for n in range(4):
                f = 4 * h + n
                place = pl.ds(pl.multiple_of((f % 2 * 4 + j) * 128, 128), 128)
                pool[GRAD_UP + f // 2, :, place] = grad[:, n * 128 : (n + 1) * 128]

        pl.when(j < 2)(lambda: fetch_w(11 + j, j % 2).start())
        pl.when(j >= 2)(lambda: fetch_w(3 + j, j % 2).start())
        pl.when(j < 2)(lambda: fetch_slope(j + 2).start())
        when(j >= 1)(lambda: feed(j))
        when(j == 0)(lambda: load(1))
        when(j == 1)(lambda: load(2))
        when(j == 2)(lambda: load(3))
        when(j >= 1)(lambda: run(j - 1, j))

    for_each(4, activ_back)
    fetch(q_h, QUERY).start()
    fetch(k_h, KEY).start()
    fetch(normed2_h, NORMED2).wait()

    def up_back(j):
        fetch_w(5 + j, j % 2).wait()
        for h in range(2):
            more = lax.dot_general(pool[GRAD_UP + j], half_rows(j % 2, h), NT, preferred_element_type=WIDE)

            @pl.when(j == 0)
            def _():
                gn[:, half_cols(h)] = more

            @pl.when(j > 0)
            def _():
                gn[:, half_cols(h)] = gn[:, half_cols(h)] + more

        pl.when(j < 2)(lambda: fetch_w(7 + j, j % 2).start())
        pl.when(j == 2)(lambda: fetch_w(4, 0).start())
        pl.when(j == 3)(lambda: fetch_w(1, 1).start())
        column_sums(GRAD_UP + j, BIAS_U + j)
        when(j == 2)(lambda: load(4))
        when(j == 3)(lambda: feed(4))
        pl.when(j % 2 == 1)(lambda: up(j // 2))
        when(j % 2 == 0)(lambda: run(3 + j // 2, 4 + j // 2))

    for_each(4, up_back)
    fetch(v_h, VALUE).start()
    fetch_share(0).start()
    fetch_share(1).start()

    sums[...] = jnp.zeros_like(sums)

    def norm_back(which, gain, value_of, done):
        def body(i):
            rows = rows_at(i)
            s = i // (per // TILE)
            at_scale, at_shift = part_of(which, 0, seqs) + s, part_of(which, 1, seqs) + s
            scale = table[gain : gain + 1, :] + row_of(mods, at_scale)
            normed, inverse = normalise(value_of(rows).astype(WIDE))
            grad = gn[rows, :]
            sums[pl.ds(at_scale, 1), :] += jnp.sum(grad * normed, axis=0, keepdims=True)
            sums[pl.ds(at_shift, 1), :] += jnp.sum(grad, axis=0, keepdims=True)
            hat = grad * scale
            done(rows, inverse * (hat - lane_mean(hat) - normed * lane_mean(hat * normed)))

        for_each(tokens_n // TILE, body)
        for n in range(2):
            at = part_of(which, n, seqs)
            gtab[gain + n : gain + n + 1, :] = jnp.sum(sums[at : at + seqs, :], axis=0, keepdims=True)
        if comm:
            time_sums.share(which, sums)

    mid_in.wait()

    def done2(rows, grad):
        total = pool[COT, rows, :].astype(WIDE) + grad
        mid[rows, :] = total
        pool[GRAD_BRANCH, rows, :] = total.astype(LOW)

    norm_back(1, GAIN2, lambda rows: mid[rows, :], done2)
    load(5)
    run(5, 7)

    column_sums(GRAD_BRANCH, BIAS_O)
    fetch_w(4, 0).wait()
    for h in range(2):
        grad = lax.dot_general(pool[GRAD_BRANCH], half_rows(0, h), NT, preferred_element_type=WIDE)
        pool[GRAD_CONTEXT, :, half_cols(h)] = grad.astype(LOW)
    fetch_w(2, 0).start()
    feed(5)
    up(2)
    run(7, 8)
    for src, i in ((q_h, QUERY), (k_h, KEY), (v_h, VALUE), (ctx_h, CONTEXT), (tokens_h, TOKENS), (normed1_h, NORMED1)):
        fetch(src, i).wait()

    lane = lax.broadcasted_iota(jnp.int32, (1, 128), 1)
    first_head = (lane < 64).astype(WIDE)
    second_head = 1.0 - first_head

    def split(v):
        return jnp.concatenate([v * first_head.astype(LOW), v * second_head.astype(LOW)], axis=0)

    def unturned(v):
        return v * cosine[...] - swapped(v) * sine[...]

    def heads(n):
        cols = pl.ds(pl.multiple_of(n * 128, 128), 128)
        fetch_share(n).wait()
        for s in range(seqs):
            rows = slice(s * per, (s + 1) * per)
            keys = pool[KEY, rows, cols]
            both = split(pool[QUERY, rows, cols])
            grads = split(pool[GRAD_CONTEXT, rows, cols])
            share = shares[n % 2, 2 * s * per : 2 * (s + 1) * per, :]
            probs = share.astype(WIDE)
            grad_probs = lax.dot_general(grads, pool[VALUE, rows, cols], NT, preferred_element_type=WIDE)
            inner = jnp.sum(grad_probs * probs, axis=-1, keepdims=True)
            grad_scores = (probs * (grad_probs - inner)).astype(LOW)
            grad_v = lax.dot_general(share, grads, TN, preferred_element_type=WIDE)
            grad_k = lax.dot_general(grad_scores, both, TN, preferred_element_type=WIDE)
            grad_q = jnp.dot(grad_scores, keys, preferred_element_type=WIDE)
            grad_q = (grad_q[:per] * first_head + grad_q[per:] * second_head) * 0.125
            pool[QUERY, rows, cols] = unturned(grad_q).astype(LOW)
            pool[KEY, rows, cols] = unturned(grad_k).astype(LOW)
            pool[VALUE, rows, cols] = grad_v.astype(LOW)

        pl.when(n < 6)(lambda: fetch_share(n + 2).start())
        when(n % 3 == 0)(lambda: load(6 + n // 3))
        when(jnp.logical_and(n % 3 == 1, n < 7))(lambda: feed(6 + n // 3))
        when(n == 7)(lambda: feed(8))

        @pl.when(jnp.logical_or(n == 2, n == 5))
        def _():
            lhs = jnp.where(n == 2, NORMED2, CONTEXT)
            rhs = jnp.where(n == 2, GRAD_UP + 3, GRAD_BRANCH)
            produce(6 + (n + 1) // 3, pool.at[lhs], times(rhs))

        done = 8 + n - (n + 2) // 3
        when(n % 3 != 0)(lambda: run(done, done + 1))

    for_each(8, heads)
    for j, i in enumerate(LAST):
        fetch(activ_h.at[j], i).start()

    def project(j):
        column_sums(QUERY + j, BIAS_P + j)
        when(j == 2)(lambda: feed(9))
        produce(9 + j, pool.at[NORMED1], times(QUERY + j))
        when(j >= 1)(lambda: load(8 + j))
        run(13 + j, 14 + j)

    for_each(3, project)

    def project_back(j):
        slot = (1 + j) % 2
        fetch_w(1 + j, slot).wait()
        for h in range(2):
            more = lax.dot_general(pool[QUERY + j], half_rows(slot, h), NT, preferred_element_type=WIDE)

            @pl.when(j == 0)
            def _():
                gn[:, half_cols(h)] = more

            @pl.when(j > 0)
            def _():
                gn[:, half_cols(h)] = gn[:, half_cols(h)] + more

        pl.when(j == 0)(lambda: fetch_w(3, 1).start())
        pl.when(j >= 1)(lambda: fetch_w(8 + j, (j + 1) % 2).start())
        when(j < 2)(lambda: feed(10 + j))
        when(j == 0)(lambda: load(11))
        when(j < 2)(lambda: run(16 + j, 17 + j))

    for_each(3, project_back)

    def done1(rows, grad):
        mid[rows, :] = mid[rows, :] + grad

    norm_back(0, GAIN1, lambda rows: pool[TOKENS, rows, :], done1)
    input_copy = pltpu.make_async_copy(mid, input_o, sem_mid)
    input_copy.start()
    middle_in = pltpu.make_async_copy(mid_h, gn, sem_out.at[0])
    middle_in.start()
    run(18, 20)
    if comm:
        for f in range(8):
            for row in range(13):
                r, b = vector_spot(row, f)
                parts[f, row : row + 1, :] = gtab[r : r + 1, b * 128 : (b + 1) * 128]
            parts[f, 13:16, :] = jnp.zeros((3, 128), WIDE)
        start, middle, end = sum_vectors(red.at, parts, vgot, vsums, vec_out, vsend, vrecv)
        start()
    else:
        vec_out[...] = gtab[...]

    def outer(lhs, h):
        terms = sums[:, half_cols(h)]
        high = terms.astype(LOW)
        rest = (terms - high.astype(WIDE)).astype(LOW)
        return lax.dot_general(lhs[...], high, TN, preferred_element_type=WIDE) + lax.dot_general(
            lhs[...], rest, TN, preferred_element_type=WIDE
        )

    if not comm:
        produce(12, feat, outer)

    middle_in.wait()
    for j, i in enumerate(LAST):
        run(20 + 2 * j, 22 + 2 * j)
        fetch(activ_h.at[j], i).wait()
        fetch_w(9 + j, j % 2).wait()
        for h in range(2):
            cols = half_cols(h)
            w = weights[j % 2, ..., cols].reshape(1024, HALF) if comm else weights[j % 2, :, cols]
            total = gn[:, cols] + jnp.dot(pool[i], w, preferred_element_type=WIDE)
            if j < 3:
                gn[:, cols] = total
            else:
                pool[COT, :, cols] = (total + table[BIAS_D : BIAS_D + 1, cols]).astype(LOW)
        if j < 2:
            fetch_w(11 + j, j % 2).start()
        if comm and j >= 1:
            (time_sums.combine, time_sums.cross, time_sums.finish)[j - 1]()
    layer_copy = pltpu.make_async_copy(pool.at[COT], layer_o, sem_out.at[1])
    layer_copy.start()
    if comm:
        middle()
        time_sums.give()
        end()
        run(28, red.drains)
        time_sums.end()
        red.end()
    else:
        for b in (11, 12):
            pltpu.make_async_copy(slots.at[b % 2], out.at[b - READY], sem_slot.at[b % 2]).wait()
    input_copy.wait()
    layer_copy.wait()


def backward_call(comm, full, cot, saved, tokens, table, mods, feat, cosine, sine, seqs):
    n, width = tokens.shape
    vmem, hbm = pl.BlockSpec(memory_space=pltpu.VMEM), pl.BlockSpec(memory_space=pl.ANY)
    ready, q, k, v, ctx, mid, normed1, normed2, activ, slope, probs = saved
    block = (4, 2, 2, 2, 32, width) if comm else (width, width)
    rows = width // 8
    if comm:
        shapes = [(rows, 3 * width), (rows, width), (rows, 4 * width), (4 * rows, width), (TE // 8, 2 * width), (TE // 8, 2 * width)]
    else:
        shapes = [(BLOCKS - READY, width, width)]
    outs = [(jax.ShapeDtypeStruct(shape, LOW), hbm) for shape in shapes] + [
        (jax.ShapeDtypeStruct((16, 128) if comm else (16, width), WIDE), vmem),
        (jax.ShapeDtypeStruct((n, width), WIDE), hbm),
        (jax.ShapeDtypeStruct((n, width), LOW), hbm),
    ]
    extra = []
    if comm:
        part = lambda count: (jax.ShapeDtypeStruct((count, 4, 2, 2, 32, width), LOW), hbm)
        outs += [part(REDUCED - READY), part(REDUCED)]
        extra = [
            pltpu.VMEM((8, 16, 128), WIDE),
            pltpu.VMEM((7, 16, 128), WIDE),
            pltpu.VMEM((4, 16, 128), WIDE),
            pltpu.SemaphoreType.DMA((10,)),
            pltpu.SemaphoreType.DMA((10,)),
            pltpu.VMEM((8, feat.shape[0], 128), LOW),
            pltpu.VMEM((8, feat.shape[0], width), LOW),
            pltpu.VMEM((128, width), LOW),
            pltpu.VMEM((64, width), LOW),
            pltpu.VMEM((32, width), LOW),
            pltpu.VMEM((128, width), LOW),
            pltpu.SemaphoreType.DMA((25,)),
            pltpu.SemaphoreType.DMA((25,)),
            pltpu.SemaphoreType.DMA((4,)),
        ] + REDUCE_SCRATCH
        full = full.reshape((BLOCKS,) + block)
    got = pl.pallas_call(
        functools.partial(backward_kernel, comm, seqs),
        out_shape=tuple(s for s, _ in outs),
        in_specs=[hbm] * 14 + [vmem] * 5,
        out_specs=tuple(m for _, m in outs),
        scratch_shapes=[
            pltpu.VMEM((12, n, width), LOW),
            pltpu.VMEM((n, width), WIDE),
            pltpu.VMEM((n, width), WIDE),
            pltpu.VMEM((2,) + block, LOW),
            pltpu.VMEM((2,) + block, LOW),
            pltpu.VMEM((2,) + probs.shape[1:], LOW),
            pltpu.VMEM((feat.shape[0], width), WIDE),
            pltpu.VMEM((16, width), WIDE),
            pltpu.SemaphoreType.DMA((12,)),
            pltpu.SemaphoreType.DMA((2,)),
            pltpu.SemaphoreType.DMA((2,)),
            pltpu.SemaphoreType.DMA,
            pltpu.SemaphoreType.DMA((2,)),
            pltpu.SemaphoreType.DMA((2,)),
            pltpu.SemaphoreType.DMA((2,)),
        ]
        + extra,
        compiler_params=pltpu.CompilerParams(
            collective_id=1 if comm else None, has_side_effects=comm, vmem_limit_bytes=62 * 2**20
        ),
        name="backward",
    )(full, cot, activ, slope, normed1, normed2, mid, q, k, v, ctx, probs, tokens, ready, table, mods, feat, cosine, sine)
    return got[: len(shapes) + 3]


def widen(arrays, vec, sizes):
    count = len(arrays)

    def kernel(vec_in, *refs):
        srcs, dsts, lines = refs[:count], refs[count : 2 * count], refs[2 * count : 2 * count + len(sizes)]
        rest = refs[2 * count + len(sizes) :]
        lows, wides, sems = rest[:count], rest[count : 2 * count], rest[-1]
        ins = [pltpu.make_async_copy(s, v, sems.at[i]) for i, (s, v) in enumerate(zip(srcs, lows))]
        outs = [pltpu.make_async_copy(v, d, sems.at[i]) for i, (v, d) in enumerate(zip(wides, dsts))]
        for copy in ins:
            copy.start()
        row = 0
        for line, size in zip(lines, sizes):
            for k in range(size // 128):
                line[pl.ds(128 * k, 128)] = vec_in[row, :]
                row += 1
        for i in range(count):
            ins[i].wait()

            def body(n, i=i):
                at = pl.ds(pl.multiple_of(n * 16, 16), 16)
                wides[i][at, :] = lows[i][at, :].astype(WIDE)

            for_each(lows[i].shape[0] // 16, body)
            outs[i].start()
        for copy in outs:
            copy.wait()

    hbm, vmem = pl.BlockSpec(memory_space=pl.ANY), pl.BlockSpec(memory_space=pltpu.VMEM)
    got = pl.pallas_call(
        kernel,
        out_shape=tuple(jax.ShapeDtypeStruct(a.shape, WIDE) for a in arrays)
        + tuple(jax.ShapeDtypeStruct((size,), WIDE) for size in sizes),
        in_specs=[vmem] + [hbm] * count,
        out_specs=(hbm,) * count + (vmem,) * len(sizes),
        scratch_shapes=[pltpu.VMEM(a.shape, LOW) for a in arrays]
        + [pltpu.VMEM(a.shape, WIDE) for a in arrays]
        + [pltpu.SemaphoreType.DMA((count,))],
        compiler_params=pltpu.CompilerParams(vmem_limit_bytes=60 * 2**20),
        name="widen",
    )(vec, *arrays)
    return got[:count], got[count:]


def rotary_constants(length, head_dim):
    half_width = head_dim // 2
    inverse = np.exp(np.arange(half_width, dtype=np.float32) * np.float32(-math.log(10000.0) / half_width))
    angles = np.arange(length, dtype=np.float32)[:, None] * inverse[None, :]
    cosine, sine = np.cos(angles), np.sin(angles)
    pair = np.concatenate([cosine, cosine], axis=1), np.concatenate([-sine, sine], axis=1)
    return tuple(np.concatenate([t, t], axis=1).astype(np.float32) for t in pair)


def wide_features(noise_times, width):
    seqs = noise_times.shape[0]
    half_width = TE // 2
    column = np.arange(width)
    feature = column // 128 * 32 + column % 32
    rates = np.exp((feature % half_width).astype(np.float32) * np.float32(math.log(100.0) / half_width))
    each = part_of(1, 0, seqs)
    row = np.arange(2 * each)
    part = np.where(row % each < 2 * seqs, row // each * 2 + row % each // seqs, -1)
    mine = row[:, None] % each % seqs == np.arange(seqs)[None, :]
    times = jnp.sum(jnp.where(mine, noise_times[None, :], 0.0), axis=1)
    phases = (jnp.log(times) * 0.25)[:, None] * rates[None, :]
    feat = jnp.where((feature < half_width)[None, :], jnp.sin(phases), jnp.cos(phases))
    return jnp.where((column // 32 % 4)[None, :] == part[:, None], feat, 0.0).astype(LOW)


def gather_plain(weights, vectors):
    project, output, up, down, time1, time2 = weights
    rows, width = output.shape
    each = time1.shape[0]
    columns = lambda w: w.reshape(rows, -1, width).transpose(1, 0, 2)
    times = jnp.stack([time1, time2]).reshape(2, each, 2, width).transpose(0, 2, 1, 3)
    own = jnp.concatenate(
        [times.reshape(1, rows, width), columns(project), output[None], columns(up), down.reshape(4, rows, width)]
    )
    full = lax.all_gather(own, "fsdp", axis=1, tiled=True)
    times = full[0].reshape(-1, 2, 2, each, width).transpose(1, 2, 0, 3, 4).reshape(2, 2, 8, 32, width)
    down = full[9:].reshape(4, -1, rows, width).transpose(1, 0, 2, 3).reshape(8, 4, 128, width)
    full = jnp.concatenate(
        [
            times.transpose(2, 0, 1, 3, 4).reshape(1, width, width),
            full[1:9],
            down.transpose(1, 0, 2, 3).reshape(4, width, width),
        ]
    )
    sizes = [v.shape[0] for v in vectors]
    whole = pieces_of(lax.all_gather(jnp.concatenate(vectors), "fsdp", axis=0), sizes)
    table = jnp.concatenate([w.reshape(-1, width) for w in whole]).astype(WIDE)
    return full, jnp.pad(table, ((0, 3), (0, 0)))


def reduce_plain(parts, table, sizes, shards_of):
    width = parts.shape[-1]
    rows, each = width // shards_of, TE // shards_of
    down = parts[:4].reshape(4, 8, 128, width).transpose(1, 0, 2, 3).reshape(shards_of, 4, rows, width)
    times = parts[12].reshape(8, 2, 2, 32, width).transpose(1, 2, 0, 3, 4).reshape(2, 2, shards_of, each, width)
    own = jnp.concatenate(
        [
            down.transpose(1, 0, 2, 3).reshape(4, width, width),
            parts[4:12],
            times.transpose(2, 0, 1, 3, 4).reshape(1, width, width),
        ]
    )
    mine = lax.psum(lax.psum_scatter(own, "fsdp", scatter_dimension=1, tiled=True), "rep")
    whole = pieces_of(table[:13].reshape(-1), [shards_of * size for size in sizes])
    vec = jnp.concatenate([w.reshape(shards_of, -1) for w in whole], axis=1)
    vec = lax.psum(lax.psum_scatter(vec, "fsdp", scatter_dimension=0, tiled=True)[0], "rep")
    columns = lambda w: w.transpose(1, 0, 2).reshape(rows, -1)
    times = mine[12].reshape(2, 2, each, width).transpose(0, 2, 1, 3).reshape(2, each, 2 * width)
    return columns(mine[9:12]), mine[8], columns(mine[4:8]), mine[:4].reshape(-1, width), times[0], times[1], vec


def pieces_of(flat, sizes):
    at, got = 0, []
    for size in sizes:
        got.append(flat[..., at : at + size])
        at += size
    return got


def shards(
    inputs,
    noise_times,
    cotangent,
    norm1_gain,
    norm1_bias,
    norm1_time,
    project_weight,
    project_bias,
    output_weight,
    output_bias,
    norm2_gain,
    norm2_bias,
    norm2_time,
    up_weight,
    up_bias,
    down_weight,
    down_bias,
):
    seqs = noise_times.shape[0]
    tokens_n, width = inputs.shape
    rows = output_weight.shape[0]
    shards_of = width // rows
    comm = shards_of == 8
    feat = wide_features(noise_times, width)
    cosine, sine = rotary_constants(tokens_n // seqs, width // HEADS)
    weights = (project_weight, output_weight, up_weight, down_weight, norm1_time, norm2_time)
    vectors = (norm1_gain, norm1_bias, project_bias, output_bias, norm2_gain, norm2_bias, up_bias, down_bias)
    sizes = [v.shape[0] for v in vectors]
    if comm:
        at, table = 0, jnp.zeros((16, 128), WIDE)
        for v in vectors:
            lines = v.astype(WIDE).reshape(-1, 128)
            table = table + jnp.pad(lines, ((at, 16 - at - lines.shape[0]), (0, 0)))
            at += lines.shape[0]
    else:
        full, table = gather_plain(weights, vectors)
        weights = (full,)
    full, table, mods, *saved = forward_call(
        comm, weights, table, inputs, cotangent, feat, cosine, sine, seqs
    )
    *sums, input_grad, layer_out = backward_call(comm, full, cotangent, saved, inputs, table, mods, feat, cosine, sine, seqs)
    if not comm:
        sums = reduce_plain(jnp.concatenate([saved[0], sums[0]]), sums[1], sizes, shards_of)
    if comm:
        wide, got = widen(sums[:6], sums[6], sizes)
    else:
        wide, got = [s.astype(WIDE) for s in sums[:6]], pieces_of(sums[6], sizes)
    project, output, up, down, time1, time2 = wide
    return (
        layer_out,
        input_grad,
        got[0],
        got[1],
        time1,
        project,
        got[2],
        output,
        got[3],
        got[4],
        got[5],
        time2,
        up,
        got[6],
        down,
        got[7],
    )


def solution(mesh):
    placed = (
        P(("rep", "fsdp"), None),
        P(("rep", "fsdp")),
        P(("rep", "fsdp"), None),
        P("fsdp"),
        P("fsdp"),
        P("fsdp", None),
        P("fsdp", None),
        P("fsdp"),
        P("fsdp", None),
        P("fsdp"),
        P("fsdp"),
        P("fsdp"),
        P("fsdp", None),
        P("fsdp", None),
        P("fsdp"),
        P("fsdp", None),
        P("fsdp"),
    )
    return jax.shard_map(
        shards,
        mesh=mesh,
        in_specs=placed,
        out_specs=(
            P(("rep", "fsdp"), None),
            P(("rep", "fsdp"), None),
            P("fsdp"),
            P("fsdp"),
            P("fsdp", None),
            P("fsdp", None),
            P("fsdp"),
            P("fsdp", None),
            P("fsdp"),
            P("fsdp"),
            P("fsdp"),
            P("fsdp", None),
            P("fsdp", None),
            P("fsdp"),
            P("fsdp", None),
            P("fsdp"),
        ),
        check_vma=False,
    )
```

```python
import functools
import math

import jax
import jax.numpy as jnp
import numpy as np
from jax import lax
from jax.experimental import pallas as pl
from jax.experimental.pallas import tpu as pltpu
from jax.sharding import PartitionSpec as P

HEADS = 16
TE = 256
epsilon = 1e-05


MESH = pl.DeviceIdType.MESH
LOW, WIDE = jnp.bfloat16, jnp.float32
FRONT = 384
BLOCKS = 13
PIECES = 2 * BLOCKS
NT = (((1,), (1,)), ((), ()))
TN = (((0,), (0,)), ((), ()))


class Place:
    def __init__(self):
        r, f = lax.axis_index("rep"), lax.axis_index("fsdp")
        self.r, self.f = r, f
        self.x, self.core = r // 2, r % 2
        self.z, self.y = f // 2, f % 2
        z = self.z
        self.zs = [z, z + 1 - 2 * (z % 2), (z + 2) % 4, 3 - z]
        self.same = [zk * 2 + self.y for zk in self.zs]
        self.other = [zk * 2 + 1 - self.y for zk in self.zs]
        self.across_x = ((1 - self.x) * 2 + self.core, f)
        self.across_y = (r, self.other[0])
        self.across_core = (self.x * 2 + 1 - self.core, f)
        self.diagonal = ((1 - self.x) * 2 + 1 - self.core, f)
        self.along_z = [(r, fk) for fk in self.same]
        self.shards = self.same[1:] + self.other
        self.group = [(r, fk) for fk in self.shards]


def greet(peers):
    barrier = pltpu.get_barrier_semaphore()
    for peer in peers:
        pl.semaphore_signal(barrier, inc=1, device_id=peer, device_id_type=MESH)
    pl.semaphore_wait(barrier, len(peers))


def remote(src, dst, send, recv, peer):
    return pltpu.make_async_remote_copy(
        src_ref=src, dst_ref=dst, send_sem=send, recv_sem=recv, device_id=peer, device_id_type=MESH
    )


class Gather:
    def __init__(self, own, vec, full, vecs, send, recv, vsend, vrecv, lsem):
        self.at = Place()
        self.own, self.full, self.send, self.recv, self.lsem = own, full, send, recv, lsem
        self.vec, self.vecs, self.vsend, self.vrecv = vec, vecs, vsend, vrecv
        x = self.at.x
        self.middle = jnp.logical_and(self.at.z >= 1, self.at.z <= 2)
        rest = 1024 - FRONT
        self.mine = pl.ds(pl.multiple_of(x * FRONT, 128), rest)
        self.xcols = pl.ds(pl.multiple_of(x * rest, 128), FRONT)
        self.xland = pl.ds(pl.multiple_of((1 - x) * rest, 128), FRONT)

    def spot(self, c, z, y, cols, core=None):
        core = self.at.core if core is None else core
        return self.full.at[c // 2, z, y, core, c % 2, :, cols]

    def pair(self, c, i, src, dst, peer):
        return remote(src, dst, self.send.at[c, i], self.recv.at[c, i], peer)

    def owned(self, c, cols):
        return self.own.at[c // 2, pl.ds(pl.multiple_of(self.at.core * 64 + c % 2 * 32, 32), 32), cols]

    def z_copy(self, c, k):
        at = self.at
        src = self.owned(c, self.mine)
        return self.pair(c, k - 1, src, self.spot(c, at.z, at.y, self.mine), at.along_z[k])

    def z_relay(self, c):
        dst = self.spot(c, self.at.zs[2], self.at.y, self.mine)
        return remote(dst, dst, self.send.at[c, 12], self.recv.at[c, 2], self.at.along_z[1])

    def z_land(self, c, k):
        dst = self.spot(c, self.at.zs[k], self.at.y, self.mine)
        return self.pair(c, k - 1, dst, dst, self.at.along_z[k])

    def y_copy(self, c, k):
        at = self.at
        dst = self.spot(c, at.zs[k], at.y, self.mine)
        src = self.owned(c, self.mine) if k == 0 else dst
        return self.pair(c, 3 + k, src, dst, at.across_y)

    def y_land(self, c, k):
        dst = self.spot(c, self.at.zs[k], 1 - self.at.y, self.mine)
        return self.pair(c, 3 + k, dst, dst, self.at.across_y)

    def x_place(self, c, k, cols):
        at = self.at
        if k < 3:
            return self.spot(c, at.zs[k + 1], at.y, cols)
        return self.spot(c, slice(None), 1 - at.y, cols)

    def x_copy(self, c, k):
        src = self.x_place(c, k, self.xcols)
        return self.pair(c, 7 + k, src, src, self.at.across_x)

    def x_land(self, c, k):
        dst = self.x_place(c, k, self.xland)
        return self.pair(c, 7 + k, dst, dst, self.at.across_x)

    def core_copy(self, c, core=None):
        part = self.spot(c, slice(None), slice(None), slice(None), core)
        return self.pair(c, 11, part, part, self.at.across_core)

    def local(self, c):
        at = self.at
        dst = self.spot(c, at.z, at.y, slice(None))
        return pltpu.make_async_copy(self.owned(c, slice(None)), dst, self.lsem.at[c])

    def first(self, c):
        for k in range(1, 3):
            self.z_copy(c, k).start()
        pl.when(self.middle)(lambda: self.z_copy(c, 3).start())
        self.y_copy(c, 0).start()
        self.local(c).start()

    ahead = 4

    def begin(self):
        at = self.at
        greet([at.across_core, at.across_x] + at.group)
        for i, peer in enumerate(at.group):
            remote(self.vec, self.vecs.at[at.f], self.vsend.at[i], self.vrecv.at[i], peer).start()

    def start(self):
        for c in range(self.ahead):
            self.first(c)

    def vectors(self):
        at = self.at
        self.vecs[at.f] = self.vec[...]
        for i, peer in enumerate(at.group):
            remote(self.vec, self.vecs.at[at.shards[i]], self.vsend.at[i], self.vrecv.at[i], peer).wait()

    lag_x, lag_core, lag_done = 2, 4, 5

    def step(self, t):
        lag_x, lag_core, lag_done = self.lag_x, self.lag_core, self.lag_done

        @pl.when(t + self.ahead < PIECES)
        def _():
            self.first(t + self.ahead)

        @pl.when(t < PIECES)
        def _():
            for k in (2, 1, 3):
                self.z_land(t, k).wait_recv()
                if k == 2:
                    pl.when(self.middle)(lambda: self.z_relay(t).start())
                self.y_copy(t, k).start()

        @pl.when(jnp.logical_and(t >= lag_x, t < PIECES + lag_x))
        def _():
            c = t - lag_x
            for k in range(4):
                if k == 3:
                    for j in range(4):
                        self.y_land(c, j).wait_recv()
                self.x_copy(c, k).start()

        @pl.when(jnp.logical_and(t >= lag_core, t < PIECES + lag_core))
        def _():
            c = t - lag_core
            self.local(c).wait()
            for k in range(4):
                self.x_land(c, k).wait_recv()
            self.core_copy(c).start()

        @pl.when(jnp.logical_and(t >= lag_done, t < PIECES + lag_done))
        def _():
            c = t - lag_done
            self.core_copy(c, 1 - self.at.core).wait_recv()
            for k in range(1, 3):
                self.z_copy(c, k).wait_send()

            @pl.when(self.middle)
            def _():
                self.z_copy(c, 3).wait_send()
                self.z_relay(c).wait_send()

            for k in range(4):
                self.y_copy(c, k).wait_send()
                self.x_copy(c, k).wait_send()
            self.core_copy(c).wait_send()

    steps = PIECES + lag_done

    def ready(self, block):
        return 2 * block + 2 + self.lag_done

    def run(self, lo, hi):
        def one(t, carry):
            self.step(t)
            return carry

        lax.fori_loop(lo, hi, one, 0)


GATHER_SCRATCH = [
    pltpu.VMEM((8, 16, 128), WIDE),
    pltpu.SemaphoreType.DMA((PIECES, 13)),
    pltpu.SemaphoreType.DMA((PIECES, 12)),
    pltpu.SemaphoreType.DMA((7,)),
    pltpu.SemaphoreType.DMA((7,)),
    pltpu.SemaphoreType.DMA((PIECES,)),
]


GAIN1, BIAS1, BIAS_P, BIAS_O, GAIN2, BIAS2, BIAS_U, BIAS_D = 0, 1, 2, 5, 6, 7, 8, 12
HALF = 512
TILE = 32


def vector_spot(row, f):
    for first, count in ((BIAS_P, 3), (BIAS_U, 4)):
        if first <= row < first + count:
            block = f * count + row - first
            return first + block // 8, block % 8
    return row, f


def for_each(count, body):
    def one(i, carry):
        body(i)
        return carry

    lax.fori_loop(0, count, one, 0)


def in_pairs(count, body):
    def two(i):
        body(2 * i)
        body(2 * i + 1)

    for_each(count // 2, two)
    if count % 2:
        body(count - 1)


def rows_at(i, size=TILE):
    return pl.ds(pl.multiple_of(i * size, size), size)


def lane_mean(v):
    return jnp.mean(v, axis=-1, keepdims=True)


def normalise(v):
    centred = v - lane_mean(v)
    inverse = lax.rsqrt(lane_mean(centred * centred) + epsilon)
    return centred * inverse, inverse


def row_of(ref, i):
    return ref[pl.ds(i, 1), :]


def part_of(norm, shift, seqs):
    return norm * (-(-2 * seqs // 16) * 16) + shift * seqs


def modulated(ref, out, table, mods, gain, which, seqs):
    per = ref.shape[0] // seqs // TILE

    def body(i):
        s = i // per
        scale = table[gain : gain + 1, :] + row_of(mods, part_of(which, 0, seqs) + s)
        shift = table[gain + 1 : gain + 2, :] + row_of(mods, part_of(which, 1, seqs) + s)
        rows = rows_at(i)
        normed, _ = normalise(ref[rows, :].astype(WIDE))
        out[rows, :] = (normed * scale + shift).astype(LOW)

    for_each(ref.shape[0] // TILE, body)


def swapped(v):
    lane = lax.broadcasted_iota(jnp.int32, v.shape, 1)
    return jnp.where(lane % 64 < 32, pltpu.roll(v, 96, 1), pltpu.roll(v, 32, 1))


def pack(local, own, sems):
    project, output, up, down, time1, time2 = local
    pairs = [(t.at[:, pl.ds(1024 * h, 1024)], own.at[0, pl.ds(64 * n + 32 * h, 32)]) for n, t in enumerate((time1, time2)) for h in range(2)]
    pairs += [(project.at[:, pl.ds(1024 * j, 1024)], own.at[1 + j]) for j in range(3)] + [(output, own.at[4])]
    pairs += [(up.at[:, pl.ds(1024 * j, 1024)], own.at[5 + j]) for j in range(4)]
    pairs += [(down.at[pl.ds(128 * j, 128)], own.at[9 + j]) for j in range(4)]
    return [pltpu.make_async_copy(src, dst, sems.at[i]) for i, (src, dst) in enumerate(pairs)]


def forward_kernel(comm, seqs, *refs):
    refs = list(refs)
    take = lambda n: [refs.pop(0) for _ in range(n)]
    if comm:
        local, vec = take(6), take(1)[0]
    else:
        full_in, table_in = take(2)
    tokens_hbm, cot_hbm, feat, cosine, sine = take(5)
    if comm:
        (full,) = take(1)
    else:
        full = full_in
    table, mods = take(2)
    grad_o, q_o, k_o, v_o, ctx_o, mid_o, normed1_o, normed2_o, activ_o, slope_o, probs_o = take(11)
    tokens, cot, weights, normed, normed2, q, k, v, ctx, mid, activ, slope, wide, probs, grads = take(15)
    sem_in, sem_w, sem_out, sem_grad = take(4)
    tokens_n = tokens.shape[0]
    per = tokens_n // seqs

    tokens_in = pltpu.make_async_copy(tokens_hbm, tokens, sem_in.at[0])
    tokens_in.start()
    cot_in = pltpu.make_async_copy(cot_hbm, cot, sem_in.at[1])
    cot_in.start()
    if comm:
        own, sem_own = take(2)
        gather = Gather(own, vec, full, *refs)
        packing = pack(local, own, sem_own)
        for copy in packing:
            copy.start()
        gather.begin()
        for copy in packing:
            copy.wait()
        gather.start()
        gather.vectors()
        for f in range(8):
            block = gather.vecs[f]
            for row in range(13):
                r, b = vector_spot(row, f)
                table[r : r + 1, b * 128 : (b + 1) * 128] = block[row : row + 1, :]
        run = gather.run
    else:
        table[...] = table_in[...]
        run = lambda lo, hi: None

    def fetch(c):
        return pltpu.make_async_copy(full.at[c], weights.at[c % 2], sem_w.at[c % 2])

    def arrive(c, lo, hi):
        run(lo, hi)
        fetch(c).start()

    def weight(c):
        fetch(c).wait()
        return weights.at[c % 2]

    ready = Gather.lag_done + 2
    flat = (lambda w: w[...].reshape(1024, 1024)) if comm else (lambda w: w[...])

    saves = []

    def save(src, dst):
        copy = pltpu.make_async_copy(src, dst, sem_out.at[len(saves)])
        copy.start()
        saves.append(copy)

    arrive(0, 0, ready)
    w = weight(0)
    mods[...] = jnp.dot(feat[...], flat(w), preferred_element_type=WIDE)
    tokens_in.wait()
    arrive(1, ready, ready + 2)
    modulated(tokens, normed, table, mods, GAIN1, 0, seqs)
    save(normed, normed1_o)

    for j, (dst, dst_o) in enumerate([(q, q_o), (k, k_o), (v, v_o)]):
        w = weight(1 + j)
        for h in range(2):
            cols = slice(h * HALF, (h + 1) * HALF)
            wide[...] = jnp.dot(normed[...], half_of(w, cols, comm), preferred_element_type=WIDE)
            if h == 1:
                run(ready + 2 + 2 * j, ready + 4 + 2 * j)
                fetch(2 + j).start()
            bias = table[BIAS_P + j : BIAS_P + j + 1, cols]

            def body(i, h=h, bias=bias, dst=dst, j=j):
                rows = rows_at(i)
                where = pl.ds(pl.multiple_of((i % (per // TILE)) * TILE, TILE), TILE)
                piece = wide[rows, :] + bias
                if j == 2:
                    dst[rows, h * HALF : (h + 1) * HALF] = piece.astype(LOW)
                    return
                for n in range(HALF // 128):
                    part = piece[:, n * 128 : (n + 1) * 128]
                    turned = part * cosine[where, :] + swapped(part) * sine[where, :]
                    if j == 0:
                        turned = turned * 0.125
                    at = h * HALF + n * 128
                    dst[rows, at : at + 128] = turned.astype(LOW)

            for_each(tokens_n // TILE, body)
        save(dst, dst_o)

    lane = lax.broadcasted_iota(jnp.int32, (1, 128), 1)
    first_head = (lane < 64).astype(WIDE)
    second_head = 1.0 - first_head

    def heads(n):
        cols = pl.ds(pl.multiple_of(n * 128, 128), 128)
        def one(s):
            rows = rows_at(s, per)
            qs = q[rows, cols]
            both = jnp.concatenate([qs * first_head.astype(LOW), qs * second_head.astype(LOW)], axis=0)
            scores = lax.dot_general(both, k[rows, cols], NT, preferred_element_type=WIDE)
            grown = jnp.exp(scores - jnp.max(scores, axis=-1, keepdims=True))
            share = (grown / jnp.sum(grown, axis=-1, keepdims=True)).astype(LOW)
            probs[n, rows_at(s, 2 * per), :] = share
            mixed = jnp.dot(share, v[rows, cols], preferred_element_type=WIDE)
            ctx[rows, cols] = (mixed[:per] * first_head + mixed[per:] * second_head).astype(LOW)
        in_pairs(seqs, one)
        if comm:
            pl.when(n >= 2)(lambda: gather.step(ready + 6 + n))

    for_each(8, heads)
    save(ctx, ctx_o)
    save(probs, probs_o)

    w = weight(4)
    for h in range(2):
        cols = slice(h * HALF, (h + 1) * HALF)
        dot = jnp.dot(ctx[...], half_of(w, cols, comm), preferred_element_type=WIDE)
        mid[:, cols] = tokens[:, cols].astype(WIDE) + (dot + table[BIAS_O : BIAS_O + 1, cols])
    arrive(5, ready + 14, ready + 15)
    save(mid, mid_o)
    modulated(mid, normed2, table, mods, GAIN2, 1, seqs)
    save(normed2, normed2_o)

    def up(j):
        w = weight(5 + j)
        for h in range(2):
            cols = slice(h * HALF, (h + 1) * HALF)
            wide[...] = jnp.dot(normed2[...], half_of(w, cols, comm), preferred_element_type=WIDE)
            if h == 1:
                once = ready + 15 + 2 * j - jnp.maximum(j - 2, 0)
                run(once, once + 1 + (j < 2).astype(jnp.int32))
                pl.when(j < 3)(lambda: fetch(6 + j).start())

            def body(i, h=h, cols=cols):
                rows = rows_at(i)
                u = wide[rows, :] + table[pl.ds(BIAS_U + j, 1), cols]
                phi = 0.5 + 0.5 * lax.erf(u * (0.5**0.5))
                bell = jnp.exp(-0.5 * (u * u)) * (1.0 / math.sqrt(2.0 * math.pi))
                result, grow = (u * phi).astype(LOW), (phi + u * bell).astype(LOW)
                place = pl.ds(pl.multiple_of((2 * j + h) * 128, 128), 128)
                for n in range(4):
                    activ[n, rows, place] = result[:, n * 128 : (n + 1) * 128]
                    slope[n, rows, place] = grow[:, n * 128 : (n + 1) * 128]

            for_each(tokens_n // TILE, body)

    for_each(4, up)
    save(activ, activ_o)
    save(slope, slope_o)

    cot_in.wait()

    def grad_copy(j):
        return pltpu.make_async_copy(grads.at[j % 2], grad_o.at[j], sem_grad.at[j % 2])

    def down(j):
        pl.when(j >= 2)(lambda: grad_copy(j - 2).wait())
        for h in range(2):
            cols = slice(h * HALF, (h + 1) * HALF)
            block = lax.dot_general(activ[j], cot[:, cols], TN, preferred_element_type=WIDE).astype(LOW)
            if comm:
                grads[j % 2, :, :, :, :, :, cols] = block.reshape(4, 2, 2, 2, 32, HALF)
            else:
                grads[j % 2, :, cols] = block
        grad_copy(j).start()
        if comm:
            pl.when(j < 3)(lambda: run(ready + 21 + j, ready + 22 + j))

    for_each(4, down)
    grad_copy(2).wait()
    grad_copy(3).wait()
    for copy in saves:
        copy.wait()


def half_of(w, cols, comm):
    if comm:
        return w[..., cols].reshape(1024, HALF)
    return w[:, cols]


def forward_call(comm, weights, vectors, tokens, cot, feat, cosine, sine, seqs):
    n, width = tokens.shape
    vmem, hbm = pl.BlockSpec(memory_space=pltpu.VMEM), pl.BlockSpec(memory_space=pl.ANY)
    low = jax.ShapeDtypeStruct((n, width), LOW)
    wide = jax.ShapeDtypeStruct((n, width), WIDE)
    shape4 = jax.ShapeDtypeStruct((4, n, width), LOW)
    block = (4, 2, 2, 2, 32, width) if comm else (width, width)
    outs = [
        (jax.ShapeDtypeStruct((16, width), WIDE), vmem),
        (jax.ShapeDtypeStruct((feat.shape[0], width), WIDE), vmem),
    ]
    share = (8, 2 * n, 128)
    saved = (jax.ShapeDtypeStruct((4,) + block, LOW), low, low, low, low, wide, low, low, shape4, shape4)
    outs += [(s, hbm) for s in saved + (jax.ShapeDtypeStruct(share, LOW),)]
    extra = []
    if comm:
        outs = [(jax.ShapeDtypeStruct((BLOCKS,) + block, LOW), hbm)] + outs
        extra = [pltpu.VMEM((BLOCKS, 128, width), LOW), pltpu.SemaphoreType.DMA((16,))] + GATHER_SCRATCH
    buffer = pltpu.VMEM((n, width), LOW)
    got = pl.pallas_call(
        functools.partial(forward_kernel, comm, seqs),
        out_shape=tuple(s for s, _ in outs),
        in_specs=[hbm] * len(weights) + [vmem, hbm, hbm, vmem, vmem, vmem],
        out_specs=tuple(m for _, m in outs),
        scratch_shapes=[
            buffer,
            buffer,
            pltpu.VMEM((2,) + block, LOW),
            buffer,
            buffer,
            buffer,
            buffer,
            buffer,
            buffer,
            pltpu.VMEM((n, width), WIDE),
            pltpu.VMEM((4, n, width), LOW),
            pltpu.VMEM((4, n, width), LOW),
            pltpu.VMEM((n, HALF), WIDE),
            pltpu.VMEM(share, LOW),
            pltpu.VMEM((2,) + block, LOW),
            pltpu.SemaphoreType.DMA((2,)),
            pltpu.SemaphoreType.DMA((2,)),
            pltpu.SemaphoreType.DMA((10,)),
            pltpu.SemaphoreType.DMA((2,)),
        ]
        + extra,
        compiler_params=pltpu.CompilerParams(
            collective_id=0 if comm else None, has_side_effects=comm, vmem_limit_bytes=60 * 2**20
        ),
        name="forward",
    )(*weights, vectors, tokens, cot, feat, cosine, sine)
    if not comm:
        return (weights[0], vectors) + tuple(got[1:])
    return (got[0].reshape(BLOCKS, width, width),) + tuple(got[1:])


RING = 10
REDUCED = 12
PARTS = 2 * REDUCED
READY = 4


class Reduce:
    def __init__(self, ready, slots, own, l0, outs, *scratch):
        self.at = Place()
        self.ready, self.slots, self.own, self.l0, self.outs = ready, slots, own, l0, outs
        (self.held, self.s0, self.l1a, self.l1b, self.l2, self.l3, self.la) = scratch[:7]
        (self.bsend, self.brecv, self.lsem, self.send, self.recv, self.osem) = scratch[7:13]
        x = self.at.x
        self.front, self.back = pl.ds(0, FRONT), pl.ds(FRONT, 1024 - FRONT)
        self.mine = pl.ds(pl.multiple_of(x * 16, 16), 16)
        self.theirs = pl.ds(pl.multiple_of((1 - x) * 16, 16), 16)

    def begin(self):
        at = self.at
        greet([at.across_core, at.across_x, at.diagonal] + at.group)
        for b in range(READY):
            src = self.ready.at[b, :, :, 1 - at.core]
            remote(src, self.l0.at[b], self.bsend.at[b], self.brecv.at[b], at.across_core).start()

    def core_copy(self, b):
        src = self.slots.at[b % 2, :, :, 1 - self.at.core]
        return remote(src, self.l0.at[b], self.bsend.at[b], self.brecv.at[b], self.at.across_core)

    def own_copy(self, b):
        return pltpu.make_async_copy(self.slots.at[b % 2, :, :, self.at.core], self.own.at[b - READY], self.lsem.at[b % 2])

    def loads(self, b, ready=False):
        src = self.ready.at[b, :, :, self.at.core] if ready else self.own.at[b - READY]
        return (
            pltpu.make_async_copy(src, self.held.at[0], self.lsem.at[2]),
            pltpu.make_async_copy(self.l0.at[b], self.held.at[1], self.lsem.at[3]),
        )

    def free(self, b):
        self.core_copy(b - 2).wait_send()

    def produced(self, b):
        self.core_copy(b).start()
        self.own_copy(b).start()

    def load(self, b):
        self.core_copy(b).wait_recv()
        if isinstance(b, int) and b < READY:
            for copy in self.loads(b, True):
                copy.start()
            return
        self.own_copy(b).wait()
        for copy in self.loads(b):
            copy.start()

    def feed(self, b):
        for copy in self.loads(READY):
            copy.wait()

        def add(z):
            for h in range(2):
                self.s0[(2 * b + h) % RING, z] = self.held[0, z, :, h] + self.held[1, z, :, h]

        for_each(4, add)
        for h in range(2):
            self.x_one(2 * b + h).start()
            self.y_one(2 * b + h).start()

    def pair(self, p, i, src, dst, peer):
        return remote(src, dst, self.send.at[p, i], self.recv.at[p, i], peer)

    def x_one(self, p):
        src = self.s0.at[p % RING, :, :, self.theirs, self.front]
        return self.pair(p, 0, src, self.l1a.at[p], self.at.across_x)

    def y_one(self, p):
        src = self.s0.at[p % RING, :, 1 - self.at.y, :, self.back]
        return self.pair(p, 1, src, self.l1b.at[p], self.at.across_y)

    def y_two(self, p):
        return self.pair(p, 2, self.l1a.at[p, :, 1 - self.at.y], self.l2.at[p, :, :, self.front], self.at.across_y)

    def x_two(self, p):
        return self.pair(p, 3, self.l1b.at[p, :, self.theirs], self.l2.at[p, :, :, self.back], self.at.across_x)

    def z_copy(self, p, k):
        return self.pair(p, 3 + k, self.l2.at[p, self.at.zs[k]], self.l3.at[p, k - 1], self.at.along_z[k])

    def x_back(self, p, x=None):
        piece = self.la.at[p, self.at.core, pl.ds(pl.multiple_of((self.at.x if x is None else x) * 16, 16), 16)]
        return self.pair(p, 7, piece, piece, self.at.across_x)

    def core_back(self, p, core=None):
        piece = self.la.at[p, self.at.core if core is None else core]
        return self.pair(p, 8, piece, piece, self.at.across_core)

    def store(self, p, dsts):
        for core, dst in enumerate(dsts):
            pltpu.make_async_copy(self.la.at[p, core], dst, self.osem.at[p, core]).start()

    def store_all(self, p):
        project, output, up, down = self.outs[:4]
        b, h = p // 2, p % 2

        def rows(core, first=0):
            return pl.ds(pl.multiple_of(first + core * 64 + h * 32, 32), 32)

        def cols(j):
            return pl.ds(pl.multiple_of(j * 1024, 1024), 1024)

        pl.when(b < 4)(lambda: self.store(p, [down.at[rows(c, b * 128)] for c in range(2)]))
        pl.when(jnp.logical_and(b >= 4, b < 8))(lambda: self.store(p, [up.at[rows(c), cols(b - 4)] for c in range(2)]))
        pl.when(b == 8)(lambda: self.store(p, [output.at[rows(c)] for c in range(2)]))
        pl.when(jnp.logical_and(b >= 9, b < 12))(lambda: self.store(p, [project.at[rows(c), cols(b - 9)] for c in range(2)]))

    lags = (4, 6, 10, 11)

    def drain(self, d):
        at, lags = self.at, self.lags

        @pl.when(d < PARTS)
        def _():
            p = d
            self.x_one(p).wait()

            self.l1a[p] = self.l1a[p] + self.s0[p % RING, :, :, self.mine, self.front]
            self.y_two(p).start()
            self.y_one(p).wait()
            self.l1b[p] = self.l1b[p] + self.s0[p % RING, :, at.y, :, self.back]
            self.x_two(p).start()

        @pl.when(jnp.logical_and(d >= lags[0], d < PARTS + lags[0]))
        def _():
            p = d - lags[0]
            self.y_two(p).wait()
            self.x_two(p).wait()

            self.l2[p, :, :, self.front] = self.l2[p, :, :, self.front] + self.l1a[p, :, at.y]
            self.l2[p, :, :, self.back] = self.l2[p, :, :, self.back] + self.l1b[p, :, self.mine]
            for k in range(1, 4):
                self.z_copy(p, k).start()

        @pl.when(jnp.logical_and(d >= lags[1], d < PARTS + lags[1]))
        def _():
            p = d - lags[1]
            total = self.l2[p, at.z].astype(WIDE)
            for k in range(1, 4):
                self.z_copy(p, k).wait()
            for k in range(3):
                total = total + self.l3[p, k].astype(WIDE)
            self.la[p, at.core, self.mine] = total.astype(LOW)
            self.x_back(p).start()

        @pl.when(jnp.logical_and(d >= lags[2], d < PARTS + lags[2]))
        def _():
            p = d - lags[2]
            self.x_back(p, 1 - at.x).wait_recv()
            self.core_back(p).start()

        @pl.when(jnp.logical_and(d >= lags[3], d < PARTS + lags[3]))
        def _():
            p = d - lags[3]
            self.x_back(p).wait_send()
            self.core_back(p).wait_send()
            self.core_back(p, 1 - at.core).wait_recv()
            self.store_all(p)

    drains = PARTS + lags[3]

    def run(self, lo, hi):
        def one(d, carry):
            self.drain(d)
            return carry

        lax.fori_loop(lo, hi, one, 0)

    def end(self):
        for b in range(READY - 2):
            self.core_copy(b).wait_send()
        self.core_copy(REDUCED - 2).wait_send()
        self.core_copy(REDUCED - 1).wait_send()

        def stored(p):
            for core in range(2):
                pltpu.make_async_copy(self.la.at[p, core], self.outs[1].at[pl.ds(0, 32)], self.osem.at[p, core]).wait()

        for_each(PARTS, stored)


REDUCE_SCRATCH = [
    pltpu.VMEM((2, 4, 2, 2, 32, 1024), LOW),
    pltpu.VMEM((RING, 4, 2, 32, 1024), LOW),
    pltpu.VMEM((PARTS, 4, 2, 16, FRONT), LOW),
    pltpu.VMEM((PARTS, 4, 32, 1024 - FRONT), LOW),
    pltpu.VMEM((PARTS, 4, 16, 1024), LOW),
    pltpu.VMEM((PARTS, 3, 16, 1024), LOW),
    pltpu.VMEM((PARTS, 2, 32, 1024), LOW),
    pltpu.SemaphoreType.DMA((REDUCED,)),
    pltpu.SemaphoreType.DMA((REDUCED,)),
    pltpu.SemaphoreType.DMA((4,)),
    pltpu.SemaphoreType.DMA((PARTS, 9)),
    pltpu.SemaphoreType.DMA((PARTS, 9)),
    pltpu.SemaphoreType.DMA((PARTS, 2)),
]


class TimeSums:
    def __init__(self, at, feat, outs, featg, sumg, part, core_in, x_in, final, send, recv, sems):
        self.at, self.outs, self.feat = at, outs, feat
        self.featg, self.sumg, self.part, self.core_in, self.x_in, self.final = featg, sumg, part, core_in, x_in, final
        self.send, self.recv, self.sems = send, recv, sems
        self.half = pl.ds(pl.multiple_of(at.core * 64, 64), 64)
        self.rows = sumg.shape[1] // 2

    def feat_copy(self, i):
        src = self.feat.at[:, pl.ds(pl.multiple_of(self.at.shards[i] * 128, 128), 128)]
        return remote(src, self.featg.at[i], self.send.at[i], self.recv.at[i], self.at.group[i])

    def begin(self):
        for i in range(7):
            self.feat_copy(i).start()
        self.featg[7] = self.feat[:, pl.ds(pl.multiple_of(self.at.f * 128, 128), 128)]

    def sum_copy(self, norm, i):
        rows = pl.ds(norm * self.rows, self.rows)
        sem = 7 + 7 * norm + i
        return remote(
            self.sumg.at[7, rows], self.sumg.at[i, rows], self.send.at[sem], self.recv.at[sem], self.at.group[i]
        )

    def share(self, norm, sums):
        rows = slice(norm * self.rows, (norm + 1) * self.rows)
        self.sumg[7, rows, :] = sums[rows, :].astype(LOW)
        for i in range(7):
            self.sum_copy(norm, i).start()

    def core_copy(self):
        src = self.part.at[pl.ds(pl.multiple_of((1 - self.at.core) * 64, 64), 64)]
        return remote(src, self.core_in, self.send.at[21], self.recv.at[21], self.at.across_core)

    def quarter(self, x):
        return pl.ds(pl.multiple_of(self.at.core * 64 + x * 32, 32), 32)

    def x_copy(self):
        src = self.part.at[self.quarter(1 - self.at.x)]
        return remote(src, self.x_in, self.send.at[22], self.recv.at[22], self.at.across_x)

    def x_back(self, x):
        piece = self.final.at[self.quarter(x)]
        return remote(piece, piece, self.send.at[23], self.recv.at[23], self.at.across_x)

    def core_back(self, core):
        piece = self.final.at[pl.ds(pl.multiple_of(core * 64, 64), 64)]
        return remote(piece, piece, self.send.at[24], self.recv.at[24], self.at.across_core)

    def combine(self):
        for i in range(7):
            self.feat_copy(i).wait()
            for norm in range(2):
                self.sum_copy(norm, i).wait()
        rows = 8 * self.sumg.shape[1]
        for h in range(2):
            cols = slice(h * HALF, (h + 1) * HALF)
            terms = self.sumg[:, :, cols].reshape(rows, HALF)
            total = lax.dot_general(self.featg[...].reshape(rows, 128), terms, TN, preferred_element_type=WIDE)
            self.part[:, cols] = total.astype(LOW)
        self.core_copy().start()

    def cross(self):
        self.core_copy().wait()
        self.part[self.half, :] = self.part[self.half, :] + self.core_in[...]
        self.x_copy().start()

    def finish(self):
        at = self.at
        self.x_copy().wait()
        mine = self.quarter(at.x)
        self.final[mine, :] = self.part[mine, :] + self.x_in[...]
        self.x_back(at.x).start()

    def give(self):
        at = self.at
        self.x_back(at.x).wait_send()
        self.x_back(1 - at.x).wait_recv()
        self.core_back(at.core).start()

    def end(self):
        at = self.at
        self.core_back(at.core).wait_send()
        self.core_back(1 - at.core).wait_recv()
        copies = [
            pltpu.make_async_copy(
                self.final.at[pl.ds(64 * n + 32 * h, 32)], self.outs[n].at[:, pl.ds(1024 * h, 1024)], self.sems.at[2 * n + h]
            )
            for n in range(2)
            for h in range(2)
        ]
        for copy in copies:
            copy.start()
        for copy in copies:
            copy.wait()


def sum_vectors(at, parts, got, sums, out, send, recv):
    def part(i):
        return remote(parts.at[at.shards[i]], got.at[i], send.at[i], recv.at[i], at.group[i])

    reps = [at.across_x, at.across_core, at.diagonal]

    def rest(i):
        return remote(sums.at[3], sums.at[i], send.at[7 + i], recv.at[7 + i], reps[i])

    def start():
        for i in range(7):
            part(i).start()

    def middle():
        total = parts[at.f]
        for i in range(7):
            part(i).wait()
            total = total + got[i]
        sums[3] = total
        for i in range(3):
            rest(i).start()

    def end():
        total = sums[3]
        for i in range(3):
            rest(i).wait()
            total = total + sums[i]
        out[...] = total

    return start, middle, end


COT, NORMED2, PAIR, GRAD_UP, TOKENS, NORMED1 = 0, 1, 2, 4, 8, 9
QUERY, KEY, VALUE, GRAD_CONTEXT, GRAD_BRANCH, CONTEXT = 2, 3, 4, 5, 10, 11
LAST = (5, 6, 7, 1)


def backward_kernel(comm, seqs, *refs):
    refs = list(refs)
    take = lambda n: [refs.pop(0) for _ in range(n)]
    full, cot_h, activ_h, slope_h, normed1_h, normed2_h, mid_h, q_h, k_h, v_h, ctx_h, probs_h, tokens_h, ready = take(14)
    table, mods, feat, cosine, sine = take(5)
    outs = take(6 if comm else 1)
    vec_out, input_o, layer_o = take(3)
    if comm:
        own, l0 = take(2)
    else:
        (out,) = outs
    pool, gn, mid, weights, slots, shares, sums, gtab, sem_in, sem_pair, sem_w, sem_mid, sem_slot, sem_share, sem_out = take(15)
    if comm:
        parts, vgot, vsums, vsend, vrecv = take(5)
        time_scratch = take(9)
        red = Reduce(ready, slots, own, l0, outs, *refs)
    tokens_n = pool.shape[1]
    per = tokens_n // seqs

    def fetch(src, i):
        return pltpu.make_async_copy(src, pool.at[i], sem_in.at[i])

    def fetch_slope(j):
        return pltpu.make_async_copy(slope_h.at[j], pool.at[PAIR + j % 2], sem_pair.at[j % 2])

    def fetch_share(n):
        return pltpu.make_async_copy(probs_h.at[n], shares.at[n % 2], sem_share.at[n % 2])

    def fetch_w(c, slot):
        return pltpu.make_async_copy(full.at[c], weights.at[slot], sem_w.at[slot])

    mid_in = pltpu.make_async_copy(mid_h, mid, sem_mid)
    fetch(cot_h, COT).start()
    fetch_slope(0).start()
    fetch_slope(1).start()
    fetch(normed2_h, NORMED2).start()
    fetch_w(9, 0).start()
    fetch_w(10, 1).start()
    mid_in.start()
    for src, i in ((tokens_h, TOKENS), (normed1_h, NORMED1), (ctx_h, CONTEXT)):
        fetch(src, i).start()
    if comm:
        red.begin()
        time_sums = TimeSums(red.at, feat, outs[4:], *time_scratch)
        time_sums.begin()
        run, load, feed = red.run, red.load, red.feed
    else:
        run = load = feed = lambda *a: None
    when = pl.when if comm else (lambda cond: lambda body: None)

    half_cols = lambda h: slice(h * HALF, (h + 1) * HALF)

    def half_rows(slot, h):
        if comm:
            return weights[slot, 2 * h : 2 * h + 2].reshape(HALF, 1024)
        return weights[slot, half_cols(h), :]

    def produce(b, lhs, rhs_of):
        if comm:
            red.free(b)
        else:
            pl.when(b >= READY + 2)(
                lambda: pltpu.make_async_copy(slots.at[b % 2], out.at[b - READY - 2], sem_slot.at[b % 2]).wait()
            )
        for h in range(2):
            block = rhs_of(lhs, h).astype(LOW)
            if comm:
                slots[b % 2, :, :, :, :, :, half_cols(h)] = block.reshape(4, 2, 2, 2, 32, HALF)
            else:
                slots[b % 2, :, half_cols(h)] = block
        if comm:
            red.produced(b)
        else:
            pltpu.make_async_copy(slots.at[b % 2], out.at[b - READY], sem_slot.at[b % 2]).start()

    def times(i):
        return lambda lhs, h: lax.dot_general(lhs[...], pool[i, :, half_cols(h)], TN, preferred_element_type=WIDE)

    ones = jnp.ones((8, tokens_n), LOW)

    def column_sums(i, row):
        gtab[pl.ds(row, 1), :] = jnp.dot(ones, pool[i], preferred_element_type=WIDE)[:1]

    def up(j):
        produce(4 + j, pool.at[NORMED2], times(GRAD_UP + j))

    fetch(cot_h, COT).wait()
    load(0)
    feed(0)
    column_sums(COT, BIAS_D)

    def activ_back(j):
        fetch_slope(j).wait()
        fetch_w(9 + j, j % 2).wait()
        for h in range(2):
            grad = lax.dot_general(pool[COT], half_rows(j % 2, h), NT, preferred_element_type=WIDE)
            grad = (grad * pool[PAIR + j % 2, :, half_cols(h)].astype(WIDE)).astype(LOW)
            for n in range(4):
                f = 4 * h + n
                place = pl.ds(pl.multiple_of((f % 2 * 4 + j) * 128, 128), 128)
                pool[GRAD_UP + f // 2, :, place] = grad[:, n * 128 : (n + 1) * 128]

        pl.when(j < 2)(lambda: fetch_w(11 + j, j % 2).start())
        pl.when(j >= 2)(lambda: fetch_w(3 + j, j % 2).start())
        pl.when(j < 2)(lambda: fetch_slope(j + 2).start())
        when(j >= 1)(lambda: feed(j))
        when(j == 0)(lambda: load(1))
        when(j == 1)(lambda: load(2))
        when(j == 2)(lambda: load(3))
        when(j >= 1)(lambda: run(j - 1, j))

    for_each(4, activ_back)
    fetch(q_h, QUERY).start()
    fetch(k_h, KEY).start()
    fetch(normed2_h, NORMED2).wait()

    def up_back(j):
        fetch_w(5 + j, j % 2).wait()
        for h in range(2):
            more = lax.dot_general(pool[GRAD_UP + j], half_rows(j % 2, h), NT, preferred_element_type=WIDE)

            @pl.when(j == 0)
            def _():
                gn[:, half_cols(h)] = more

            @pl.when(j > 0)
            def _():
                gn[:, half_cols(h)] = gn[:, half_cols(h)] + more

        pl.when(j < 2)(lambda: fetch_w(7 + j, j % 2).start())
        pl.when(j == 2)(lambda: fetch_w(4, 0).start())
        pl.when(j == 3)(lambda: fetch_w(1, 1).start())
        column_sums(GRAD_UP + j, BIAS_U + j)
        when(j == 2)(lambda: load(4))
        when(j == 3)(lambda: feed(4))
        pl.when(j % 2 == 1)(lambda: up(j // 2))
        when(j % 2 == 0)(lambda: run(3 + j // 2, 4 + j // 2))

    for_each(4, up_back)
    fetch(v_h, VALUE).start()
    fetch_share(0).start()
    fetch_share(1).start()

    sums[...] = jnp.zeros_like(sums)

    def norm_back(which, gain, value_of, done):
        def body(i):
            rows = rows_at(i)
            s = i // (per // TILE)
            at_scale, at_shift = part_of(which, 0, seqs) + s, part_of(which, 1, seqs) + s
            scale = table[gain : gain + 1, :] + row_of(mods, at_scale)
            normed, inverse = normalise(value_of(rows).astype(WIDE))
            grad = gn[rows, :]
            sums[pl.ds(at_scale, 1), :] += jnp.sum(grad * normed, axis=0, keepdims=True)
            sums[pl.ds(at_shift, 1), :] += jnp.sum(grad, axis=0, keepdims=True)
            hat = grad * scale
            done(rows, inverse * (hat - lane_mean(hat) - normed * lane_mean(hat * normed)))

        for_each(tokens_n // TILE, body)
        for n in range(2):
            at = part_of(which, n, seqs)
            gtab[gain + n : gain + n + 1, :] = jnp.sum(sums[at : at + seqs, :], axis=0, keepdims=True)
        if comm:
            time_sums.share(which, sums)

    mid_in.wait()

    def done2(rows, grad):
        total = pool[COT, rows, :].astype(WIDE) + grad
        mid[rows, :] = total
        pool[GRAD_BRANCH, rows, :] = total.astype(LOW)

    norm_back(1, GAIN2, lambda rows: mid[rows, :], done2)
    load(5)
    run(5, 7)

    column_sums(GRAD_BRANCH, BIAS_O)
    fetch_w(4, 0).wait()
    for h in range(2):
        grad = lax.dot_general(pool[GRAD_BRANCH], half_rows(0, h), NT, preferred_element_type=WIDE)
        pool[GRAD_CONTEXT, :, half_cols(h)] = grad.astype(LOW)
    fetch_w(2, 0).start()
    feed(5)
    up(2)
    run(7, 8)
    for src, i in ((q_h, QUERY), (k_h, KEY), (v_h, VALUE), (ctx_h, CONTEXT), (tokens_h, TOKENS), (normed1_h, NORMED1)):
        fetch(src, i).wait()

    lane = lax.broadcasted_iota(jnp.int32, (1, 128), 1)
    first_head = (lane < 64).astype(WIDE)
    second_head = 1.0 - first_head

    def split(v):
        return jnp.concatenate([v * first_head.astype(LOW), v * second_head.astype(LOW)], axis=0)

    def unturned(v):
        return v * cosine[...] - swapped(v) * sine[...]

    def heads(n):
        cols = pl.ds(pl.multiple_of(n * 128, 128), 128)
        fetch_share(n).wait()
        def one(s):
            rows = rows_at(s, per)
            keys = pool[KEY, rows, cols]
            both = split(pool[QUERY, rows, cols])
            grads = split(pool[GRAD_CONTEXT, rows, cols])
            share = shares[n % 2, rows_at(s, 2 * per), :]
            probs = share.astype(WIDE)
            grad_probs = lax.dot_general(grads, pool[VALUE, rows, cols], NT, preferred_element_type=WIDE)
            inner = jnp.sum(grad_probs * probs, axis=-1, keepdims=True)
            grad_scores = (probs * (grad_probs - inner)).astype(LOW)
            grad_v = lax.dot_general(share, grads, TN, preferred_element_type=WIDE)
            grad_k = lax.dot_general(grad_scores, both, TN, preferred_element_type=WIDE)
            grad_q = jnp.dot(grad_scores, keys, preferred_element_type=WIDE)
            grad_q = (grad_q[:per] * first_head + grad_q[per:] * second_head) * 0.125
            pool[QUERY, rows, cols] = unturned(grad_q).astype(LOW)
            pool[KEY, rows, cols] = unturned(grad_k).astype(LOW)
            pool[VALUE, rows, cols] = grad_v.astype(LOW)

        in_pairs(seqs, one)

        pl.when(n < 6)(lambda: fetch_share(n + 2).start())
        when(n % 3 == 0)(lambda: load(6 + n // 3))
        when(jnp.logical_and(n % 3 == 1, n < 7))(lambda: feed(6 + n // 3))
        when(n == 7)(lambda: feed(8))

        @pl.when(jnp.logical_or(n == 2, n == 5))
        def _():
            lhs = jnp.where(n == 2, NORMED2, CONTEXT)
            rhs = jnp.where(n == 2, GRAD_UP + 3, GRAD_BRANCH)
            produce(6 + (n + 1) // 3, pool.at[lhs], times(rhs))

        done = 8 + n - (n + 2) // 3
        when(n % 3 != 0)(lambda: run(done, done + 1))

    for_each(8, heads)
    for j, i in enumerate(LAST):
        fetch(activ_h.at[j], i).start()

    def project(j):
        column_sums(QUERY + j, BIAS_P + j)
        when(j == 2)(lambda: feed(9))
        produce(9 + j, pool.at[NORMED1], times(QUERY + j))
        when(j >= 1)(lambda: load(8 + j))
        run(13 + j, 14 + j)

    for_each(3, project)

    def project_back(j):
        slot = (1 + j) % 2
        fetch_w(1 + j, slot).wait()
        for h in range(2):
            more = lax.dot_general(pool[QUERY + j], half_rows(slot, h), NT, preferred_element_type=WIDE)

            @pl.when(j == 0)
            def _():
                gn[:, half_cols(h)] = more

            @pl.when(j > 0)
            def _():
                gn[:, half_cols(h)] = gn[:, half_cols(h)] + more

        pl.when(j == 0)(lambda: fetch_w(3, 1).start())
        pl.when(j >= 1)(lambda: fetch_w(8 + j, (j + 1) % 2).start())
        when(j < 2)(lambda: feed(10 + j))
        when(j == 0)(lambda: load(11))
        when(j < 2)(lambda: run(16 + j, 17 + j))

    for_each(3, project_back)

    def done1(rows, grad):
        mid[rows, :] = mid[rows, :] + grad

    norm_back(0, GAIN1, lambda rows: pool[TOKENS, rows, :], done1)
    input_copy = pltpu.make_async_copy(mid, input_o, sem_mid)
    input_copy.start()
    middle_in = pltpu.make_async_copy(mid_h, gn, sem_out.at[0])
    middle_in.start()
    run(18, 20)
    if comm:
        for f in range(8):
            for row in range(13):
                r, b = vector_spot(row, f)
                parts[f, row : row + 1, :] = gtab[r : r + 1, b * 128 : (b + 1) * 128]
            parts[f, 13:16, :] = jnp.zeros((3, 128), WIDE)
        start, middle, end = sum_vectors(red.at, parts, vgot, vsums, vec_out, vsend, vrecv)
        start()
    else:
        vec_out[...] = gtab[...]

    def outer(lhs, h):
        terms = sums[:, half_cols(h)]
        high = terms.astype(LOW)
        rest = (terms - high.astype(WIDE)).astype(LOW)
        return lax.dot_general(lhs[...], high, TN, preferred_element_type=WIDE) + lax.dot_general(
            lhs[...], rest, TN, preferred_element_type=WIDE
        )

    if not comm:
        produce(12, feat, outer)

    middle_in.wait()
    for j, i in enumerate(LAST):
        run(20 + 2 * j, 22 + 2 * j)
        fetch(activ_h.at[j], i).wait()
        fetch_w(9 + j, j % 2).wait()
        for h in range(2):
            cols = half_cols(h)
            w = weights[j % 2, ..., cols].reshape(1024, HALF) if comm else weights[j % 2, :, cols]
            total = gn[:, cols] + jnp.dot(pool[i], w, preferred_element_type=WIDE)
            if j < 3:
                gn[:, cols] = total
            else:
                pool[COT, :, cols] = (total + table[BIAS_D : BIAS_D + 1, cols]).astype(LOW)
        if j < 2:
            fetch_w(11 + j, j % 2).start()
        if comm and j >= 1:
            (time_sums.combine, time_sums.cross, time_sums.finish)[j - 1]()
    layer_copy = pltpu.make_async_copy(pool.at[COT], layer_o, sem_out.at[1])
    layer_copy.start()
    if comm:
        middle()
        time_sums.give()
        end()
        run(28, red.drains)
        time_sums.end()
        red.end()
    else:
        for b in (11, 12):
            pltpu.make_async_copy(slots.at[b % 2], out.at[b - READY], sem_slot.at[b % 2]).wait()
    input_copy.wait()
    layer_copy.wait()


def backward_call(comm, full, cot, saved, tokens, table, mods, feat, cosine, sine, seqs):
    n, width = tokens.shape
    vmem, hbm = pl.BlockSpec(memory_space=pltpu.VMEM), pl.BlockSpec(memory_space=pl.ANY)
    ready, q, k, v, ctx, mid, normed1, normed2, activ, slope, probs = saved
    block = (4, 2, 2, 2, 32, width) if comm else (width, width)
    rows = width // 8
    if comm:
        shapes = [(rows, 3 * width), (rows, width), (rows, 4 * width), (4 * rows, width), (TE // 8, 2 * width), (TE // 8, 2 * width)]
    else:
        shapes = [(BLOCKS - READY, width, width)]
    outs = [(jax.ShapeDtypeStruct(shape, LOW), hbm) for shape in shapes] + [
        (jax.ShapeDtypeStruct((16, 128) if comm else (16, width), WIDE), vmem),
        (jax.ShapeDtypeStruct((n, width), WIDE), hbm),
        (jax.ShapeDtypeStruct((n, width), LOW), hbm),
    ]
    extra = []
    if comm:
        part = lambda count: (jax.ShapeDtypeStruct((count, 4, 2, 2, 32, width), LOW), hbm)
        outs += [part(REDUCED - READY), part(REDUCED)]
        extra = [
            pltpu.VMEM((8, 16, 128), WIDE),
            pltpu.VMEM((7, 16, 128), WIDE),
            pltpu.VMEM((4, 16, 128), WIDE),
            pltpu.SemaphoreType.DMA((10,)),
            pltpu.SemaphoreType.DMA((10,)),
            pltpu.VMEM((8, feat.shape[0], 128), LOW),
            pltpu.VMEM((8, feat.shape[0], width), LOW),
            pltpu.VMEM((128, width), LOW),
            pltpu.VMEM((64, width), LOW),
            pltpu.VMEM((32, width), LOW),
            pltpu.VMEM((128, width), LOW),
            pltpu.SemaphoreType.DMA((25,)),
            pltpu.SemaphoreType.DMA((25,)),
            pltpu.SemaphoreType.DMA((4,)),
        ] + REDUCE_SCRATCH
        full = full.reshape((BLOCKS,) + block)
    got = pl.pallas_call(
        functools.partial(backward_kernel, comm, seqs),
        out_shape=tuple(s for s, _ in outs),
        in_specs=[hbm] * 14 + [vmem] * 5,
        out_specs=tuple(m for _, m in outs),
        scratch_shapes=[
            pltpu.VMEM((12, n, width), LOW),
            pltpu.VMEM((n, width), WIDE),
            pltpu.VMEM((n, width), WIDE),
            pltpu.VMEM((2,) + block, LOW),
            pltpu.VMEM((2,) + block, LOW),
            pltpu.VMEM((2,) + probs.shape[1:], LOW),
            pltpu.VMEM((feat.shape[0], width), WIDE),
            pltpu.VMEM((16, width), WIDE),
            pltpu.SemaphoreType.DMA((12,)),
            pltpu.SemaphoreType.DMA((2,)),
            pltpu.SemaphoreType.DMA((2,)),
            pltpu.SemaphoreType.DMA,
            pltpu.SemaphoreType.DMA((2,)),
            pltpu.SemaphoreType.DMA((2,)),
            pltpu.SemaphoreType.DMA((2,)),
        ]
        + extra,
        compiler_params=pltpu.CompilerParams(
            collective_id=1 if comm else None, has_side_effects=comm, vmem_limit_bytes=62 * 2**20
        ),
        name="backward",
    )(full, cot, activ, slope, normed1, normed2, mid, q, k, v, ctx, probs, tokens, ready, table, mods, feat, cosine, sine)
    return got[: len(shapes) + 3]


def widen(arrays, vec, sizes):
    count = len(arrays)

    def kernel(vec_in, *refs):
        srcs, dsts, lines = refs[:count], refs[count : 2 * count], refs[2 * count : 2 * count + len(sizes)]
        rest = refs[2 * count + len(sizes) :]
        lows, wides, sems = rest[:count], rest[count : 2 * count], rest[-1]
        ins = [pltpu.make_async_copy(s, v, sems.at[i]) for i, (s, v) in enumerate(zip(srcs, lows))]
        outs = [pltpu.make_async_copy(v, d, sems.at[i]) for i, (v, d) in enumerate(zip(wides, dsts))]
        for copy in ins:
            copy.start()
        row = 0
        for line, size in zip(lines, sizes):
            for k in range(size // 128):
                line[pl.ds(128 * k, 128)] = vec_in[row, :]
                row += 1
        for i in range(count):
            ins[i].wait()

            def body(n, i=i):
                at = pl.ds(pl.multiple_of(n * 16, 16), 16)
                wides[i][at, :] = lows[i][at, :].astype(WIDE)

            for_each(lows[i].shape[0] // 16, body)
            outs[i].start()
        for copy in outs:
            copy.wait()

    hbm, vmem = pl.BlockSpec(memory_space=pl.ANY), pl.BlockSpec(memory_space=pltpu.VMEM)
    got = pl.pallas_call(
        kernel,
        out_shape=tuple(jax.ShapeDtypeStruct(a.shape, WIDE) for a in arrays)
        + tuple(jax.ShapeDtypeStruct((size,), WIDE) for size in sizes),
        in_specs=[vmem] + [hbm] * count,
        out_specs=(hbm,) * count + (vmem,) * len(sizes),
        scratch_shapes=[pltpu.VMEM(a.shape, LOW) for a in arrays]
        + [pltpu.VMEM(a.shape, WIDE) for a in arrays]
        + [pltpu.SemaphoreType.DMA((count,))],
        compiler_params=pltpu.CompilerParams(vmem_limit_bytes=60 * 2**20),
        name="widen",
    )(vec, *arrays)
    return got[:count], got[count:]


def rotary_constants(length, head_dim):
    half_width = head_dim // 2
    inverse = np.exp(np.arange(half_width, dtype=np.float32) * np.float32(-math.log(10000.0) / half_width))
    angles = np.arange(length, dtype=np.float32)[:, None] * inverse[None, :]
    cosine, sine = np.cos(angles), np.sin(angles)
    pair = np.concatenate([cosine, cosine], axis=1), np.concatenate([-sine, sine], axis=1)
    return tuple(np.concatenate([t, t], axis=1).astype(np.float32) for t in pair)


def wide_features(noise_times, width):
    seqs = noise_times.shape[0]
    half_width = TE // 2
    column = np.arange(width)
    feature = column // 128 * 32 + column % 32
    rates = np.exp((feature % half_width).astype(np.float32) * np.float32(math.log(100.0) / half_width))
    each = part_of(1, 0, seqs)
    row = np.arange(2 * each)
    part = np.where(row % each < 2 * seqs, row // each * 2 + row % each // seqs, -1)
    mine = row[:, None] % each % seqs == np.arange(seqs)[None, :]
    times = jnp.sum(jnp.where(mine, noise_times[None, :], 0.0), axis=1)
    phases = (jnp.log(times) * 0.25)[:, None] * rates[None, :]
    feat = jnp.where((feature < half_width)[None, :], jnp.sin(phases), jnp.cos(phases))
    return jnp.where((column // 32 % 4)[None, :] == part[:, None], feat, 0.0).astype(LOW)


def gather_plain(weights, vectors):
    project, output, up, down, time1, time2 = weights
    rows, width = output.shape
    each = time1.shape[0]
    columns = lambda w: w.reshape(rows, -1, width).transpose(1, 0, 2)
    times = jnp.stack([time1, time2]).reshape(2, each, 2, width).transpose(0, 2, 1, 3)
    own = jnp.concatenate(
        [times.reshape(1, rows, width), columns(project), output[None], columns(up), down.reshape(4, rows, width)]
    )
    full = lax.all_gather(own, "fsdp", axis=1, tiled=True)
    times = full[0].reshape(-1, 2, 2, each, width).transpose(1, 2, 0, 3, 4).reshape(2, 2, 8, 32, width)
    down = full[9:].reshape(4, -1, rows, width).transpose(1, 0, 2, 3).reshape(8, 4, 128, width)
    full = jnp.concatenate(
        [
            times.transpose(2, 0, 1, 3, 4).reshape(1, width, width),
            full[1:9],
            down.transpose(1, 0, 2, 3).reshape(4, width, width),
        ]
    )
    sizes = [v.shape[0] for v in vectors]
    whole = pieces_of(lax.all_gather(jnp.concatenate(vectors), "fsdp", axis=0), sizes)
    table = jnp.concatenate([w.reshape(-1, width) for w in whole]).astype(WIDE)
    return full, jnp.pad(table, ((0, 3), (0, 0)))


def reduce_plain(parts, table, sizes, shards_of):
    width = parts.shape[-1]
    rows, each = width // shards_of, TE // shards_of
    down = parts[:4].reshape(4, 8, 128, width).transpose(1, 0, 2, 3).reshape(shards_of, 4, rows, width)
    times = parts[12].reshape(8, 2, 2, 32, width).transpose(1, 2, 0, 3, 4).reshape(2, 2, shards_of, each, width)
    own = jnp.concatenate(
        [
            down.transpose(1, 0, 2, 3).reshape(4, width, width),
            parts[4:12],
            times.transpose(2, 0, 1, 3, 4).reshape(1, width, width),
        ]
    )
    mine = lax.psum(lax.psum_scatter(own, "fsdp", scatter_dimension=1, tiled=True), "rep")
    whole = pieces_of(table[:13].reshape(-1), [shards_of * size for size in sizes])
    vec = jnp.concatenate([w.reshape(shards_of, -1) for w in whole], axis=1)
    vec = lax.psum(lax.psum_scatter(vec, "fsdp", scatter_dimension=0, tiled=True)[0], "rep")
    columns = lambda w: w.transpose(1, 0, 2).reshape(rows, -1)
    times = mine[12].reshape(2, 2, each, width).transpose(0, 2, 1, 3).reshape(2, each, 2 * width)
    return columns(mine[9:12]), mine[8], columns(mine[4:8]), mine[:4].reshape(-1, width), times[0], times[1], vec


def pieces_of(flat, sizes):
    at, got = 0, []
    for size in sizes:
        got.append(flat[..., at : at + size])
        at += size
    return got


def shards(
    inputs,
    noise_times,
    cotangent,
    norm1_gain,
    norm1_bias,
    norm1_time,
    project_weight,
    project_bias,
    output_weight,
    output_bias,
    norm2_gain,
    norm2_bias,
    norm2_time,
    up_weight,
    up_bias,
    down_weight,
    down_bias,
):
    seqs = noise_times.shape[0]
    tokens_n, width = inputs.shape
    rows = output_weight.shape[0]
    shards_of = width // rows
    comm = shards_of == 8
    feat = wide_features(noise_times, width)
    cosine, sine = rotary_constants(tokens_n // seqs, width // HEADS)
    weights = (project_weight, output_weight, up_weight, down_weight, norm1_time, norm2_time)
    vectors = (norm1_gain, norm1_bias, project_bias, output_bias, norm2_gain, norm2_bias, up_bias, down_bias)
    sizes = [v.shape[0] for v in vectors]
    if comm:
        at, table = 0, jnp.zeros((16, 128), WIDE)
        for v in vectors:
            lines = v.astype(WIDE).reshape(-1, 128)
            table = table + jnp.pad(lines, ((at, 16 - at - lines.shape[0]), (0, 0)))
            at += lines.shape[0]
    else:
        full, table = gather_plain(weights, vectors)
        weights = (full,)
    full, table, mods, *saved = forward_call(
        comm, weights, table, inputs, cotangent, feat, cosine, sine, seqs
    )
    *sums, input_grad, layer_out = backward_call(comm, full, cotangent, saved, inputs, table, mods, feat, cosine, sine, seqs)
    if not comm:
        sums = reduce_plain(jnp.concatenate([saved[0], sums[0]]), sums[1], sizes, shards_of)
    if comm:
        wide, got = widen(sums[:6], sums[6], sizes)
    else:
        wide, got = [s.astype(WIDE) for s in sums[:6]], pieces_of(sums[6], sizes)
    project, output, up, down, time1, time2 = wide
    return (
        layer_out,
        input_grad,
        got[0],
        got[1],
        time1,
        project,
        got[2],
        output,
        got[3],
        got[4],
        got[5],
        time2,
        up,
        got[6],
        down,
        got[7],
    )


def solution(mesh):
    placed = (
        P(("rep", "fsdp"), None),
        P(("rep", "fsdp")),
        P(("rep", "fsdp"), None),
        P("fsdp"),
        P("fsdp"),
        P("fsdp", None),
        P("fsdp", None),
        P("fsdp"),
        P("fsdp", None),
        P("fsdp"),
        P("fsdp"),
        P("fsdp"),
        P("fsdp", None),
        P("fsdp", None),
        P("fsdp"),
        P("fsdp", None),
        P("fsdp"),
    )
    return jax.shard_map(
        shards,
        mesh=mesh,
        in_specs=placed,
        out_specs=(
            P(("rep", "fsdp"), None),
            P(("rep", "fsdp"), None),
            P("fsdp"),
            P("fsdp"),
            P("fsdp", None),
            P("fsdp", None),
            P("fsdp"),
            P("fsdp", None),
            P("fsdp"),
            P("fsdp"),
            P("fsdp"),
            P("fsdp", None),
            P("fsdp", None),
            P("fsdp"),
            P("fsdp", None),
            P("fsdp"),
        ),
        check_vma=False,
    )
```
